128 devices in a mesh: dp: 16 (over z_hi, y, core), tensor: 8 (over z_lo, x).
Axes of the slice: x: 4, y: 4, z: 4 (z_hi: 2, z_lo: 2; z = z_hi * 2 + z_lo), core: 2. Of those that a mesh axis runs over, the one named last changes fastest.
Arguments:
- x_in: bfloat16 [18688, 1024], P(('dp', 'tensor')), may hold values from -6 to 6
- valid_len: int32 [32], P('dp'), may hold values from 480 to 577, as said below
- w_qkv: bfloat16 [2, 1024, 3, 1024], P(None, 'dp', None, 'tensor'), may hold values from -0.1875 to 0.1875
- w_out: bfloat16 [2, 1024, 1024], P(None, 'tensor', 'dp'), may hold values from -0.75 to 0.75
- w_up: bfloat16 [2, 1024, 4096], P(None, 'dp', 'tensor'), may hold values from -0.1875 to 0.1875
- w_down: bfloat16 [2, 4096, 1024], P(None, 'tensor', 'dp'), may hold values from -0.09375 to 0.09375
- norm_gain: float32 [2, 2, 1024], replicated, may hold values from 0.1 to 1.9
- norm_shift: float32 [2, 2, 1024], replicated, may hold values from -3 to 3
- bias: float32 [2, 4, 1024], replicated, may hold values from -3 to 3
- up_bias: float32 [2, 4096], replicated, may hold values from -3 to 3
- cotangent: bfloat16 [18688, 1024], P(('dp', 'tensor')), may hold values from -6 to 6
Outputs:
- out_rows: bfloat16 [18688, 1024], P(('dp', 'tensor'))
- grad_input: float32 [18688, 1024], P(('dp', 'tensor'))
- grad_qkv: float32 [2, 1024, 3, 1024], P(None, 'dp', None, 'tensor')
- grad_out: float32 [2, 1024, 1024], P(None, 'tensor', 'dp')
- grad_up: float32 [2, 1024, 4096], P(None, 'dp', 'tensor')
- grad_down: float32 [2, 4096, 1024], P(None, 'tensor', 'dp')
- grad_gain: float32 [2, 2, 1024], replicated
- grad_shift: float32 [2, 2, 1024], replicated
- grad_bias: float32 [2, 4, 1024], replicated
- grad_up_bias: float32 [2, 4096], replicated
The draws below stay inside these ranges and needn't reach their ends.
Inputs may be any that keep to these rules, and one draw needn't show every extreme that they name: `valid_len`: the number of valid leading positions of each image; padding follows them; some image has 577 and some has 480.
All inputs are finite; a program needn't handle non-finite values.
Results may differ from the reference program's by a relative error of at most 0.02.
Values may be sent and summed in bfloat16 or wider, within the bound.
A program may use at most 128 MiB of HBM per device.

```python
import jax
import jax.numpy as jnp
from jax import lax

D = 1024
HEADS = 16
HEAD_DIM = 64
FF = 4096
SEQ = 584
VALID = 577
MIN_VALID = 480
LAYERS = 2
IMAGES = 32
TOKENS = 18688


def draw_valid_len(key, part):
    key = jax.random.fold_in(key, 7)
    lengths = jax.random.randint(key, (IMAGES,), MIN_VALID, VALID + 1)
    lengths = lengths.at[0].set(VALID)
    return lengths.at[IMAGES - 1].set(MIN_VALID).astype(jnp.int32)


def level_of(rng, dims, pieces, smallest, high):
    gain, own = 1.0, jax.random.fold_in(rng, 6)
    for axis_at, shards_of in pieces:
        steps = jnp.exp(jax.random.uniform(jax.random.fold_in(own, axis_at), (shards_of,), jnp.float32, smallest / len(pieces), high / len(pieces)))
        gain = gain * jnp.repeat(steps, dims[axis_at] // shards_of).reshape([-1 if axis == axis_at else 1 for axis in range(len(dims))])
    return gain


def normal_values(stream_key, dims, width, most, cuts=(), held_as=jnp.bfloat16):
    level = level_of(stream_key, dims, cuts, -0.22, 0.18) if cuts else 1.0
    entries = jax.random.normal(stream_key, dims, jnp.float32) * width * level
    return jnp.minimum(jnp.maximum(entries, -most), most).astype(held_as)


def setup_inputs(seed: int = 0) -> dict:
    keys = jax.random.split(jax.random.key(seed), 12)
    return {
        "x_in": normal_values(keys[0], (TOKENS, D), 1.0, 6.0, ((0, 128),)),
        "valid_len": draw_valid_len(jax.random.fold_in(keys[11], 71), 0),
        "w_qkv": normal_values(keys[2], (LAYERS, D, 3, D), D ** -0.5, 0.1875, ((1, 16), (3, 8))),
        "w_out": normal_values(keys[3], (LAYERS, D, D), (D // 16) ** -0.5, 0.75, ((1, 8), (2, 16))),
        "w_up": normal_values(keys[4], (LAYERS, D, FF), D ** -0.5, 0.1875, ((1, 16), (2, 8))),
        "w_down": normal_values(keys[5], (LAYERS, FF, D), FF ** -0.5, 0.09375, ((1, 8), (2, 16))),
        "norm_gain": jnp.clip(1.0 + 0.18 * jax.random.normal(keys[6], (LAYERS, 2, D), jnp.float32), 0.1, 1.9),
        "norm_shift": normal_values(keys[7], (LAYERS, 2, D), 0.5, 3.0, (), jnp.float32),
        "bias": normal_values(keys[8], (LAYERS, 4, D), 0.5, 3.0, (), jnp.float32),
        "up_bias": normal_values(keys[9], (LAYERS, FF), 0.5, 3.0, (), jnp.float32),
        "cotangent": normal_values(keys[10], (TOKENS, D), 1.0, 6.0, ((0, 128),)),
    }


EPSILON = 1e-06
NEG_FILL = -1e+30
HIGHEST = lax.Precision.HIGHEST
GROUP_IMAGES = 4

@jax.custom_vjp
def low(v):
    return lax.optimization_barrier(v.astype(jnp.bfloat16)).astype(jnp.float32)

@jax.custom_vjp
def low_back(v):
    return v

def low_keep(v):
    return (low(v), None)

def low_pass(kept, grad):
    return (grad,)

def back_keep(v):
    return (v, None)

def back_low(kept, grad):
    return (low(grad),)
low.defvjp(low_keep, low_pass)
low_back.defvjp(back_keep, back_low)

def layer_norm(inputs, gains, offset):
    row_mean = lax.optimization_barrier(jnp.mean(inputs, axis=-1, keepdims=True))
    centred = inputs - row_mean
    spread = lax.optimization_barrier(jnp.mean(centred * centred, axis=-1, keepdims=True))
    return centred * lax.rsqrt(spread + EPSILON) * gains + offset

def attend(queries, key_rows, value_rows, length):
    scores = jnp.einsum('qhc,khc->hqk', queries, key_rows, precision=HIGHEST) * HEAD_DIM ** (-0.5)
    scores = low_back(scores)
    key_valid = jnp.arange(key_rows.shape[0]) < length
    scores = jnp.where(key_valid[None, None, :], scores, NEG_FILL)
    weights = jax.nn.softmax(scores, axis=-1)
    return jnp.einsum('hqk,khc->qhc', low(weights), value_rows, precision=HIGHEST)

def one_layer(rows_in, lengths, w_qkv, w_out, w_up, w_down, gains, offsets, biases, hidden_bias):
    group_size = lengths.shape[0]
    normed_one = low(layer_norm(rows_in, gains[0], offsets[0]))
    projected = jnp.einsum('rd,dkc->rkc', normed_one, w_qkv, precision=HIGHEST)
    queries = low(low_back(projected[:, 0] + biases[0]))
    key_rows = low(low_back(projected[:, 1]))
    value_rows = low(low_back(projected[:, 2] + biases[1]))
    head_shape = (group_size, SEQ, HEADS, HEAD_DIM)
    attended = jax.vmap(jax.checkpoint(attend))(queries.reshape(head_shape), key_rows.reshape(head_shape), value_rows.reshape(head_shape), lengths)
    attended = low(low_back(attended.reshape(-1, D)))
    middle = rows_in + low_back(jnp.dot(attended, w_out, precision=HIGHEST)) + biases[2]
    normed_two = low(layer_norm(middle, gains[1], offsets[1]))
    hidden = low_back(jnp.dot(normed_two, w_up, precision=HIGHEST) + hidden_bias)
    activated = low(jax.nn.gelu(hidden, approximate=False))
    return middle + low_back(jnp.dot(activated, w_down, precision=HIGHEST)) + biases[3]

def whole_block(rows_in, lengths, parameters):
    for layer in range(LAYERS):
        rows_in = one_layer(rows_in, lengths, *[item[layer] for item in parameters])
    return rows_in

def reference(x_in, valid_len, w_qkv, w_out, w_up, w_down, norm_gain, norm_shift, bias, up_bias, cotangent):
    parameters = tuple((item.astype(jnp.float32) for item in (w_qkv, w_out, w_up, w_down, norm_gain, norm_shift, bias, up_bias)))
    groups = IMAGES // GROUP_IMAGES
    rows_all = x_in.astype(jnp.float32).reshape(groups, GROUP_IMAGES * SEQ, D)
    cot_all = cotangent.astype(jnp.float32).reshape(groups, GROUP_IMAGES * SEQ, D)
    len_all = valid_len.reshape(groups, GROUP_IMAGES)

    def step(totals, packed):
        rows_in, lengths, cot_rows = packed
        result, pull_back = jax.vjp(lambda rows, params: whole_block(rows, lengths, params), rows_in, parameters)
        grad_rows, grad_params = pull_back(cot_rows)
        totals = jax.tree.map(jnp.add, totals, grad_params)
        return (totals, (result.astype(jnp.bfloat16), grad_rows))
    start = jax.tree.map(jnp.zeros_like, parameters)
    totals, (results, grad_rows) = lax.scan(step, start, (rows_all, len_all, cot_all))
    return (results.reshape(TOKENS, D), grad_rows.reshape(TOKENS, D), totals[0], totals[1], totals[2], totals[3], totals[4], totals[5], totals[6], totals[7])
```

```python
import functools

import jax
import jax.numpy as jnp
from jax import lax
from jax.experimental import pallas as pl
from jax.experimental.pallas import tpu as pltpu
from jax.sharding import PartitionSpec as P

MESH = pl.DeviceIdType.MESH
F32, BF16 = jnp.float32, jnp.bfloat16

D = 1024
ROWS = 146
PAD = 160
COLS = 128
HEAD = 64
HID = 512
MEMBERS = 8
WCOLS = 1536
EPSILON = 1e-06
NEG_FILL = -1e30
VMEM_BYTES = 60 * 1024 * 1024

NN = (((1,), (0,)), ((), ()))
NT = (((1,), (1,)), ((), ()))
TN = (((0,), (0,)), ((), ()))


def dot(a, b, dims=NN):
    return lax.dot_general(a, b, dims, preferred_element_type=F32)


class Place:
    def __init__(self):
        self.dp = lax.axis_index("dp")
        self.tensor = lax.axis_index("tensor")
        self.core = self.dp % 2
        self.pair = self.dp // 2
        self.zlo = self.tensor // 4
        self.x = self.tensor % 4
        self.slot = self.core * 4 + self.x
        self.group = self.pair * 2 + self.zlo

    def peer(self, core, x):
        return {"dp": self.pair * 2 + core, "tensor": self.zlo * 4 + x}

    def sibling(self):
        return self.peer(1 - self.core, self.x)


def greet(me, plane):
    barrier = pltpu.get_barrier_semaphore()

    def member(i, carry):
        pl.semaphore_signal(
            barrier,
            inc=1,
            device_id=me.peer((me.core + i // 4) % 2, (me.x + i) % 4),
            device_id_type=MESH,
        )
        return carry

    lax.fori_loop(1, MEMBERS, member, 0)
    count = MEMBERS - 1
    if plane:

        def other(i, carry):
            pair = (me.pair + i // 4) % 8
            zlo = (me.zlo + (i // 2) % 2) % 2
            pl.semaphore_signal(
                barrier,
                inc=1,
                device_id={"dp": pair * 2 + i % 2, "tensor": zlo * 4 + me.x},
                device_id_type=MESH,
            )
            return carry

        lax.fori_loop(2, 32, other, 0)
        count += 30
    pl.semaphore_wait(barrier, count)


def remote(src, dst, send, recv, device):
    return pltpu.make_async_remote_copy(
        src_ref=src,
        dst_ref=dst,
        send_sem=send,
        recv_sem=recv,
        device_id=device,
        device_id_type=MESH,
    )


def near(o):
    return o + (o // 2) * (5 - 2 * o)


def gather_start(me, g, send, recv):
    own = g.at[me.slot]
    remote(own, own, send.at[4], recv.at[4], me.sibling()).start()
    for dx in (1, 3, 2):
        remote(own, own, send.at[dx], recv.at[dx], me.peer(me.core, (me.x + dx) % 4)).start()


def gather_run(me, g, send, recv, consume):
    def step(i, carry):
        dx, dc = near(i // 2), i % 2
        k = dc * 4 + dx
        slot = ((me.core + dc) % 2) * 4 + (me.x + 4 - dx) % 4
        block = g.at[slot]

        @pl.when(i > 0)
        def _():
            remote(block, block, send.at[k], recv.at[k], me.sibling()).wait_recv()

        @pl.when((dc == 0) & (i > 0))
        def _():
            remote(block, block, send.at[4 + dx], recv.at[4 + dx], me.sibling()).start()

        consume(slot)
        return carry

    lax.fori_loop(0, MEMBERS, step, 0)


def gather_end(me, g, send, recv):
    def step(k, carry):
        block = g.at[0]
        remote(block, block, send.at[k], recv.at[k], me.sibling()).wait_send()
        return carry

    lax.fori_loop(1, MEMBERS, step, 0)


GATHER_SEMS = [pltpu.SemaphoreType.DMA((8,)), pltpu.SemaphoreType.DMA((8,))]

SUM_SCRATCH = [
    pltpu.VMEM((4, PAD, D), BF16),
    pltpu.VMEM((4, PAD, D), BF16),
    pltpu.VMEM((3, PAD, D), BF16),
    pltpu.VMEM((3, PAD, D), BF16),
    pltpu.VMEM((PAD, D), F32),
    pltpu.SemaphoreType.DMA((4,)),
    pltpu.SemaphoreType.DMA((4,)),
    pltpu.SemaphoreType.DMA((3,)),
    pltpu.SemaphoreType.DMA((3,)),
]


def sum_rows(me, produce, bufs, fill=None):
    s1, r1, s2, r2, acc, ss1, rs1, ss2, rs2 = bufs
    sibling = me.sibling()

    def to_sibling(i):
        return remote(s1.at[i], r1.at[i], ss1.at[i], rs1.at[i], sibling)

    def to_chip(i):
        peer = me.peer(me.core, (me.x + i + 1) % 4)
        return remote(s2.at[i], r2.at[i], ss2.at[i], rs2.at[i], peer)

    def first(i, carry):
        s1[i] = produce((1 - me.core) * 4 + (me.x + i + 1) % 4).astype(BF16)
        to_sibling(i).start()
        return carry

    lax.fori_loop(0, 4, first, 0)

    def second(i, carry):
        part = produce(me.core * 4 + (me.x + i + 1) % 4)
        to_sibling(i).wait_recv()
        s2[i] = (part + r1[i].astype(F32)).astype(BF16)
        to_chip(i).start()
        return carry

    lax.fori_loop(0, 3, second, 0)
    part = produce(me.slot)
    to_sibling(3).wait_recv()
    acc[...] = part + r1[3].astype(F32)
    if fill is not None:
        fill()
    for i in range(3):
        to_chip(i).wait_recv()
    total = acc[...] + r2[0].astype(F32) + r2[1].astype(F32) + r2[2].astype(F32)
    for i in range(4):
        to_sibling(i).wait_send()
    for i in range(3):
        to_chip(i).wait_send()
    return total


PLANE_SEMS = [pltpu.SemaphoreType.DMA((16,)), pltpu.SemaphoreType.DMA((16,))]


def weights_copy(me, i, shard, full, send, recv):
    pair, zlo = (me.pair + i // 2) % 8, (me.zlo + i) % 2
    device = {"dp": pair * 2 + me.zlo, "tensor": zlo * 4 + me.x}
    return remote(shard, full.at[me.dp], send.at[i], recv.at[me.dp], device)


def weights_start(me, shard, full, send, recv):
    def step(i, carry):
        weights_copy(me, i, shard, full, send, recv).start()
        return carry

    own = me.core == me.zlo

    @pl.when(own)
    def _():
        pltpu.make_async_copy(shard, full.at[me.dp], recv.at[me.dp]).start()

    @pl.when(jnp.logical_not(own))
    def _():
        weights_copy(me, 0, shard, full, send, recv).start()

    lax.fori_loop(1, 16, step, 0)


def weights_arrived(me, shard, full, send, recv):
    def step(i, carry):
        remote(shard, full.at[i], send.at[i], recv.at[i], me.sibling()).wait_recv()
        return carry

    lax.fori_loop(0, 16, step, 0)


def weights_sent(me, shard, full, send, recv):
    @pl.when(me.core != me.zlo)
    def _():
        weights_copy(me, 0, shard, full, send, recv).wait_send()

    def step(i, carry):
        weights_copy(me, i, shard, full, send, recv).wait_send()
        return carry

    lax.fori_loop(1, 16, step, 0)


def grads_copy(me, i, part, land, send, recv):
    to = (me.dp + i) % 16
    device = {"dp": to, "tensor": me.slot}
    return remote(part.at[to], land.at[me.group], send.at[i], recv.at[me.group], device)


def grads_start(me, part, land, send, recv):
    own = me.zlo == me.core

    @pl.when(own)
    def _():
        pltpu.make_async_copy(part.at[me.dp], land.at[me.group], recv.at[me.group]).start()

    @pl.when(jnp.logical_not(own))
    def _():
        grads_copy(me, 0, part, land, send, recv).start()

    def step(i, carry):
        grads_copy(me, i, part, land, send, recv).start()
        return carry

    lax.fori_loop(1, 16, step, 0)


def grads_end(me, part, land, send, recv, out):
    def arrived(i, carry):
        remote(part.at[0], land.at[i], send.at[i], recv.at[i], me.sibling()).wait_recv()
        return carry

    lax.fori_loop(0, 16, arrived, 0)

    @pl.when(me.zlo != me.core)
    def _():
        grads_copy(me, 0, part, land, send, recv).wait_send()

    def sent(i, carry):
        grads_copy(me, i, part, land, send, recv).wait_send()
        return carry

    lax.fori_loop(1, 16, sent, 0)
    total = land[0].astype(F32)
    for i in range(1, 16):
        total = total + land[i].astype(F32)
    out[...] = total


def normalized(rows):
    centred = rows - jnp.mean(rows, axis=-1, keepdims=True)
    scale = lax.rsqrt(jnp.mean(centred * centred, axis=-1, keepdims=True) + EPSILON)
    return centred * scale, scale


def layer_norm(rows, gain, shift):
    return normalized(rows)[0] * gain + shift


def layer_norm_back(rows, gain, grad):
    unit, scale = normalized(rows)
    inner = grad * gain
    mean_one = jnp.mean(inner, axis=-1, keepdims=True)
    mean_two = jnp.mean(inner * unit, axis=-1, keepdims=True)
    back = scale * (inner - mean_one - unit * mean_two)
    return back, jnp.sum(grad * unit, axis=0, keepdims=True), jnp.sum(grad, axis=0, keepdims=True)


def erf(v):
    v = jnp.clip(v, -4.0, 4.0)
    s = v * v
    top = F32(-2.72614225801306e-10)
    for a in (
        2.77068142495902e-08,
        -2.10102402082508e-06,
        -5.69250639462346e-05,
        -7.34990630326855e-04,
        -2.95459980854025e-03,
        -1.60960333262415e-02,
    ):
        top = top * s + F32(a)
    low = F32(-1.45660718464996e-05)
    for b in (
        -2.13374055278905e-04,
        -1.68282697438203e-03,
        -7.37332916720468e-03,
        -1.42647390514189e-02,
    ):
        low = low * s + F32(b)
    return v * top / low


def normal_below(v):
    return 0.5 * (1.0 + erf(v * F32(0.7071067811865476)))


def gelu_slope(v):
    return normal_below(v) + v * jnp.exp(-0.5 * v * v) * F32(0.3989422804014327)


def weight_grad(left, right, out, at, width):
    def tile(i, carry):
        a = left[:, :, pl.ds(pl.multiple_of(i * 256, 256), 256)].reshape(MEMBERS * PAD, 256)
        b = right[...].reshape(MEMBERS * PAD, width)
        block = dot(a, b, TN).astype(BF16).reshape(4, 64, width)
        out[pl.ds(i * 4, 4), :, at : at + width] = block
        return carry

    lax.fori_loop(0, D // 256, tile, 0)


def columns(w, at, width):
    return w[:, :, at : at + width].reshape(D, width)


def column_sum(ref):
    def step(i, total):
        return total + jnp.sum(ref[i].astype(F32), axis=0, keepdims=True)

    return lax.fori_loop(0, MEMBERS, step, jnp.zeros((1, ref.shape[2]), F32))


def call(kernel, outs, scratch, collective_id, args, flops):
    return pl.pallas_call(
        kernel,
        out_shape=[jax.ShapeDtypeStruct(s, t) for s, t in outs],
        in_specs=[pl.BlockSpec(memory_space=pltpu.VMEM)] * len(args),
        out_specs=[pl.BlockSpec(memory_space=pltpu.VMEM)] * len(outs),
        scratch_shapes=scratch,
        compiler_params=pltpu.CompilerParams(
            collective_id=collective_id, has_side_effects=True, vmem_limit_bytes=VMEM_BYTES
        ),
        cost_estimate=pl.CostEstimate(flops=flops, bytes_accessed=1 << 20, transcendentals=0),
    )(*args)


def project(me, g, w, bias, qkv):
    def consume(slot):
        qkv[slot] = (dot(g[slot], columns(w, 0, 384)) + bias[...]).astype(BF16)

    return consume


def enter_kernel(x, shard, gain, shift, qbias, qkv, normed, w, *sems):
    gs, gr, ws, wr = sems
    me = Place()
    greet(me, True)
    weights_start(me, shard, w, ws, wr)
    normed[me.slot] = layer_norm(x[...].astype(F32), gain[...], shift[...]).astype(BF16)
    gather_start(me, normed, gs, gr)
    weights_arrived(me, shard, w, ws, wr)
    gather_run(me, normed, gs, gr, project(me, normed, w, qbias, qkv))
    gather_end(me, normed, gs, gr)
    weights_sent(me, shard, w, ws, wr)


def forward_rest(me, attended, state, w, gain, shift, bias_out, up_bias, middle, normed, hidden, act, sum1, sum2, gather):
    def out_product(slot):
        return dot(attended[slot], columns(w, 384, 128), NT)

    branch = sum_rows(me, out_product, sum1)
    middle[...] = state[...].astype(F32) + (branch + bias_out[...])
    normed[me.slot] = layer_norm(middle[...], gain[...], shift[...]).astype(BF16)
    gs, gr = gather
    gather_start(me, normed, gs, gr)

    def consume(slot):
        h = dot(normed[slot], columns(w, 512, 512)) + up_bias[...]
        hidden[slot] = h
        act[slot] = (h * normal_below(h)).astype(BF16)

    gather_run(me, normed, gs, gr, consume)

    def down_product(slot):
        return dot(act[slot], columns(w, 1024, 512), NT)

    total = sum_rows(me, down_product, sum2)
    gather_end(me, normed, gs, gr)
    return middle[...] + total


def between_kernel(
    attended, state, w, shard, gain, shift, bias_out, up_bias, bias_down, gain_next, shift_next, qbias,
    middle, normed_two, hidden, act, new_state, normed_next, qkv, w_next, *scratch,
):
    sum1, sum2, g1, g2, wsem = scratch[0:9], scratch[9:18], scratch[18:20], scratch[20:22], scratch[22:24]
    me = Place()
    greet(me, True)
    weights_start(me, shard, w_next, *wsem)
    new_state[...] = (
        forward_rest(
            me, attended, state, w, gain, shift, bias_out, up_bias, middle, normed_two, hidden, act, sum1, sum2, g1
        )
        + bias_down[...]
    )
    normed_next[me.slot] = layer_norm(new_state[...], gain_next[...], shift_next[...]).astype(BF16)
    gather_start(me, normed_next, *g2)
    weights_arrived(me, shard, w_next, *wsem)
    gather_run(me, normed_next, *g2, project(me, normed_next, w_next, qbias, qkv))
    gather_end(me, normed_next, *g2)
    weights_sent(me, shard, w_next, *wsem)


def backward_rest(
    me, g_own, g_rows, w, hidden, act, normed, middle, gain, grad_hid, dw, grad_mid, g_attn, grad_att, wide, row, up_sum,
    gather1, sums, gather2,
):
    def consume(slot):
        grad_act = dot(g_rows[slot], columns(w, 1024, 512))
        grad_hid[slot] = (grad_act * gelu_slope(hidden[slot])).astype(BF16)

    gather_run(me, g_rows, *gather1, consume)

    def up_back(slot):
        return dot(grad_hid[slot], columns(w, 512, 512), NT)

    def fill():
        weight_grad(g_rows, act, dw, 512, 512)
        up_sum[...] = column_sum(grad_hid)

    grad = sum_rows(me, up_back, sums, fill)
    gather_end(me, g_rows, *gather1)
    back, gain_sum, shift_sum = layer_norm_back(middle[...], gain[...], grad)
    mid = g_own[...].astype(F32) + back
    grad_mid[...] = mid
    g_attn[me.slot] = mid.astype(BF16)
    gather_start(me, g_attn, *gather2)
    wide[row : row + 1] = jnp.sum(g_own[...].astype(F32), axis=0, keepdims=True)
    wide[row + 1 : row + 2] = gain_sum
    wide[row + 2 : row + 3] = shift_sum
    wide[row + 3 : row + 4] = jnp.sum(mid, axis=0, keepdims=True)
    weight_grad(normed, grad_hid, dw, 0, 512)

    def att_back(slot):
        grad_att[slot] = dot(g_attn[slot], columns(w, 384, 128)).astype(BF16)

    gather_run(me, g_attn, *gather2, att_back)
    gather_end(me, g_attn, *gather2)


def turn_kernel(
    attended, state, w, cot, gain, shift, bias_out, up_bias, bias_down,
    out_rows, dw, grad_mid, g_attn, grad_att, wide, up_sum, *scratch,
):
    sum1, sum2, sum3 = scratch[0:9], scratch[9:18], scratch[18:27]
    g1, g2, g3 = scratch[27:29], scratch[29:31], scratch[31:33]
    middle, normed, hidden, act, g_rows, grad_hid = scratch[33:39]
    me = Place()
    greet(me, False)
    g_rows[me.slot] = cot[...]
    gather_start(me, g_rows, *g2)
    total = forward_rest(
        me, attended, state, w, gain, shift, bias_out, up_bias, middle, normed, hidden, act, sum1, sum2, g1
    )
    out_rows[...] = (total + bias_down[...]).astype(BF16)
    wide[...] = jnp.zeros_like(wide)
    backward_rest(
        me, cot, g_rows, w, hidden, act, normed, middle, gain, grad_hid, dw, grad_mid, g_attn, grad_att, wide, 0, up_sum,
        g2, sum3, g3,
    )


def first_back(me, grad_qkv, normed_one, w, g_attn, attended, state, grad_mid, gain, dwb, wide, row, q_sum, sums, more):
    def back_product(slot):
        return dot(grad_qkv[slot], columns(w, 0, 384), NT)

    def fill():
        weight_grad(normed_one, grad_qkv, dwb, 0, 384)
        weight_grad(g_attn, attended, dwb, 384, 128)
        more()
        q_sum[...] = column_sum(grad_qkv)

    grad = sum_rows(me, back_product, sums, fill)
    back, gain_sum, shift_sum = layer_norm_back(state[...].astype(F32), gain[...], grad)
    wide[row : row + 1] = gain_sum
    wide[row + 1 : row + 2] = shift_sum
    return grad_mid[...] + back


def back_kernel(
    grad_qkv, normed_one, w, g_attn_one, attended_one, state, grad_mid_one, gain_one, dwa_one,
    w_low, hidden, act, normed_two, middle, gain_two,
    suma, sumb, dw, grad_mid, g_attn, grad_att, wide, up_sum, q_sum, *scratch,
):
    sum1, sum2 = scratch[0:9], scratch[9:18]
    g2, g3 = scratch[18:20], scratch[20:22]
    pa, pb = scratch[22:24], scratch[24:26]
    landa, landb, dwb, gradient, g_rows, grad_hid = scratch[26:32]
    me = Place()
    greet(me, True)
    grads_start(me, dwa_one, landa, *pa)
    wide[...] = jnp.zeros_like(wide)

    def more():
        grads_start(me, dwb, landb, *pb)

    gradient[...] = first_back(
        me, grad_qkv, normed_one, w, g_attn_one, attended_one, state, grad_mid_one, gain_one, dwb, wide, 0, q_sum,
        sum1, more,
    )
    g_rows[me.slot] = gradient[...].astype(BF16)
    gather_start(me, g_rows, *g2)
    backward_rest(
        me, gradient, g_rows, w_low, hidden, act, normed_two, middle, gain_two, grad_hid, dw, grad_mid, g_attn,
        grad_att, wide, 2, up_sum, g2, sum2, g3,
    )
    grads_end(me, dwa_one, landa, *pa, suma)
    grads_end(me, dwb, landb, *pb, sumb)


def vectors_start(me, wide, va, vl, send, recv):
    for s in range(MEMBERS):
        va[s] = wide[:, s * 128 : (s + 1) * 128]

    def step(i, carry):
        core, x = (me.core + i // 4) % 2, (me.x + i) % 4
        remote(va.at[core * 4 + x], vl.at[i], send.at[i], recv.at[i], me.peer(core, x)).start()
        return carry

    lax.fori_loop(1, MEMBERS, step, 0)


def vectors_end(me, narrow, va, vl, send, recv, vb, piece, send2, recv2, out, send3, recv3):
    total = va[me.slot]
    for i in range(1, MEMBERS):
        remote(va.at[0], vl.at[i], send.at[i], recv.at[i], me.sibling()).wait()
        total = total + vl[i]
    piece[0:16] = total
    piece[16:32] = narrow[...]

    def to_group(i):
        pair, zlo = (me.pair + i // 2) % 8, (me.zlo + i) % 2
        device = {"dp": pair * 2 + me.core, "tensor": zlo * 4 + me.x}
        return remote(piece, vb.at[me.group], send2.at[i], recv2.at[me.group], device)

    def start(i, carry):
        to_group(i).start()
        return carry

    lax.fori_loop(1, 16, start, 0)
    vb[me.group] = piece[...]

    def end(i, carry):
        to_group(i).wait_send()
        group = (me.group + i) % 16
        remote(piece, vb.at[group], send2.at[i], recv2.at[group], me.sibling()).wait_recv()
        return carry

    lax.fori_loop(1, 16, end, 0)
    total = vb[0]
    for i in range(1, 16):
        total = total + vb[i]
    out[me.slot] = total
    own = out.at[me.slot]

    def to_member(i):
        core, x = (me.core + i // 4) % 2, (me.x + i) % 4
        return remote(own, own, send3.at[i], recv3.at[me.slot], me.peer(core, x))

    def start_three(i, carry):
        to_member(i).start()
        return carry

    lax.fori_loop(1, MEMBERS, start_three, 0)

    def end_three(i, carry):
        to_member(i).wait_send()
        slot = ((me.core + i // 4) % 2) * 4 + (me.x + i) % 4
        remote(own, out.at[slot], send3.at[i], recv3.at[slot], me.sibling()).wait_recv()
        return carry

    lax.fori_loop(1, MEMBERS, end_three, 0)


def exit_kernel(
    grad_qkv, normed_one, w, g_attn, attended, state, grad_mid, gain, dwa, wide_in, narrow_in,
    gradient, suma, sumb, vectors, *scratch,
):
    sum1, pa, pb = scratch[0:9], scratch[9:11], scratch[11:13]
    landa, landb, dwb, wide, q_sum, narrow, va, vl, vb, piece = scratch[13:23]
    v1, v2, v3 = scratch[23:25], scratch[25:27], scratch[27:29]
    me = Place()
    greet(me, True)
    grads_start(me, dwa, landa, *pa)

    def more():
        grads_start(me, dwb, landb, *pb)

    wide[...] = wide_in[...]
    gradient[...] = first_back(
        me, grad_qkv, normed_one, w, g_attn, attended, state, grad_mid, gain, dwb, wide, 0, q_sum, sum1, more
    )
    narrow[...] = narrow_in[...]
    narrow[0:1] = q_sum[:, 0:128]
    narrow[1:2] = q_sum[:, 256:384]
    vectors_start(me, wide, va, vl, *v1)
    vectors_end(me, narrow, va, vl, *v1, vb, piece, *v2, vectors, *v3)
    grads_end(me, dwa, landa, *pa, suma)
    grads_end(me, dwb, landb, *pb, sumb)


def key_mask(shape, dim, length):
    at = lax.broadcasted_iota(jnp.int32, shape, dim)
    block = (at >= PAD).astype(jnp.int32) + (at >= 2 * PAD).astype(jnp.int32) + (at >= 3 * PAD).astype(jnp.int32)
    row = at - block * PAD
    return (row < ROWS) & (row + block * ROWS < length)


def head_parts(qkv, at):
    return qkv[:, :, at * COLS : (at + 1) * COLS].reshape(4 * PAD, COLS)


def attend_kernel(length, qkv, out):
    q, k, v = (head_parts(qkv, i) for i in range(3))
    valid = key_mask((1, 4 * PAD), 1, length[pl.program_id(0)])
    lane = lax.broadcasted_iota(jnp.int32, (1, COLS), 1)
    total = None
    for h in range(2):
        mine = (lane >= h * HEAD) & (lane < (h + 1) * HEAD)
        scores = dot(jnp.where(mine, q, jnp.zeros_like(q)), k, NT) * F32(HEAD**-0.5)
        scores = jnp.where(valid, scores, NEG_FILL)
        e = jnp.exp(scores - jnp.max(scores, axis=-1, keepdims=True))
        prob = (e * (1.0 / jnp.sum(e, axis=-1, keepdims=True))).astype(BF16)
        mixed = dot(prob, v)
        total = mixed if total is None else jnp.where(mine, mixed, total)
    out[...] = total.astype(BF16).reshape(4, PAD, COLS)


def attend_back_kernel(length, qkv, grad, out):
    q, k, v = (head_parts(qkv, i) for i in range(3))
    g = grad[...].reshape(4 * PAD, COLS)
    valid = key_mask((4 * PAD, 1), 0, length[pl.program_id(0)])
    lane = lax.broadcasted_iota(jnp.int32, (1, COLS), 1)
    parts = [None, None, None]
    for h in range(2):
        mine = (lane >= h * HEAD) & (lane < (h + 1) * HEAD)
        scores = dot(k, jnp.where(mine, q, jnp.zeros_like(q)), NT) * F32(HEAD**-0.5)
        scores = jnp.where(valid, scores, NEG_FILL)
        e = jnp.exp(scores - jnp.max(scores, axis=0, keepdims=True))
        prob = e * (1.0 / jnp.sum(e, axis=0, keepdims=True))
        grad_value = dot(prob.astype(BF16), g)
        grad_prob = dot(v, jnp.where(mine, g, jnp.zeros_like(g)), NT)
        inner = jnp.sum(grad_prob * prob, axis=0, keepdims=True)
        grad_scores = (prob * (grad_prob - inner)).astype(BF16)
        grad_key = dot(grad_scores, q) * F32(HEAD**-0.5)
        grad_query = dot(grad_scores, k, TN) * F32(HEAD**-0.5)
        new = [grad_query, grad_key, grad_value]
        parts = new if h == 0 else [jnp.where(mine, n, p) for n, p in zip(new, parts)]
    for i in range(3):
        out[:, :, i * COLS : (i + 1) * COLS] = parts[i].astype(BF16).reshape(4, PAD, COLS)


def attention(kernel, length, arrays, width):
    def spec(w):
        return pl.BlockSpec((4, PAD, w), lambda i: (i, 0, 0))

    return pl.pallas_call(
        kernel,
        grid=(2,),
        out_shape=jax.ShapeDtypeStruct((MEMBERS, PAD, width), BF16),
        in_specs=[pl.BlockSpec(memory_space=pltpu.SMEM)] + [spec(a.shape[2]) for a in arrays],
        out_specs=spec(width),
        compiler_params=pltpu.CompilerParams(vmem_limit_bytes=VMEM_BYTES),
    )(length, *arrays)


def swap(value):
    pairs = []
    for pair in range(8):
        for a in range(2):
            for b in range(2):
                for x in range(4):
                    pairs.append(((pair * 2 + a) * 8 + b * 4 + x, (pair * 2 + b) * 8 + a * 4 + x))
    return lax.ppermute(value, ("dp", "tensor"), pairs)


def per_device(
    x_in, valid_len, w_qkv, w_out, w_up, w_down, norm_gain, norm_shift, bias, up_bias, cotangent
):
    dp, tensor = lax.axis_index("dp"), lax.axis_index("tensor")
    slot = (dp % 2) * 4 + tensor % 4

    def padded(rows):
        return jnp.pad(rows, ((0, PAD - ROWS), (0, 0)))

    x = padded(swap(x_in))
    cot = padded(swap(cotangent))
    length = swap(valid_len)
    shards = jnp.concatenate(
        [
            w_qkv.reshape(2, 64, 384),
            jnp.swapaxes(w_out, 1, 2),
            w_up,
            jnp.swapaxes(w_down, 1, 2),
        ],
        axis=2,
    )
    gain = [[norm_gain[l, i][None] for i in range(2)] for l in range(2)]
    shift = [[norm_shift[l, i][None] for i in range(2)] for l in range(2)]
    bias_rows = [[bias[l, i][None] for i in range(4)] for l in range(2)]
    own_bias = lax.dynamic_slice_in_dim(bias, slot * COLS, COLS, axis=2)
    own_up = lax.dynamic_slice_in_dim(up_bias, slot * HID, HID, axis=1)
    qbias = [
        jnp.concatenate([own_bias[l, 0], jnp.zeros((COLS,), F32), own_bias[l, 1]])[None] for l in range(2)
    ]
    ubias = [own_up[l][None] for l in range(2)]

    rows_all, rows_own = (MEMBERS, PAD, D), (PAD, D)
    qkv0, normed0, w0 = call(
        enter_kernel,
        [((MEMBERS, PAD, 384), BF16), (rows_all, BF16), ((16, 64, WCOLS), BF16)],
        GATHER_SEMS + PLANE_SEMS,
        0,
        [x, shards[0], gain[0][0], shift[0][0], qbias[0]],
        1 << 30,
    )
    attended0 = attention(attend_kernel, length, [qkv0], COLS)
    middle0, normed_two0, hidden0, act0, state1, normed1, qkv1, w1 = call(
        between_kernel,
        [
            (rows_own, F32),
            (rows_all, BF16),
            ((MEMBERS, PAD, HID), F32),
            ((MEMBERS, PAD, HID), BF16),
            (rows_own, F32),
            (rows_all, BF16),
            ((MEMBERS, PAD, 384), BF16),
            ((16, 64, WCOLS), BF16),
        ],
        SUM_SCRATCH * 2 + GATHER_SEMS * 2 + PLANE_SEMS,
        1,
        [
            attended0, x, w0, shards[1], gain[0][1], shift[0][1], bias_rows[0][2], ubias[0], bias_rows[0][3],
            gain[1][0], shift[1][0], qbias[1],
        ],
        4 << 30,
    )
    attended1 = attention(attend_kernel, length, [qkv1], COLS)
    out_rows, dwa1, grad_mid1, g_attn1, grad_att1, wide1, up1 = call(
        turn_kernel,
        [
            (rows_own, BF16),
            ((16, 64, 1024), BF16),
            (rows_own, F32),
            (rows_all, BF16),
            ((MEMBERS, PAD, COLS), BF16),
            ((8, D), F32),
            ((1, HID), F32),
        ],
        SUM_SCRATCH * 3
        + GATHER_SEMS * 3
        + [
            pltpu.VMEM(rows_own, F32),
            pltpu.VMEM(rows_all, BF16),
            pltpu.VMEM((MEMBERS, PAD, HID), F32),
            pltpu.VMEM((MEMBERS, PAD, HID), BF16),
            pltpu.VMEM(rows_all, BF16),
            pltpu.VMEM((MEMBERS, PAD, HID), BF16),
        ],
        2,
        [attended1, state1, w1, cot, gain[1][1], shift[1][1], bias_rows[1][2], ubias[1], bias_rows[1][3]],
        8 << 30,
    )
    out_rows = swap(out_rows[:ROWS])
    grad_qkv1 = attention(attend_back_kernel, length, [qkv1, grad_att1], 384)
    suma1, sumb1, dwa0, grad_mid0, g_attn0, grad_att0, wide0, up0, q1 = call(
        back_kernel,
        [
            ((64, 1024), F32),
            ((64, 512), F32),
            ((16, 64, 1024), BF16),
            (rows_own, F32),
            (rows_all, BF16),
            ((MEMBERS, PAD, COLS), BF16),
            ((8, D), F32),
            ((1, HID), F32),
            ((1, 384), F32),
        ],
        SUM_SCRATCH * 2
        + GATHER_SEMS * 2
        + PLANE_SEMS * 2
        + [
            pltpu.VMEM((16, 64, 1024), BF16),
            pltpu.VMEM((16, 64, 512), BF16),
            pltpu.VMEM((16, 64, 512), BF16),
            pltpu.VMEM(rows_own, F32),
            pltpu.VMEM(rows_all, BF16),
            pltpu.VMEM((MEMBERS, PAD, HID), BF16),
        ],
        3,
        [
            grad_qkv1, normed1, w1, g_attn1, attended1, state1, grad_mid1, gain[1][0], dwa1,
            w0, hidden0, act0, normed_two0, middle0, gain[0][1],
        ],
        8 << 30,
    )
    grad_qkv0 = attention(attend_back_kernel, length, [qkv0, grad_att0], 384)
    wide = jnp.concatenate(
        [jnp.zeros((2, D), F32), wide0[2:6], wide0[0:2], wide1[0:4], jnp.zeros((4, D), F32)], axis=0
    )
    zeros = jnp.zeros((2, COLS), F32)
    narrow = jnp.concatenate(
        [
            zeros,
            up0.reshape(4, COLS),
            q1[:, 0:COLS],
            q1[:, 2 * COLS :],
            up1.reshape(4, COLS),
            jnp.zeros((4, COLS), F32),
        ],
        axis=0,
    )
    gradient, suma0, sumb0, vectors = call(
        exit_kernel,
        [(rows_own, F32), ((64, 1024), F32), ((64, 512), F32), ((MEMBERS, 32, 128), F32)],
        SUM_SCRATCH
        + PLANE_SEMS * 2
        + [
            pltpu.VMEM((16, 64, 1024), BF16),
            pltpu.VMEM((16, 64, 512), BF16),
            pltpu.VMEM((16, 64, 512), BF16),
            pltpu.VMEM((16, D), F32),
            pltpu.VMEM((1, 384), F32),
            pltpu.VMEM((16, 128), F32),
            pltpu.VMEM((MEMBERS, 16, 128), F32),
            pltpu.VMEM((MEMBERS, 16, 128), F32),
            pltpu.VMEM((16, 32, 128), F32),
            pltpu.VMEM((32, 128), F32),
        ]
        + [pltpu.SemaphoreType.DMA((8,))] * 2
        + PLANE_SEMS
        + [pltpu.SemaphoreType.DMA((8,))] * 2,
        4,
        [grad_qkv0, normed0, w0, g_attn0, attended0, x, grad_mid0, gain[0][0], dwa0, wide, narrow],
        4 << 30,
    )
    suma, sumb = jnp.stack([suma0, suma1]), jnp.stack([sumb0, sumb1])
    full = jnp.transpose(vectors[:, 0:12], (1, 0, 2)).reshape(2, 6, D)
    own = vectors[:, 16:28].reshape(MEMBERS, 2, 6, COLS)
    q_bias = jnp.transpose(own[:, :, 0], (1, 0, 2)).reshape(2, D)
    v_bias = jnp.transpose(own[:, :, 1], (1, 0, 2)).reshape(2, D)
    return (
        out_rows,
        swap(gradient[:ROWS]),
        sumb[:, :, 0:384].reshape(2, 64, 3, COLS),
        jnp.swapaxes(sumb[:, :, 384:], 1, 2),
        suma[:, :, 0:HID],
        jnp.swapaxes(suma[:, :, HID:], 1, 2),
        jnp.stack([full[:, 0], full[:, 3]], axis=1),
        jnp.stack([full[:, 1], full[:, 4]], axis=1),
        jnp.stack([q_bias, v_bias, full[:, 5], full[:, 2]], axis=1),
        jnp.transpose(own[:, :, 2:], (1, 0, 2, 3)).reshape(2, 4096),
    )


def solution(mesh):
    rows = P(("dp", "tensor"), None)
    weights = (P(None, "dp", None, "tensor"), P(None, "tensor", "dp"), P(None, "dp", "tensor"), P(None, "tensor", "dp"))
    return jax.shard_map(
        per_device,
        mesh=mesh,
        in_specs=(rows, P("dp"), *weights, P(), P(), P(), P(), rows),
        out_specs=(rows, rows, *weights, P(), P(), P(), P()),
        check_vma=False,
    )
```

```python
import functools

import jax
import jax.numpy as jnp
from jax import lax
from jax.experimental import pallas as pl
from jax.experimental.pallas import tpu as pltpu
from jax.sharding import PartitionSpec as P

MESH = pl.DeviceIdType.MESH
F32, BF16 = jnp.float32, jnp.bfloat16

D = 1024
ROWS = 146
PAD = 160
COLS = 128
HEAD = 64
HID = 512
MEMBERS = 8
WCOLS = 1536
EPSILON = 1e-06
NEG_FILL = -1e30
VMEM_BYTES = 60 * 1024 * 1024

NN = (((1,), (0,)), ((), ()))
NT = (((1,), (1,)), ((), ()))
TN = (((0,), (0,)), ((), ()))


def dot(a, b, dims=NN):
    return lax.dot_general(a, b, dims, preferred_element_type=F32)


class Place:
    def __init__(self):
        self.dp = lax.axis_index("dp")
        self.tensor = lax.axis_index("tensor")
        self.core = self.dp % 2
        self.pair = self.dp // 2
        self.zlo = self.tensor // 4
        self.x = self.tensor % 4
        self.slot = self.core * 4 + self.x
        self.group = self.pair * 2 + self.zlo

    def peer(self, core, x):
        return {"dp": self.pair * 2 + core, "tensor": self.zlo * 4 + x}

    def sibling(self):
        return self.peer(1 - self.core, self.x)


def greet(me, plane):
    barrier = pltpu.get_barrier_semaphore()

    def member(i, carry):
        pl.semaphore_signal(
            barrier,
            inc=1,
            device_id=me.peer((me.core + i // 4) % 2, (me.x + i) % 4),
            device_id_type=MESH,
        )
        return carry

    lax.fori_loop(1, MEMBERS, member, 0)
    count = MEMBERS - 1
    if plane:

        def other(i, carry):
            pair = (me.pair + i // 4) % 8
            zlo = (me.zlo + (i // 2) % 2) % 2
            pl.semaphore_signal(
                barrier,
                inc=1,
                device_id={"dp": pair * 2 + i % 2, "tensor": zlo * 4 + me.x},
                device_id_type=MESH,
            )
            return carry

        lax.fori_loop(2, 32, other, 0)
        count += 30
    pl.semaphore_wait(barrier, count)


def remote(src, dst, send, recv, device):
    return pltpu.make_async_remote_copy(
        src_ref=src,
        dst_ref=dst,
        send_sem=send,
        recv_sem=recv,
        device_id=device,
        device_id_type=MESH,
    )


def slot_at(me, i):
    sibling = (i == 1) | (i == 4) | (i == 5) | (i == 7)
    far = (i >= 6).astype(jnp.int32) * 2
    left = ((i == 2) | (i == 4)).astype(jnp.int32) * 3
    right = ((i == 3) | (i == 5)).astype(jnp.int32)
    core = (me.core + sibling.astype(jnp.int32)) % 2
    return core * 4 + (me.x + far + left + right) % 4


HALF = PAD // 2
TOP, BOTTOM = pl.ds(0, HALF), pl.ds(HALF, HALF)


class Gather:
    def __init__(self, me, g, send, recv):
        self.me, self.g, self.send, self.recv = me, g, send, recv
        self.right = me.peer(me.core, (me.x + 1) % 4)
        self.left = me.peer(me.core, (me.x + 3) % 4)
        self.from_left = me.core * 4 + (me.x + 3) % 4
        self.from_right = me.core * 4 + (me.x + 1) % 4
        self.from_far = me.core * 4 + (me.x + 2) % 4

    def copy(self, k, slot, rows, device):
        block = self.g.at[slot] if rows is None else self.g.at[slot, rows]
        return remote(block, block, self.send.at[k], self.recv.at[k], device)

    def table(self):
        me = self.me
        sibling = me.sibling()
        return [
            (0, me.slot, TOP, self.right),
            (1, me.slot, BOTTOM, self.right),
            (2, me.slot, TOP, self.left),
            (3, me.slot, BOTTOM, self.left),
            (4, self.from_left, TOP, self.right),
            (5, self.from_right, BOTTOM, self.left),
            (6, me.slot, None, sibling),
            (7, self.from_left, None, sibling),
            (8, self.from_right, None, sibling),
            (9, self.from_far, None, sibling),
        ]

    def start_copies(self, *which):
        for k in which:
            self.copy(*self.table()[k]).start()

    def start(self):
        self.start_copies(6, 0, 3, 1, 2)

    def arrived(self, *which):
        for k in which:
            _, slot, rows, device = self.table()[k]
            self.copy(k, slot, rows, device).wait_recv()

    def relay(self):
        self.arrived(0)
        self.start_copies(4)
        self.arrived(3)
        self.start_copies(5)

    def run(self, consume, fill=None, relayed=False):
        def step(i, carry):
            @pl.when(i == 1)
            def _():
                self.arrived(6)

            @pl.when(i == 2)
            def _():
                if not relayed:
                    self.relay()
                if fill is not None:
                    fill()
                self.arrived(1)
                self.start_copies(7)

            @pl.when(i == 3)
            def _():
                self.arrived(2)
                self.start_copies(8)

            @pl.when(i == 4)
            def _():
                self.arrived(7)

            @pl.when(i == 5)
            def _():
                self.arrived(8)

            @pl.when(i == 6)
            def _():
                self.arrived(4, 5)
                self.start_copies(9)

            @pl.when(i == 7)
            def _():
                self.arrived(9)

            consume(slot_at(self.me, i))
            return carry

        lax.fori_loop(0, MEMBERS, step, 0)

    def end(self):
        for row in self.table():
            self.copy(*row).wait_send()


GATHER_SEMS = [pltpu.SemaphoreType.DMA((10,)), pltpu.SemaphoreType.DMA((10,))]

SUM_SCRATCH = [
    pltpu.VMEM((4, PAD, D), BF16),
    pltpu.VMEM((4, PAD, D), BF16),
    pltpu.VMEM((3, PAD, D), BF16),
    pltpu.VMEM((PAD, D), BF16),
    pltpu.VMEM((2, PAD, D), BF16),
    pltpu.VMEM((PAD, D), F32),
    pltpu.VMEM((2, HALF, D), F32),
    pltpu.SemaphoreType.DMA((4,)),
    pltpu.SemaphoreType.DMA((4,)),
    pltpu.SemaphoreType.DMA((6,)),
    pltpu.SemaphoreType.DMA((6,)),
]
NSUM = len(SUM_SCRATCH)


def sum_rows(me, produce, bufs, fill=None):
    s1, r1, s2, ra, rb, acc, hold, ss1, rs1, ss2, rs2 = bufs
    sibling = me.sibling()
    right, left = me.peer(me.core, (me.x + 1) % 4), me.peer(me.core, (me.x + 3) % 4)

    def chip(i):
        return (me.x + 2 + (i == 1).astype(jnp.int32) * 3 + (i == 2).astype(jnp.int32) + (i == 3).astype(jnp.int32) * 2) % 4

    def to_sibling(i):
        return remote(s1.at[i], r1.at[i], ss1.at[i], rs1.at[i], sibling)

    def along(k):
        src, dst, device = (
            (s2.at[0, TOP], ra.at[TOP], right),
            (s2.at[0, BOTTOM], ra.at[BOTTOM], left),
            (s2.at[1, BOTTOM], rb.at[0, BOTTOM], right),
            (s2.at[2, TOP], rb.at[1, TOP], left),
            (s2.at[1, TOP], rb.at[0, TOP], right),
            (s2.at[2, BOTTOM], rb.at[1, BOTTOM], left),
        )[k]
        return remote(src, dst, ss2.at[k], rs2.at[k], device)

    def for_sibling(i, carry):
        s1[i] = produce((1 - me.core) * 4 + chip(i)).astype(BF16)
        to_sibling(i).start()
        return carry

    def own(i, carry):
        part = produce(me.core * 4 + chip(i))
        to_sibling(i).wait_recv()
        acc[...] = part + r1[i].astype(F32)

        @pl.when(i == 0)
        def _():
            s2[0] = acc[...].astype(BF16)
            along(0).start()
            along(1).start()

        @pl.when(i == 1)
        def _():
            s2[1, BOTTOM] = acc[BOTTOM].astype(BF16)
            along(2).start()
            hold[0] = acc[TOP]

        @pl.when(i == 2)
        def _():
            s2[2, TOP] = acc[TOP].astype(BF16)
            along(3).start()
            hold[1] = acc[BOTTOM]

        @pl.when(i < 2)
        def _():
            for_sibling(i + 2, 0)

        return carry

    lax.fori_loop(0, 2, for_sibling, 0)
    lax.fori_loop(0, 4, own, 0)
    along(0).wait_recv()
    s2[1, TOP] = (hold[0] + ra[TOP].astype(F32)).astype(BF16)
    along(4).start()
    along(1).wait_recv()
    s2[2, BOTTOM] = (hold[1] + ra[BOTTOM].astype(F32)).astype(BF16)
    along(5).start()
    if fill is not None:
        fill()
    for k in range(2, 6):
        along(k).wait_recv()
    total = acc[...] + rb[0].astype(F32) + rb[1].astype(F32)
    for i in range(4):
        to_sibling(i).wait_send()
    for k in range(6):
        along(k).wait_send()
    return total


PLANE_SEMS = [pltpu.SemaphoreType.DMA((16,)), pltpu.SemaphoreType.DMA((16,))]


def weights_copy(me, i, shard, full, send, recv):
    pair, zlo = (me.pair + i // 2) % 8, (me.zlo + i) % 2
    device = {"dp": pair * 2 + me.zlo, "tensor": zlo * 4 + me.x}
    return remote(shard, full.at[me.dp], send.at[i], recv.at[me.dp], device)


def weights_start(me, shard, full, send, recv):
    def step(i, carry):
        weights_copy(me, i, shard, full, send, recv).start()
        return carry

    own = me.core == me.zlo

    @pl.when(own)
    def _():
        pltpu.make_async_copy(shard, full.at[me.dp], recv.at[me.dp]).start()

    @pl.when(jnp.logical_not(own))
    def _():
        weights_copy(me, 0, shard, full, send, recv).start()

    lax.fori_loop(1, 16, step, 0)


def weights_arrived(me, shard, full, send, recv):
    def step(i, carry):
        remote(shard, full.at[i], send.at[i], recv.at[i], me.sibling()).wait_recv()
        return carry

    lax.fori_loop(0, 16, step, 0)


def weights_sent(me, shard, full, send, recv):
    @pl.when(me.core != me.zlo)
    def _():
        weights_copy(me, 0, shard, full, send, recv).wait_send()

    def step(i, carry):
        weights_copy(me, i, shard, full, send, recv).wait_send()
        return carry

    lax.fori_loop(1, 16, step, 0)


def grads_copy(me, i, part, land, send, recv):
    to = (me.dp + i) % 16
    device = {"dp": to, "tensor": me.slot}
    return remote(part.at[to], land.at[me.group], send.at[i], recv.at[me.group], device)


def grads_start(me, part, land, send, recv):
    own = me.zlo == me.core

    @pl.when(own)
    def _():
        pltpu.make_async_copy(part.at[me.dp], land.at[me.group], recv.at[me.group]).start()

    @pl.when(jnp.logical_not(own))
    def _():
        grads_copy(me, 0, part, land, send, recv).start()

    def step(i, carry):
        grads_copy(me, i, part, land, send, recv).start()
        return carry

    lax.fori_loop(1, 16, step, 0)


def grads_end(me, part, land, send, recv, out):
    def arrived(i, carry):
        remote(part.at[0], land.at[i], send.at[i], recv.at[i], me.sibling()).wait_recv()
        return carry

    lax.fori_loop(0, 16, arrived, 0)

    @pl.when(me.zlo != me.core)
    def _():
        grads_copy(me, 0, part, land, send, recv).wait_send()

    def sent(i, carry):
        grads_copy(me, i, part, land, send, recv).wait_send()
        return carry

    lax.fori_loop(1, 16, sent, 0)
    total = land[0].astype(F32)
    for i in range(1, 16):
        total = total + land[i].astype(F32)
    out[...] = total


def normalized(rows):
    centred = rows - jnp.mean(rows, axis=-1, keepdims=True)
    scale = lax.rsqrt(jnp.mean(centred * centred, axis=-1, keepdims=True) + EPSILON)
    return centred * scale, scale


def layer_norm(rows, gain, shift):
    return normalized(rows)[0] * gain + shift


def layer_norm_back(rows, gain, grad):
    unit, scale = normalized(rows)
    inner = grad * gain
    mean_one = jnp.mean(inner, axis=-1, keepdims=True)
    mean_two = jnp.mean(inner * unit, axis=-1, keepdims=True)
    back = scale * (inner - mean_one - unit * mean_two)
    return back, jnp.sum(grad * unit, axis=0, keepdims=True), jnp.sum(grad, axis=0, keepdims=True)


def erf(v):
    v = jnp.clip(v, -4.0, 4.0)
    s = v * v
    top = F32(-2.72614225801306e-10)
    for a in (
        2.77068142495902e-08,
        -2.10102402082508e-06,
        -5.69250639462346e-05,
        -7.34990630326855e-04,
        -2.95459980854025e-03,
        -1.60960333262415e-02,
    ):
        top = top * s + F32(a)
    low = F32(-1.45660718464996e-05)
    for b in (
        -2.13374055278905e-04,
        -1.68282697438203e-03,
        -7.37332916720468e-03,
        -1.42647390514189e-02,
    ):
        low = low * s + F32(b)
    return v * top / low


def normal_below(v):
    return 0.5 * (1.0 + erf(v * F32(0.7071067811865476)))


def gelu_slope(v):
    return normal_below(v) + v * jnp.exp(-0.5 * v * v) * F32(0.3989422804014327)


def weight_grad(left, right, out, at, width):
    def tile(i, carry):
        a = left[:, :, pl.ds(pl.multiple_of(i * 256, 256), 256)].reshape(MEMBERS * PAD, 256)
        b = right[...].reshape(MEMBERS * PAD, width)
        block = dot(a, b, TN).astype(BF16).reshape(4, 64, width)
        out[pl.ds(i * 4, 4), :, at : at + width] = block
        return carry

    lax.fori_loop(0, D // 256, tile, 0)


def columns(w, at, width):
    return w[:, :, at : at + width].reshape(D, width)


def column_sum(ref):
    def step(i, total):
        return total + jnp.sum(ref[i].astype(F32), axis=0, keepdims=True)

    return lax.fori_loop(0, MEMBERS, step, jnp.zeros((1, ref.shape[2]), F32))


def call(kernel, outs, scratch, collective_id, args, flops):
    return pl.pallas_call(
        kernel,
        out_shape=[jax.ShapeDtypeStruct(s, t) for s, t in outs],
        in_specs=[pl.BlockSpec(memory_space=pltpu.VMEM)] * len(args),
        out_specs=[pl.BlockSpec(memory_space=pltpu.VMEM)] * len(outs),
        scratch_shapes=scratch,
        compiler_params=pltpu.CompilerParams(
            collective_id=collective_id, has_side_effects=True, vmem_limit_bytes=VMEM_BYTES
        ),
        cost_estimate=pl.CostEstimate(flops=flops, bytes_accessed=1 << 20, transcendentals=0),
    )(*args)


class Weights:
    def __init__(self, me, shard, full, send, recv):
        self.args = (me, shard, full, send, recv)

    def start(self):
        weights_start(*self.args)

    def arrived(self):
        weights_arrived(*self.args)

    def sent(self):
        weights_sent(*self.args)


def project(g, w, bias, qkv):
    def consume(slot):
        qkv[slot] = (dot(g[slot], columns(w, 0, 384)) + bias[...]).astype(BF16)

    return consume


def enter_kernel(x, shard, gain, shift, qbias, qkv, normed, w, *sems):
    me = Place()
    greet(me, True)
    weights = Weights(me, shard, w, *sems[2:4])
    weights.start()
    normed[me.slot] = layer_norm(x[...].astype(F32), gain[...], shift[...]).astype(BF16)
    gather = Gather(me, normed, *sems[0:2])
    gather.start()
    gather.relay()
    weights.arrived()
    gather.run(project(normed, w, qbias, qkv), relayed=True)
    gather.end()
    weights.sent()


def forward_rest(
    me, attended, state, w, up, down, later, gain, shift, bias_out, up_bias, middle, normed, hidden, act, sum1, sum2, gather
):
    def out_product(slot):
        return dot(attended[slot], columns(w, 384, 128), NT)

    branch = sum_rows(me, out_product, sum1)
    middle[...] = state[...].astype(F32) + (branch + bias_out[...])
    normed[me.slot] = layer_norm(middle[...], gain[...], shift[...]).astype(BF16)
    gather = Gather(me, normed, *gather)
    gather.start()
    down.start()
    up.arrived()
    up_full = up.args[2]
    down_full = down.args[2]

    def consume(slot):
        h = dot(normed[slot], columns(up_full, 0, 512)) + up_bias[...]
        hidden[slot] = h
        act[slot] = (h * normal_below(h)).astype(BF16)

    gather.run(consume)
    down.arrived()
    if later is not None:
        later.start()

    def down_product(slot):
        return dot(act[slot], columns(down_full, 0, 512), NT)

    total = sum_rows(me, down_product, sum2)
    gather.end()
    up.sent()
    down.sent()
    return middle[...] + total


def between_kernel(
    attended, state, w, up_shard, down_shard, shard, gain, shift, bias_out, up_bias, bias_down, gain_next, shift_next, qbias,
    middle, normed_two, hidden, act, new_state, normed_next, qkv, up_full, down_full, w_next, *scratch,
):
    sum1, sum2, sems = scratch[0:NSUM], scratch[NSUM : 2 * NSUM], scratch[2 * NSUM :]
    me = Place()
    greet(me, True)
    up = Weights(me, up_shard, up_full, *sems[4:6])
    down = Weights(me, down_shard, down_full, *sems[6:8])
    later = Weights(me, shard, w_next, *sems[8:10])
    up.start()
    new_state[...] = (
        forward_rest(
            me, attended, state, w, up, down, later, gain, shift, bias_out, up_bias, middle, normed_two, hidden, act, sum1,
            sum2, sems[0:2],
        )
        + bias_down[...]
    )
    normed_next[me.slot] = layer_norm(new_state[...], gain_next[...], shift_next[...]).astype(BF16)
    gather = Gather(me, normed_next, *sems[2:4])
    gather.start()
    later.arrived()
    gather.run(project(normed_next, w_next, qbias, qkv))
    gather.end()
    later.sent()


def backward_rest(
    me, g_own, g_rows, w, up_full, down_full, hidden, act, normed, middle, gain, grad_hid, dwd, dwu, after_down, after_up,
    grad_mid, g_attn, grad_att, wide, row, up_sum, gather1, sums, gather2,
):
    def consume(slot):
        grad_act = dot(g_rows[slot], columns(down_full, 0, 512))
        grad_hid[slot] = (grad_act * gelu_slope(hidden[slot])).astype(BF16)

    gather1.run(consume)

    def up_back(slot):
        return dot(grad_hid[slot], columns(up_full, 0, 512), NT)

    def fill():
        weight_grad(g_rows, act, dwd, 0, 512)
        after_down()
        up_sum[...] = column_sum(grad_hid)

    grad = sum_rows(me, up_back, sums, fill)
    gather1.end()
    back, gain_sum, shift_sum = layer_norm_back(middle[...], gain[...], grad)
    mid = g_own[...].astype(F32) + back
    grad_mid[...] = mid
    g_attn[me.slot] = mid.astype(BF16)
    gather2.start()
    wide[row : row + 1] = jnp.sum(g_own[...].astype(F32), axis=0, keepdims=True)
    wide[row + 1 : row + 2] = gain_sum
    wide[row + 2 : row + 3] = shift_sum
    wide[row + 3 : row + 4] = jnp.sum(mid, axis=0, keepdims=True)

    def fill_two():
        weight_grad(normed, grad_hid, dwu, 0, 512)
        after_up()

    def att_back(slot):
        grad_att[slot] = dot(g_attn[slot], columns(w, 384, 128)).astype(BF16)

    gather2.run(att_back, fill_two)
    gather2.end()


def nothing():
    pass


class Grads:
    def __init__(self, me, part, land, send, recv):
        self.args = (me, part, land, send, recv)

    def start(self):
        grads_start(*self.args)

    def end(self, out):
        grads_end(*self.args, out)


def turn_kernel(
    attended, state, w, up_shard, down_shard, cot, gain, shift, bias_out, up_bias, bias_down,
    out_rows, sumd, dwu, grad_mid, g_attn, grad_att, wide, up_sum, *scratch,
):
    sum1, sum2, sum3 = (scratch[i * NSUM : (i + 1) * NSUM] for i in range(3))
    sems = scratch[3 * NSUM : 3 * NSUM + 12]
    middle, normed, hidden, act, g_rows, grad_hid, up_full, down_full, dwd, land = scratch[3 * NSUM + 12 :]
    me = Place()
    greet(me, True)
    up = Weights(me, up_shard, up_full, *sems[6:8])
    down = Weights(me, down_shard, down_full, *sems[8:10])
    grads = Grads(me, dwd, land, *sems[10:12])
    up.start()
    g_rows[me.slot] = cot[...]
    gather2 = Gather(me, g_rows, *sems[2:4])
    gather2.start()
    total = forward_rest(
        me, attended, state, w, up, down, None, gain, shift, bias_out, up_bias, middle, normed, hidden, act, sum1, sum2,
        sems[0:2],
    )
    out_rows[...] = (total + bias_down[...]).astype(BF16)
    wide[...] = jnp.zeros_like(wide)
    backward_rest(
        me, cot, g_rows, w, up_full, down_full, hidden, act, normed, middle, gain, grad_hid, dwd, dwu, grads.start, nothing,
        grad_mid, g_attn, grad_att, wide, 0, up_sum, gather2, sum3, Gather(me, g_attn, *sems[4:6]),
    )
    grads.end(sumd)


def first_back(me, grad_qkv, normed_one, w, g_attn, attended, state, grad_mid, gain, dwb, wide, row, q_sum, sums, more):
    def back_product(slot):
        return dot(grad_qkv[slot], columns(w, 0, 384), NT)

    def fill():
        weight_grad(normed_one, grad_qkv, dwb, 0, 384)
        weight_grad(g_attn, attended, dwb, 384, 128)
        more()
        q_sum[...] = column_sum(grad_qkv)

    grad = sum_rows(me, back_product, sums, fill)
    back, gain_sum, shift_sum = layer_norm_back(state[...].astype(F32), gain[...], grad)
    wide[row : row + 1] = gain_sum
    wide[row + 1 : row + 2] = shift_sum
    return grad_mid[...] + back


def back_kernel(
    grad_qkv, normed_one, w, g_attn_one, attended_one, state, grad_mid_one, gain_one, dwu_one,
    w_low, up_full, down_full, hidden, act, normed_two, middle, gain_two,
    sumu_one, sumb_one, sumd, sumu, grad_mid, g_attn, grad_att, wide, up_sum, q_sum, *scratch,
):
    sum1, sum2 = scratch[0:NSUM], scratch[NSUM : 2 * NSUM]
    sems = scratch[2 * NSUM : 2 * NSUM + 12]
    landu_one, landb_one, landd, landu, dwb, dwd, dwu, gradient, g_rows, grad_hid = scratch[2 * NSUM + 12 :]
    me = Place()
    greet(me, True)
    grads_u_one = Grads(me, dwu_one, landu_one, *sems[4:6])
    grads_b_one = Grads(me, dwb, landb_one, *sems[6:8])
    grads_d = Grads(me, dwd, landd, *sems[8:10])
    grads_u = Grads(me, dwu, landu, *sems[10:12])
    grads_u_one.start()
    wide[...] = jnp.zeros_like(wide)
    gradient[...] = first_back(
        me, grad_qkv, normed_one, w, g_attn_one, attended_one, state, grad_mid_one, gain_one, dwb, wide, 0, q_sum,
        sum1, grads_b_one.start,
    )
    g_rows[me.slot] = gradient[...].astype(BF16)
    gather1 = Gather(me, g_rows, *sems[0:2])
    gather1.start()
    backward_rest(
        me, gradient, g_rows, w_low, up_full, down_full, hidden, act, normed_two, middle, gain_two, grad_hid, dwd, dwu,
        grads_d.start, grads_u.start, grad_mid, g_attn, grad_att, wide, 2, up_sum, gather1, sum2,
        Gather(me, g_attn, *sems[2:4]),
    )
    grads_u_one.end(sumu_one)
    grads_b_one.end(sumb_one)
    grads_d.end(sumd)
    grads_u.end(sumu)


def vectors_start(me, wide, va, vl, send, recv):
    for s in range(MEMBERS):
        va[s] = wide[:, s * 128 : (s + 1) * 128]

    def step(i, carry):
        core, x = (me.core + i // 4) % 2, (me.x + i) % 4
        remote(va.at[core * 4 + x], vl.at[i], send.at[i], recv.at[i], me.peer(core, x)).start()
        return carry

    lax.fori_loop(1, MEMBERS, step, 0)


def vectors_end(me, narrow, va, vl, send, recv, vb, piece, send2, recv2, out, send3, recv3):
    total = va[me.slot]
    for i in range(1, MEMBERS):
        remote(va.at[0], vl.at[i], send.at[i], recv.at[i], me.sibling()).wait()
        total = total + vl[i]
    piece[0:16] = total
    piece[16:32] = narrow[...]

    def to_group(i):
        pair, zlo = (me.pair + i // 2) % 8, (me.zlo + i) % 2
        device = {"dp": pair * 2 + me.core, "tensor": zlo * 4 + me.x}
        return remote(piece, vb.at[me.group], send2.at[i], recv2.at[me.group], device)

    def start(i, carry):
        to_group(i).start()
        return carry

    lax.fori_loop(1, 16, start, 0)
    vb[me.group] = piece[...]

    def end(i, carry):
        to_group(i).wait_send()
        group = (me.group + i) % 16
        remote(piece, vb.at[group], send2.at[i], recv2.at[group], me.sibling()).wait_recv()
        return carry

    lax.fori_loop(1, 16, end, 0)
    total = vb[0]
    for i in range(1, 16):
        total = total + vb[i]
    out[me.slot] = total
    own = out.at[me.slot]

    def to_member(i):
        core, x = (me.core + i // 4) % 2, (me.x + i) % 4
        return remote(own, own, send3.at[i], recv3.at[me.slot], me.peer(core, x))

    def start_three(i, carry):
        to_member(i).start()
        return carry

    lax.fori_loop(1, MEMBERS, start_three, 0)

    def end_three(i, carry):
        to_member(i).wait_send()
        slot = ((me.core + i // 4) % 2) * 4 + (me.x + i) % 4
        remote(own, out.at[slot], send3.at[i], recv3.at[slot], me.sibling()).wait_recv()
        return carry

    lax.fori_loop(1, MEMBERS, end_three, 0)


def exit_kernel(
    grad_qkv, normed_one, w, g_attn, attended, state, grad_mid, gain, wide_in, narrow_in,
    gradient, sumb, vectors, *scratch,
):
    sum1, scratch = scratch[0:NSUM], scratch[NSUM:]
    landb, dwb, wide, q_sum, narrow, va, vl, vb, piece = scratch[0:9]
    pb, v1, v2, v3 = scratch[9:11], scratch[11:13], scratch[13:15], scratch[15:17]
    me = Place()
    greet(me, True)
    grads = Grads(me, dwb, landb, *pb)
    wide[...] = wide_in[...]
    gradient[...] = first_back(
        me, grad_qkv, normed_one, w, g_attn, attended, state, grad_mid, gain, dwb, wide, 0, q_sum, sum1, grads.start
    )
    narrow[...] = narrow_in[...]
    narrow[0:1] = q_sum[:, 0:128]
    narrow[1:2] = q_sum[:, 256:384]
    vectors_start(me, wide, va, vl, *v1)
    vectors_end(me, narrow, va, vl, *v1, vb, piece, *v2, vectors, *v3)
    grads.end(sumb)


def key_mask(shape, dim, length):
    at = lax.broadcasted_iota(jnp.int32, shape, dim)
    block = (at >= PAD).astype(jnp.int32) + (at >= 2 * PAD).astype(jnp.int32) + (at >= 3 * PAD).astype(jnp.int32)
    row = at - block * PAD
    return (row < ROWS) & (row + block * ROWS < length)


def head_parts(qkv, at):
    return qkv[:, :, at * COLS : (at + 1) * COLS].reshape(4 * PAD, COLS)


def attend_kernel(length, qkv, out):
    q, k, v = (head_parts(qkv, i) for i in range(3))
    valid = key_mask((1, 4 * PAD), 1, length[pl.program_id(0)])
    lane = lax.broadcasted_iota(jnp.int32, (1, COLS), 1)
    total = None
    for h in range(2):
        mine = (lane >= h * HEAD) & (lane < (h + 1) * HEAD)
        scores = dot(jnp.where(mine, q, jnp.zeros_like(q)), k, NT) * F32(HEAD**-0.5)
        scores = jnp.where(valid, scores, NEG_FILL)
        e = jnp.exp(scores - jnp.max(scores, axis=-1, keepdims=True))
        prob = (e * (1.0 / jnp.sum(e, axis=-1, keepdims=True))).astype(BF16)
        mixed = dot(prob, v)
        total = mixed if total is None else jnp.where(mine, mixed, total)
    out[...] = total.astype(BF16).reshape(4, PAD, COLS)


def attend_back_kernel(length, qkv, grad, out):
    q, k, v = (head_parts(qkv, i) for i in range(3))
    g = grad[...].reshape(4 * PAD, COLS)
    valid = key_mask((4 * PAD, 1), 0, length[pl.program_id(0)])
    lane = lax.broadcasted_iota(jnp.int32, (1, COLS), 1)
    parts = [None, None, None]
    for h in range(2):
        mine = (lane >= h * HEAD) & (lane < (h + 1) * HEAD)
        scores = dot(k, jnp.where(mine, q, jnp.zeros_like(q)), NT) * F32(HEAD**-0.5)
        scores = jnp.where(valid, scores, NEG_FILL)
        e = jnp.exp(scores - jnp.max(scores, axis=0, keepdims=True))
        prob = e * (1.0 / jnp.sum(e, axis=0, keepdims=True))
        grad_value = dot(prob.astype(BF16), g)
        grad_prob = dot(v, jnp.where(mine, g, jnp.zeros_like(g)), NT)
        inner = jnp.sum(grad_prob * prob, axis=0, keepdims=True)
        grad_scores = (prob * (grad_prob - inner)).astype(BF16)
        grad_key = dot(grad_scores, q) * F32(HEAD**-0.5)
        grad_query = dot(grad_scores, k, TN) * F32(HEAD**-0.5)
        new = [grad_query, grad_key, grad_value]
        parts = new if h == 0 else [jnp.where(mine, n, p) for n, p in zip(new, parts)]
    for i in range(3):
        out[:, :, i * COLS : (i + 1) * COLS] = parts[i].astype(BF16).reshape(4, PAD, COLS)


def attention(kernel, length, arrays, width):
    def spec(w):
        return pl.BlockSpec((4, PAD, w), lambda i: (i, 0, 0))

    return pl.pallas_call(
        kernel,
        grid=(2,),
        out_shape=jax.ShapeDtypeStruct((MEMBERS, PAD, width), BF16),
        in_specs=[pl.BlockSpec(memory_space=pltpu.SMEM)] + [spec(a.shape[2]) for a in arrays],
        out_specs=spec(width),
        compiler_params=pltpu.CompilerParams(vmem_limit_bytes=VMEM_BYTES),
    )(length, *arrays)


def swap(value):
    pairs = []
    for pair in range(8):
        for a in range(2):
            for b in range(2):
                for x in range(4):
                    pairs.append(((pair * 2 + a) * 8 + b * 4 + x, (pair * 2 + b) * 8 + a * 4 + x))
    return lax.ppermute(value, ("dp", "tensor"), pairs)


def per_device(
    x_in, valid_len, w_qkv, w_out, w_up, w_down, norm_gain, norm_shift, bias, up_bias, cotangent
):
    dp, tensor = lax.axis_index("dp"), lax.axis_index("tensor")
    slot = (dp % 2) * 4 + tensor % 4

    def padded(rows):
        return jnp.pad(rows, ((0, PAD - ROWS), (0, 0)))

    x = padded(swap(x_in))
    cot = padded(swap(cotangent))
    length = swap(valid_len)
    qo_shards = jnp.concatenate([w_qkv.reshape(2, 64, 384), jnp.swapaxes(w_out, 1, 2)], axis=2)
    down_shards = jnp.swapaxes(w_down, 1, 2)
    gain = [[norm_gain[l, i][None] for i in range(2)] for l in range(2)]
    shift = [[norm_shift[l, i][None] for i in range(2)] for l in range(2)]
    bias_rows = [[bias[l, i][None] for i in range(4)] for l in range(2)]
    own_bias = lax.dynamic_slice_in_dim(bias, slot * COLS, COLS, axis=2)
    own_up = lax.dynamic_slice_in_dim(up_bias, slot * HID, HID, axis=1)
    qbias = [
        jnp.concatenate([own_bias[l, 0], jnp.zeros((COLS,), F32), own_bias[l, 1]])[None] for l in range(2)
    ]
    ubias = [own_up[l][None] for l in range(2)]

    rows_all, rows_own, part = (MEMBERS, PAD, D), (PAD, D), (16, 64, 512)
    hid, att, summed = (MEMBERS, PAD, HID), (MEMBERS, PAD, COLS), (64, 512)
    qkv0, normed0, w0 = call(
        enter_kernel,
        [((MEMBERS, PAD, 384), BF16), (rows_all, BF16), (part, BF16)],
        GATHER_SEMS + PLANE_SEMS,
        0,
        [x, qo_shards[0], gain[0][0], shift[0][0], qbias[0]],
        1 << 30,
    )
    attended0 = attention(attend_kernel, length, [qkv0], COLS)
    middle0, normed_two0, hidden0, act0, state1, normed1, qkv1, wup0, wdown0, w1 = call(
        between_kernel,
        [
            (rows_own, F32),
            (rows_all, BF16),
            (hid, F32),
            (hid, BF16),
            (rows_own, F32),
            (rows_all, BF16),
            ((MEMBERS, PAD, 384), BF16),
            (part, BF16),
            (part, BF16),
            (part, BF16),
        ],
        SUM_SCRATCH * 2 + GATHER_SEMS * 2 + PLANE_SEMS * 3,
        1,
        [
            attended0, x, w0, w_up[0], down_shards[0], qo_shards[1], gain[0][1], shift[0][1], bias_rows[0][2], ubias[0],
            bias_rows[0][3], gain[1][0], shift[1][0], qbias[1],
        ],
        4 << 30,
    )
    attended1 = attention(attend_kernel, length, [qkv1], COLS)
    out_rows, sumd1, dwu1, grad_mid1, g_attn1, grad_att1, wide1, up1 = call(
        turn_kernel,
        [
            (rows_own, BF16),
            (summed, F32),
            (part, BF16),
            (rows_own, F32),
            (rows_all, BF16),
            (att, BF16),
            ((8, D), F32),
            ((1, HID), F32),
        ],
        SUM_SCRATCH * 3
        + GATHER_SEMS * 3
        + PLANE_SEMS * 3
        + [pltpu.VMEM(rows_own, F32), pltpu.VMEM(rows_all, BF16), pltpu.VMEM(hid, F32), pltpu.VMEM(hid, BF16)]
        + [pltpu.VMEM(rows_all, BF16), pltpu.VMEM(hid, BF16)]
        + [pltpu.VMEM(part, BF16)] * 4,
        2,
        [
            attended1, state1, w1, w_up[1], down_shards[1], cot, gain[1][1], shift[1][1], bias_rows[1][2], ubias[1],
            bias_rows[1][3],
        ],
        8 << 30,
    )
    out_rows = swap(out_rows[:ROWS])
    grad_qkv1 = attention(attend_back_kernel, length, [qkv1, grad_att1], 384)
    sumu1, sumb1, sumd0, sumu0, grad_mid0, g_attn0, grad_att0, wide0, up0, q1 = call(
        back_kernel,
        [
            (summed, F32),
            (summed, F32),
            (summed, F32),
            (summed, F32),
            (rows_own, F32),
            (rows_all, BF16),
            (att, BF16),
            ((8, D), F32),
            ((1, HID), F32),
            ((1, 384), F32),
        ],
        SUM_SCRATCH * 2
        + GATHER_SEMS * 2
        + PLANE_SEMS * 4
        + [pltpu.VMEM(part, BF16)] * 7
        + [pltpu.VMEM(rows_own, F32), pltpu.VMEM(rows_all, BF16), pltpu.VMEM(hid, BF16)],
        3,
        [
            grad_qkv1, normed1, w1, g_attn1, attended1, state1, grad_mid1, gain[1][0], dwu1,
            w0, wup0, wdown0, hidden0, act0, normed_two0, middle0, gain[0][1],
        ],
        8 << 30,
    )
    grad_qkv0 = attention(attend_back_kernel, length, [qkv0, grad_att0], 384)
    wide = jnp.concatenate(
        [jnp.zeros((2, D), F32), wide0[2:6], wide0[0:2], wide1[0:4], jnp.zeros((4, D), F32)], axis=0
    )
    narrow = jnp.concatenate(
        [
            jnp.zeros((2, COLS), F32),
            up0.reshape(4, COLS),
            q1[:, 0:COLS],
            q1[:, 2 * COLS :],
            up1.reshape(4, COLS),
            jnp.zeros((4, COLS), F32),
        ],
        axis=0,
    )
    gradient, sumb0, vectors = call(
        exit_kernel,
        [(rows_own, F32), (summed, F32), ((MEMBERS, 32, 128), F32)],
        SUM_SCRATCH
        + [
            pltpu.VMEM(part, BF16),
            pltpu.VMEM(part, BF16),
            pltpu.VMEM((16, D), F32),
            pltpu.VMEM((1, 384), F32),
            pltpu.VMEM((16, 128), F32),
            pltpu.VMEM((MEMBERS, 16, 128), F32),
            pltpu.VMEM((MEMBERS, 16, 128), F32),
            pltpu.VMEM((16, 32, 128), F32),
            pltpu.VMEM((32, 128), F32),
        ]
        + PLANE_SEMS
        + [pltpu.SemaphoreType.DMA((8,))] * 2
        + PLANE_SEMS
        + [pltpu.SemaphoreType.DMA((8,))] * 2,
        4,
        [grad_qkv0, normed0, w0, g_attn0, attended0, x, grad_mid0, gain[0][0], wide, narrow],
        4 << 30,
    )
    sumb = jnp.stack([sumb0, sumb1])
    full = jnp.transpose(vectors[:, 0:12], (1, 0, 2)).reshape(2, 6, D)
    own = vectors[:, 16:28].reshape(MEMBERS, 2, 6, COLS)
    q_bias = jnp.transpose(own[:, :, 0], (1, 0, 2)).reshape(2, D)
    v_bias = jnp.transpose(own[:, :, 1], (1, 0, 2)).reshape(2, D)
    return (
        out_rows,
        swap(gradient[:ROWS]),
        sumb[:, :, 0:384].reshape(2, 64, 3, COLS),
        jnp.swapaxes(sumb[:, :, 384:], 1, 2),
        jnp.stack([sumu0, sumu1]),
        jnp.swapaxes(jnp.stack([sumd0, sumd1]), 1, 2),
        jnp.stack([full[:, 0], full[:, 3]], axis=1),
        jnp.stack([full[:, 1], full[:, 4]], axis=1),
        jnp.stack([q_bias, v_bias, full[:, 5], full[:, 2]], axis=1),
        jnp.transpose(own[:, :, 2:], (1, 0, 2, 3)).reshape(2, 4096),
    )


def solution(mesh):
    rows = P(("dp", "tensor"), None)
    weights = (P(None, "dp", None, "tensor"), P(None, "tensor", "dp"), P(None, "dp", "tensor"), P(None, "tensor", "dp"))
    return jax.shard_map(
        per_device,
        mesh=mesh,
        in_specs=(rows, P("dp"), *weights, P(), P(), P(), P(), rows),
        out_specs=(rows, rows, *weights, P(), P(), P(), P()),
        check_vma=False,
    )
```

```python
import types

import jax
import jax.numpy as jnp
from jax import lax
from jax.experimental import pallas as pl
from jax.experimental.pallas import tpu as pltpu
from jax.sharding import PartitionSpec as P

MESH = pl.DeviceIdType.MESH
F32, BF16 = jnp.float32, jnp.bfloat16

D = 1024
ROWS = 146
PAD = 160
COLS = 128
HEAD = 64
HID = 512
MEMBERS = 8
WCOLS = 1536
EPSILON = 1e-06
NEG_FILL = -1e30
VMEM_BYTES = 64 * 1024 * 1024 - 65536

NN = (((1,), (0,)), ((), ()))
NT = (((1,), (1,)), ((), ()))
TN = (((0,), (0,)), ((), ()))


def dot(a, b, dims=NN):
    return lax.dot_general(a, b, dims, preferred_element_type=F32)


class Place:
    def __init__(self):
        self.dp = lax.axis_index("dp")
        self.tensor = lax.axis_index("tensor")
        self.core = self.dp % 2
        self.pair = self.dp // 2
        self.zlo = self.tensor // 4
        self.x = self.tensor % 4
        self.slot = self.core * 4 + self.x
        self.group = self.pair * 2 + self.zlo

    def peer(self, core, x):
        return {"dp": self.pair * 2 + core, "tensor": self.zlo * 4 + x}

    def sibling(self):
        return self.peer(1 - self.core, self.x)


def greet(me, plane):
    barrier = pltpu.get_barrier_semaphore()

    def member(i, carry):
        pl.semaphore_signal(
            barrier,
            inc=1,
            device_id=me.peer((me.core + i // 4) % 2, (me.x + i) % 4),
            device_id_type=MESH,
        )
        return carry

    lax.fori_loop(1, MEMBERS, member, 0)
    count = MEMBERS - 1
    if plane:

        def other(i, carry):
            pair = (me.pair + i // 4) % 8
            zlo = (me.zlo + (i // 2) % 2) % 2
            pl.semaphore_signal(
                barrier,
                inc=1,
                device_id={"dp": pair * 2 + i % 2, "tensor": zlo * 4 + me.x},
                device_id_type=MESH,
            )
            return carry

        lax.fori_loop(2, 32, other, 0)
        count += 30
    pl.semaphore_wait(barrier, count)


def remote(src, dst, send, recv, device):
    return pltpu.make_async_remote_copy(
        src_ref=src,
        dst_ref=dst,
        send_sem=send,
        recv_sem=recv,
        device_id=device,
        device_id_type=MESH,
    )


def slot_at(me, i):
    sibling = (i == 1) | (i == 4) | (i == 5) | (i == 7)
    far = (i >= 6).astype(jnp.int32) * 2
    left = ((i == 2) | (i == 4)).astype(jnp.int32) * 3
    right = ((i == 3) | (i == 5)).astype(jnp.int32)
    core = (me.core + sibling.astype(jnp.int32)) % 2
    return core * 4 + (me.x + far + left + right) % 4


HALF = PAD // 2
TOP, BOTTOM = pl.ds(0, HALF), pl.ds(HALF, HALF)


class Gather:
    def __init__(self, me, g, send, recv):
        self.me, self.g, self.send, self.recv = me, g, send, recv
        self.right = me.peer(me.core, (me.x + 1) % 4)
        self.left = me.peer(me.core, (me.x + 3) % 4)
        self.from_left = me.core * 4 + (me.x + 3) % 4
        self.from_right = me.core * 4 + (me.x + 1) % 4
        self.from_far = me.core * 4 + (me.x + 2) % 4

    def copy(self, k, slot, rows, device):
        block = self.g.at[slot] if rows is None else self.g.at[slot, rows]
        return remote(block, block, self.send.at[k], self.recv.at[k], device)

    def table(self):
        me = self.me
        sibling = me.sibling()
        return [
            (0, me.slot, TOP, self.right),
            (1, me.slot, BOTTOM, self.right),
            (2, me.slot, TOP, self.left),
            (3, me.slot, BOTTOM, self.left),
            (4, self.from_left, TOP, self.right),
            (5, self.from_right, BOTTOM, self.left),
            (6, me.slot, None, sibling),
            (7, self.from_left, None, sibling),
            (8, self.from_right, None, sibling),
            (9, self.from_far, None, sibling),
        ]

    def start_copies(self, *which):
        for k in which:
            self.copy(*self.table()[k]).start()

    def start(self):
        self.start_copies(6, 0, 3, 1, 2)

    def arrived(self, *which):
        for k in which:
            _, slot, rows, device = self.table()[k]
            self.copy(k, slot, rows, device).wait_recv()

    def relay(self):
        self.arrived(0)
        self.start_copies(4)
        self.arrived(3)
        self.start_copies(5)

    def run(self, consume, fill=None, relayed=False):
        def step(i, carry):
            @pl.when(i == 1)
            def _():
                self.arrived(6)

            @pl.when(i == 2)
            def _():
                if not relayed:
                    self.relay()
                if fill is not None:
                    fill()
                self.arrived(1)
                self.start_copies(7)

            @pl.when(i == 3)
            def _():
                self.arrived(2)
                self.start_copies(8)

            @pl.when(i == 4)
            def _():
                self.arrived(7)

            @pl.when(i == 5)
            def _():
                self.arrived(8)

            @pl.when(i == 6)
            def _():
                self.arrived(4, 5)
                self.start_copies(9)

            @pl.when(i == 7)
            def _():
                self.arrived(9)

            consume(slot_at(self.me, i))
            return carry

        lax.fori_loop(0, MEMBERS, step, 0)

    def end(self):
        for row in self.table():
            self.copy(*row).wait_send()


GATHER_SEMS = [pltpu.SemaphoreType.DMA((10,)), pltpu.SemaphoreType.DMA((10,))]

SUM_SEND = [
    pltpu.VMEM((4, PAD, D), BF16),
    pltpu.VMEM((3, PAD, D), BF16),
    pltpu.VMEM((PAD, D), F32),
    pltpu.VMEM((2, HALF, D), F32),
]
SUM_LAND = [
    pltpu.VMEM((4, PAD, D), BF16),
    pltpu.VMEM((PAD, D), BF16),
    pltpu.VMEM((2, PAD, D), BF16),
    pltpu.SemaphoreType.DMA((4,)),
    pltpu.SemaphoreType.DMA((4,)),
    pltpu.SemaphoreType.DMA((6,)),
    pltpu.SemaphoreType.DMA((6,)),
]


def sum_rows(me, produce, send_bufs, land_bufs, fill=None):
    s1, s2, acc, hold = send_bufs
    r1, ra, rb, ss1, rs1, ss2, rs2 = land_bufs
    sibling = me.sibling()
    right, left = me.peer(me.core, (me.x + 1) % 4), me.peer(me.core, (me.x + 3) % 4)

    def chip(i):
        return (me.x + 2 + (i == 1).astype(jnp.int32) * 3 + (i == 2).astype(jnp.int32) + (i == 3).astype(jnp.int32) * 2) % 4

    def to_sibling(i):
        return remote(s1.at[i], r1.at[i], ss1.at[i], rs1.at[i], sibling)

    def along(k):
        src, dst, device = (
            (s2.at[0, TOP], ra.at[TOP], right),
            (s2.at[0, BOTTOM], ra.at[BOTTOM], left),
            (s2.at[1, BOTTOM], rb.at[0, BOTTOM], right),
            (s2.at[2, TOP], rb.at[1, TOP], left),
            (s2.at[1, TOP], rb.at[0, TOP], right),
            (s2.at[2, BOTTOM], rb.at[1, BOTTOM], left),
        )[k]
        return remote(src, dst, ss2.at[k], rs2.at[k], device)

    def for_sibling(i, carry):
        s1[i] = produce((1 - me.core) * 4 + chip(i)).astype(BF16)
        to_sibling(i).start()
        return carry

    def own(i, carry):
        part = produce(me.core * 4 + chip(i))
        to_sibling(i).wait_recv()
        acc[...] = part + r1[i].astype(F32)

        @pl.when(i == 0)
        def _():
            s2[0] = acc[...].astype(BF16)
            along(0).start()
            along(1).start()

        @pl.when(i == 1)
        def _():
            s2[1, BOTTOM] = acc[BOTTOM].astype(BF16)
            along(2).start()
            hold[0] = acc[TOP]

        @pl.when(i == 2)
        def _():
            s2[2, TOP] = acc[TOP].astype(BF16)
            along(3).start()
            hold[1] = acc[BOTTOM]

        @pl.when(i < 2)
        def _():
            for_sibling(i + 2, 0)

        return carry

    lax.fori_loop(0, 2, for_sibling, 0)
    lax.fori_loop(0, 4, own, 0)
    along(0).wait_recv()
    s2[1, TOP] = (hold[0] + ra[TOP].astype(F32)).astype(BF16)
    along(4).start()
    along(1).wait_recv()
    s2[2, BOTTOM] = (hold[1] + ra[BOTTOM].astype(F32)).astype(BF16)
    along(5).start()
    if fill is not None:
        fill()
    for k in range(2, 6):
        along(k).wait_recv()
    total = acc[...] + rb[0].astype(F32) + rb[1].astype(F32)
    for i in range(4):
        to_sibling(i).wait_send()
    for k in range(6):
        along(k).wait_send()
    return total


PLANE_SEMS = [pltpu.SemaphoreType.DMA((16,)), pltpu.SemaphoreType.DMA((16,))]


def weights_copy(me, i, shard, full, send, recv):
    pair, zlo = (me.pair + i // 2) % 8, (me.zlo + i) % 2
    device = {"dp": pair * 2 + me.zlo, "tensor": zlo * 4 + me.x}
    return remote(shard, full.at[me.dp], send.at[i], recv.at[me.dp], device)


def weights_start(me, shard, full, send, recv):
    def step(i, carry):
        weights_copy(me, i, shard, full, send, recv).start()
        return carry

    own = me.core == me.zlo

    @pl.when(own)
    def _():
        pltpu.make_async_copy(shard, full.at[me.dp], recv.at[me.dp]).start()

    @pl.when(jnp.logical_not(own))
    def _():
        weights_copy(me, 0, shard, full, send, recv).start()

    lax.fori_loop(1, 16, step, 0)


def weights_arrived(me, shard, full, send, recv):
    def step(i, carry):
        remote(shard, full.at[i], send.at[i], recv.at[i], me.sibling()).wait_recv()
        return carry

    lax.fori_loop(0, 16, step, 0)


def weights_sent(me, shard, full, send, recv):
    @pl.when(me.core != me.zlo)
    def _():
        weights_copy(me, 0, shard, full, send, recv).wait_send()

    def step(i, carry):
        weights_copy(me, i, shard, full, send, recv).wait_send()
        return carry

    lax.fori_loop(1, 16, step, 0)


def grads_copy(me, i, part, land, send, recv):
    to = (me.dp + i) % 16
    device = {"dp": to, "tensor": me.slot}
    return remote(part.at[to], land.at[me.group], send.at[i], recv.at[me.group], device)


def grads_start(me, part, land, send, recv):
    own = me.zlo == me.core

    @pl.when(own)
    def _():
        pltpu.make_async_copy(part.at[me.dp], land.at[me.group], recv.at[me.group]).start()

    @pl.when(jnp.logical_not(own))
    def _():
        grads_copy(me, 0, part, land, send, recv).start()

    def step(i, carry):
        grads_copy(me, i, part, land, send, recv).start()
        return carry

    lax.fori_loop(1, 16, step, 0)


def grads_end(me, part, land, send, recv, out):
    def arrived(i, carry):
        remote(part.at[0], land.at[i], send.at[i], recv.at[i], me.sibling()).wait_recv()
        return carry

    lax.fori_loop(0, 16, arrived, 0)

    @pl.when(me.zlo != me.core)
    def _():
        grads_copy(me, 0, part, land, send, recv).wait_send()

    def sent(i, carry):
        grads_copy(me, i, part, land, send, recv).wait_send()
        return carry

    lax.fori_loop(1, 16, sent, 0)
    total = land[0].astype(F32)
    for i in range(1, 16):
        total = total + land[i].astype(F32)
    out[...] = total


def normalized(rows):
    centred = rows - jnp.mean(rows, axis=-1, keepdims=True)
    scale = lax.rsqrt(jnp.mean(centred * centred, axis=-1, keepdims=True) + EPSILON)
    return centred * scale, scale


def layer_norm(rows, gain, shift):
    return normalized(rows)[0] * gain + shift


def layer_norm_back(rows, gain, grad):
    unit, scale = normalized(rows)
    inner = grad * gain
    mean_one = jnp.mean(inner, axis=-1, keepdims=True)
    mean_two = jnp.mean(inner * unit, axis=-1, keepdims=True)
    back = scale * (inner - mean_one - unit * mean_two)
    return back, jnp.sum(grad * unit, axis=0, keepdims=True), jnp.sum(grad, axis=0, keepdims=True)


def erf(v):
    v = jnp.clip(v, -4.0, 4.0)
    s = v * v
    top = F32(-2.72614225801306e-10)
    for a in (
        2.77068142495902e-08,
        -2.10102402082508e-06,
        -5.69250639462346e-05,
        -7.34990630326855e-04,
        -2.95459980854025e-03,
        -1.60960333262415e-02,
    ):
        top = top * s + F32(a)
    low = F32(-1.45660718464996e-05)
    for b in (
        -2.13374055278905e-04,
        -1.68282697438203e-03,
        -7.37332916720468e-03,
        -1.42647390514189e-02,
    ):
        low = low * s + F32(b)
    return v * top / low


def normal_below(v):
    return 0.5 * (1.0 + erf(v * F32(0.7071067811865476)))


def gelu_and_slope(v):
    below = normal_below(v)
    return v * below, below + v * jnp.exp(-0.5 * v * v) * F32(0.3989422804014327)


def weight_grad(left, right, out, at, width):
    def tile(i, carry):
        a = left[:, :, pl.ds(pl.multiple_of(i * 256, 256), 256)].reshape(MEMBERS * PAD, 256)
        b = right[...].reshape(MEMBERS * PAD, width)
        block = dot(a, b, TN).astype(BF16).reshape(4, 64, width)
        out[pl.ds(i * 4, 4), :, at : at + width] = block
        return carry

    lax.fori_loop(0, D // 256, tile, 0)


def columns(w, at, width):
    return w[:, :, at : at + width].reshape(D, width)


def column_sum(ref):
    def step(i, total):
        return total + jnp.sum(ref[i].astype(F32), axis=0, keepdims=True)

    return lax.fori_loop(0, MEMBERS, step, jnp.zeros((1, ref.shape[2]), F32))


def head_parts(qkv, i, at):
    return qkv[pl.ds(i * 4, 4), :, at * COLS : (at + 1) * COLS].reshape(4 * PAD, COLS)


def attend(qkv, mask, out):
    lane = lax.broadcasted_iota(jnp.int32, (1, COLS), 1)

    def image(i, carry):
        q, k, v = (head_parts(qkv, i, j) for j in range(3))
        valid = mask[i, 0:1] > 0.5
        total = None
        for h in range(2):
            mine = (lane >= h * HEAD) & (lane < (h + 1) * HEAD)
            scores = dot(jnp.where(mine, q, jnp.zeros_like(q)), k, NT) * F32(HEAD**-0.5)
            scores = jnp.where(valid, scores, NEG_FILL)
            e = jnp.exp(scores - jnp.max(scores, axis=-1, keepdims=True))
            prob = (e * (1.0 / jnp.sum(e, axis=-1, keepdims=True))).astype(BF16)
            mixed = dot(prob, v)
            total = mixed if total is None else jnp.where(mine, mixed, total)
        out[pl.ds(i * 4, 4)] = total.astype(BF16).reshape(4, PAD, COLS)
        return carry

    lax.fori_loop(0, 2, image, 0)


def attend_back(qkv, mask, grad):
    lane = lax.broadcasted_iota(jnp.int32, (1, COLS), 1)

    def image(i, carry):
        q, k, v = (head_parts(qkv, i, j) for j in range(3))
        g = grad[pl.ds(i * 4, 4)].reshape(4 * PAD, COLS)
        valid = mask[i].T[:, 0:1] > 0.5
        parts = [None, None, None]
        for h in range(2):
            mine = (lane >= h * HEAD) & (lane < (h + 1) * HEAD)
            scores = dot(k, jnp.where(mine, q, jnp.zeros_like(q)), NT) * F32(HEAD**-0.5)
            scores = jnp.where(valid, scores, NEG_FILL)
            e = jnp.exp(scores - jnp.max(scores, axis=0, keepdims=True))
            prob = e * (1.0 / jnp.sum(e, axis=0, keepdims=True))
            grad_value = dot(prob.astype(BF16), g)
            grad_prob = dot(v, jnp.where(mine, g, jnp.zeros_like(g)), NT)
            inner = jnp.sum(grad_prob * prob, axis=0, keepdims=True)
            grad_scores = (prob * (grad_prob - inner)).astype(BF16)
            grad_key = dot(grad_scores, q) * F32(HEAD**-0.5)
            grad_query = dot(grad_scores, k, TN) * F32(HEAD**-0.5)
            new = [grad_query, grad_key, grad_value]
            parts = new if h == 0 else [jnp.where(mine, n, p) for n, p in zip(new, parts)]
        for j in range(3):
            qkv[pl.ds(i * 4, 4), :, j * COLS : (j + 1) * COLS] = parts[j].astype(BF16).reshape(4, PAD, COLS)
        return carry

    lax.fori_loop(0, 2, image, 0)


def vectors_start(me, wide, va, vl, send, recv):
    for s in range(MEMBERS):
        va[s] = wide[:, s * 128 : (s + 1) * 128]

    def step(i, carry):
        core, x = (me.core + i // 4) % 2, (me.x + i) % 4
        remote(va.at[core * 4 + x], vl.at[i], send.at[i], recv.at[i], me.peer(core, x)).start()
        return carry

    lax.fori_loop(1, MEMBERS, step, 0)


def vectors_end(me, narrow, va, vl, send, recv, vb, piece, send2, recv2, out, send3, recv3):
    total = va[me.slot]
    for i in range(1, MEMBERS):
        remote(va.at[0], vl.at[i], send.at[i], recv.at[i], me.sibling()).wait()
        total = total + vl[i]
    piece[0:16] = total
    piece[16:32] = narrow[...]

    def to_group(i):
        pair, zlo = (me.pair + i // 2) % 8, (me.zlo + i) % 2
        device = {"dp": pair * 2 + me.core, "tensor": zlo * 4 + me.x}
        return remote(piece, vb.at[me.group], send2.at[i], recv2.at[me.group], device)

    def start(i, carry):
        to_group(i).start()
        return carry

    lax.fori_loop(1, 16, start, 0)
    vb[me.group] = piece[...]

    def end(i, carry):
        to_group(i).wait_send()
        group = (me.group + i) % 16
        remote(piece, vb.at[group], send2.at[i], recv2.at[group], me.sibling()).wait_recv()
        return carry

    lax.fori_loop(1, 16, end, 0)
    total = vb[0]
    for i in range(1, 16):
        total = total + vb[i]
    out[me.slot] = total
    own = out.at[me.slot]

    def to_member(i):
        core, x = (me.core + i // 4) % 2, (me.x + i) % 4
        return remote(own, own, send3.at[i], recv3.at[me.slot], me.peer(core, x))

    def start_three(i, carry):
        to_member(i).start()
        return carry

    lax.fori_loop(1, MEMBERS, start_three, 0)

    def end_three(i, carry):
        to_member(i).wait_send()
        slot = ((me.core + i // 4) % 2) * 4 + (me.x + i) % 4
        remote(own, out.at[slot], send3.at[i], recv3.at[slot], me.sibling()).wait_recv()
        return carry

    lax.fori_loop(1, MEMBERS, end_three, 0)


class Weights:
    def __init__(self, me, shard, full, send, recv):
        self.args, self.full = (me, shard, full, send, recv), full

    def start(self):
        weights_start(*self.args)

    def arrived(self):
        weights_arrived(*self.args)

    def sent(self):
        weights_sent(*self.args)


class Grads:
    def __init__(self, me, part, land, send, recv, out):
        self.args, self.part = (me, part, land, send, recv, out), part

    def start(self):
        grads_start(*self.args[:5])

    def end(self):
        grads_end(*self.args)


class Swap:
    def __init__(self, me, src, dst, sems, k):
        self.away = me.core != me.zlo
        self.src, self.dst = src, dst
        partner = {"dp": me.pair * 2 + me.zlo, "tensor": me.core * 4 + me.x}
        self.copy = remote(src, dst, sems[0].at[k], sems[1].at[k], partner)

    def start(self):
        @pl.when(self.away)
        def _():
            self.copy.start()

    def end(self):
        @pl.when(self.away)
        def _():
            self.copy.wait()

        @pl.when(jnp.logical_not(self.away))
        def _():
            self.dst[...] = self.src[...]


ROWS_ALL, ROWS_OWN, PART = (MEMBERS, PAD, D), (PAD, D), (16, 64, 512)
HID_ALL, ATT_ALL, QKV_ALL, SUMMED = (MEMBERS, PAD, HID), (MEMBERS, PAD, COLS), (MEMBERS, PAD, 384), (64, 512)
DMA = pltpu.SemaphoreType.DMA

INPUTS = ("x_in", "cot_in", "mask_in", "shards", "gain", "shift", "bias", "qbias", "ubias")
OUTPUTS = {
    "out_rows": (ROWS_OWN, BF16),
    "gradient": (ROWS_OWN, F32),
    "sum_qo": ((2, *SUMMED), F32),
    "sum_up": ((2, *SUMMED), F32),
    "sum_down": ((2, *SUMMED), F32),
    "vectors": ((MEMBERS, 32, 128), F32),
}


def scratch_table():
    table = {"padded": pltpu.VMEM(ROWS_OWN, F32)}

    def add(name, shape, dtype, count=None):
        if count is None:
            table[name] = pltpu.VMEM(shape, dtype)
        for i in range(count or 0):
            table[f"{name}{i}"] = pltpu.VMEM(shape, dtype)

    for name in ("x_own", "x_rows", "cot_own", "cot_rows", "rows_away", "rows_home"):
        add(name, ROWS_OWN, BF16)
    add("mask", (2, 8, 4 * PAD), F32)
    for name in ("qo", "up", "down", "land_qo", "land_up", "land_down"):
        add(name, PART, BF16, 2)
    for name in ("dw_qo", "dw_up", "dw_down"):
        add(name, PART, BF16)
    add("normed_one", ROWS_ALL, BF16, 2)
    add("normed_two", ROWS_ALL, BF16, 2)
    add("qkv", QKV_ALL, BF16, 2)
    add("attended", ATT_ALL, BF16, 2)
    add("slope", HID_ALL, BF16, 2)
    add("act", HID_ALL, BF16, 2)
    add("middle", ROWS_OWN, F32, 2)
    add("state", ROWS_OWN, F32)
    add("g_rows", ROWS_ALL, BF16)
    add("g_attn", ROWS_ALL, BF16)
    add("grad_att", ATT_ALL, BF16)
    add("grad_mid", ROWS_OWN, F32)
    add("grad", ROWS_OWN, F32)
    add("wide", (16, D), F32)
    add("narrow", (16, 128), F32)
    add("va", (MEMBERS, 16, 128), F32)
    add("vl", (MEMBERS, 16, 128), F32)
    add("vb", (16, 32, 128), F32)
    add("piece", (32, 128), F32)
    for i, spec in enumerate(SUM_SEND):
        table[f"sum_send{i}"] = spec
    for j in range(2):
        for i, spec in enumerate(SUM_LAND):
            table[f"sum_land{j}_{i}"] = spec
    for name, count in (("rows", 10), ("cot", 10), ("swap", 5), ("v1", 8), ("v2", 16), ("v3", 8)):
        table[name + "_send"], table[name + "_recv"] = DMA((count,)), DMA((count,))
    for name in ("w", "g"):
        table[name + "_send"], table[name + "_recv"] = DMA((6, 16)), DMA((6, 16))
    return table


def whole_kernel(*refs):
    table = scratch_table()
    names = [*INPUTS, *OUTPUTS, *table]
    b = types.SimpleNamespace(**dict(zip(names, refs, strict=True)))
    me = Place()
    greet(me, True)

    def both(name):
        return getattr(b, name + "_send"), getattr(b, name + "_recv")

    def pair(name):
        return [getattr(b, name + "0"), getattr(b, name + "1")]

    cuts = {"qo": pl.ds(0, 512), "up": pl.ds(512, 512), "down": pl.ds(1024, 512)}
    weights, grads = {}, {}
    for n, name in enumerate(cuts):
        for l in range(2):
            k = n * 2 + l
            shard = b.shards.at[l, :, cuts[name]]
            weights[name, l] = Weights(me, shard, pair(name)[l], b.w_send.at[k], b.w_recv.at[k])
            part = getattr(b, "dw_" + name)
            out = getattr(b, "sum_" + name).at[l]
            grads[name, l] = Grads(me, part, pair("land_" + name)[l], b.g_send.at[k], b.g_recv.at[k], out)
    send_bufs = [getattr(b, f"sum_send{i}") for i in range(len(SUM_SEND))]
    land = [[getattr(b, f"sum_land{j}_{i}") for i in range(len(SUM_LAND))] for j in range(2)]
    normed_one, normed_two, qkv, attended = (pair(n) for n in ("normed_one", "normed_two", "qkv", "attended"))
    slope, act, middle = (pair(n) for n in ("slope", "act", "middle"))
    weights["qo", 0].start()

    def padded(rows, out):
        b.padded[0:ROWS] = rows[...].astype(F32)
        b.padded[ROWS:PAD] = jnp.zeros((PAD - ROWS, D), F32)
        out[...] = b.padded[...].astype(BF16)

    padded(b.x_in, b.x_own)
    swap_x = Swap(me, b.x_own, b.x_rows, both("swap"), 0)
    swap_x.start()
    swap_mask = Swap(me, b.mask_in, b.mask, both("swap"), 1)
    swap_mask.start()
    padded(b.cot_in, b.cot_own)
    swap_cot = Swap(me, b.cot_own, b.cot_rows, both("swap"), 2)
    swap_cot.start()
    b.wide[...] = jnp.zeros_like(b.wide)
    b.narrow[...] = jnp.zeros_like(b.narrow)
    swap_x.end()

    def norm_rows(rows, l, i, out):
        out[me.slot] = layer_norm(rows, b.gain[l, i : i + 1], b.shift[l, i : i + 1]).astype(BF16)

    def project(l):
        w = weights["qo", l].full

        def consume(slot):
            qkv[l][slot] = (dot(normed_one[l][slot], columns(w, 0, 384)) + b.qbias[l : l + 1]).astype(BF16)

        return consume

    def forward(l, state, before_up, before_down, after_up):
        attend(qkv[l], b.mask, attended[l])
        before_up()
        w = weights["qo", l].full

        def out_product(slot):
            return dot(attended[l][slot], columns(w, 384, 128), NT)

        branch = sum_rows(me, out_product, send_bufs, land[0])
        middle[l][...] = state() + (branch + b.bias[l, 2:3])
        norm_rows(middle[l][...], l, 1, normed_two[l])
        gather = Gather(me, normed_two[l], *both("rows"))
        gather.start()
        before_down()
        weights["up", l].arrived()

        def consume(slot):
            h = dot(normed_two[l][slot], columns(weights["up", l].full, 0, 512)) + b.ubias[l : l + 1]
            value, slant = gelu_and_slope(h)
            act[l][slot] = value.astype(BF16)
            slope[l][slot] = slant.astype(BF16)

        gather.run(consume)
        weights["down", l].arrived()
        after_up()

        def down_product(slot):
            return dot(act[l][slot], columns(weights["down", l].full, 0, 512), NT)

        total = sum_rows(me, down_product, send_bufs, land[1])
        gather.end()
        return middle[l][...] + (total + b.bias[l, 3:4])

    norm_rows(b.x_rows[...].astype(F32), 0, 0, normed_one[0])
    gather = Gather(me, normed_one[0], *both("rows"))
    gather.start()
    swap_mask.end()
    swap_cot.end()
    b.g_rows[me.slot] = b.cot_rows[...]
    gather_cot = Gather(me, b.g_rows, *both("cot"))
    gather.relay()
    weights["qo", 0].arrived()
    weights["up", 0].start()
    gather.run(project(0), relayed=True)
    gather.end()
    gather_cot.start()
    b.state[...] = forward(
        0,
        lambda: b.x_rows[...].astype(F32),
        weights["down", 0].start,
        nothing,
        weights["qo", 1].start,
    )
    norm_rows(b.state[...], 1, 0, normed_one[1])
    gather = Gather(me, normed_one[1], *both("rows"))
    gather.start()
    weights["qo", 1].arrived()
    weights["up", 1].start()
    gather.run(project(1))
    gather.end()
    gather_cot.relay()
    b.rows_away[...] = forward(1, lambda: b.state[...], weights["down", 1].start, nothing, nothing).astype(BF16)
    swap_out = Swap(me, b.rows_away, b.out_rows, both("swap"), 3)
    swap_out.start()

    def narrow_sum(ref, row, at, count):
        total = column_sum(ref)
        for i in range(count):
            b.narrow[row + i : row + i + 1] = total[:, (at + i) * 128 : (at + i + 1) * 128]

    def backward(l, g_own, gather_g, after_down, after_up):
        down, up, w = weights["down", l].full, weights["up", l].full, weights["qo", l].full

        def consume(slot):
            grad_act = dot(b.g_rows[slot], columns(down, 0, 512))
            slope[l][slot] = (grad_act * slope[l][slot].astype(F32)).astype(BF16)

        gather_g.run(consume, relayed=l == 1)
        grad_hid = slope[l]

        def up_back(slot):
            return dot(grad_hid[slot], columns(up, 0, 512), NT)

        def fill():
            weight_grad(b.g_rows, act[l], b.dw_down, 0, 512)
            grads["down", l].start()
            narrow_sum(grad_hid, l * 6 + 2, 0, 4)
            after_down()

        grad = sum_rows(me, up_back, send_bufs, land[0], fill)
        gather_g.end()
        back, gain_sum, shift_sum = layer_norm_back(middle[l][...], b.gain[l, 1:2], grad)
        mid = g_own() + back
        b.grad_mid[...] = mid
        b.g_attn[me.slot] = mid.astype(BF16)
        gather = Gather(me, b.g_attn, *both("rows"))
        gather.start()
        row = l * 6 + 2
        b.wide[row : row + 1] = jnp.sum(g_own(), axis=0, keepdims=True)
        b.wide[row + 1 : row + 2] = gain_sum
        b.wide[row + 2 : row + 3] = shift_sum
        b.wide[row + 3 : row + 4] = jnp.sum(mid, axis=0, keepdims=True)

        def fill_two():
            after_up()
            weight_grad(normed_two[l], grad_hid, b.dw_up, 0, 512)
            grads["up", l].start()

        def att_back(slot):
            b.grad_att[slot] = dot(b.g_attn[slot], columns(w, 384, 128)).astype(BF16)

        gather.run(att_back, fill_two)
        gather.end()
        attend_back(qkv[l], b.mask, b.grad_att)

    def first_back(l, rows, more):
        w, grad_qkv = weights["qo", l].full, qkv[l]

        def back_product(slot):
            return dot(grad_qkv[slot], columns(w, 0, 384), NT)

        def fill():
            weight_grad(normed_one[l], grad_qkv, b.dw_qo, 0, 384)
            weight_grad(b.g_attn, attended[l], b.dw_qo, 384, 128)
            grads["qo", l].start()
            more()
            total = column_sum(grad_qkv)
            b.narrow[l * 6 : l * 6 + 1] = total[:, 0:128]
            b.narrow[l * 6 + 1 : l * 6 + 2] = total[:, 256:384]

        grad = sum_rows(me, back_product, send_bufs, land[1], fill)
        back, gain_sum, shift_sum = layer_norm_back(rows(), b.gain[l, 0:1], grad)
        b.wide[l * 6 : l * 6 + 1] = gain_sum
        b.wide[l * 6 + 1 : l * 6 + 2] = shift_sum
        return b.grad_mid[...] + back

    backward(1, lambda: b.cot_rows[...].astype(F32), gather_cot, nothing, nothing)
    b.grad[...] = first_back(1, lambda: b.state[...], grads["down", 1].end)
    b.g_rows[me.slot] = b.grad[...].astype(BF16)
    gather_g = Gather(me, b.g_rows, *both("cot"))
    gather_g.start()
    swap_out.end()
    backward(0, lambda: b.grad[...], gather_g, grads["up", 1].end, grads["qo", 1].end)
    b.gradient[...] = first_back(0, lambda: b.x_rows[...].astype(F32), grads["down", 0].end)
    b.rows_away[...] = b.gradient[...].astype(BF16)
    vectors_start(me, b.wide, b.va, b.vl, *both("v1"))
    swap_grad = Swap(me, b.rows_away, b.rows_home, both("swap"), 4)
    swap_grad.start()
    for name in cuts:
        for l in range(2):
            weights[name, l].sent()
    vectors_end(me, b.narrow, b.va, b.vl, *both("v1"), b.vb, b.piece, *both("v2"), b.vectors, *both("v3"))
    swap_grad.end()

    @pl.when(me.core != me.zlo)
    def _():
        b.gradient[...] = b.rows_home[...].astype(F32)

    grads["up", 0].end()
    grads["qo", 0].end()


def nothing():
    pass


def per_device(
    x_in, valid_len, w_qkv, w_out, w_up, w_down, norm_gain, norm_shift, bias, up_bias, cotangent
):
    dp, tensor = lax.axis_index("dp"), lax.axis_index("tensor")
    slot = (dp % 2) * 4 + tensor % 4
    at = jnp.arange(4 * PAD)
    token = (at // PAD) * ROWS + at % PAD
    mask = (at % PAD < ROWS) & (token < valid_len[:, None])
    mask = jnp.broadcast_to(mask[:, None].astype(F32), (2, 8, 4 * PAD))
    shards = jnp.concatenate(
        [w_qkv.reshape(2, 64, 384), jnp.swapaxes(w_out, 1, 2), w_up, jnp.swapaxes(w_down, 1, 2)], axis=2
    )
    own_bias = lax.dynamic_slice_in_dim(bias, slot * COLS, COLS, axis=2)
    qbias = jnp.concatenate([own_bias[:, 0], jnp.zeros((2, COLS), F32), own_bias[:, 1]], axis=1)
    ubias = lax.dynamic_slice_in_dim(up_bias, slot * HID, HID, axis=1)
    vmem = pl.BlockSpec(memory_space=pltpu.VMEM)
    out_rows, gradient, sum_qo, sum_up, sum_down, vectors = pl.pallas_call(
        whole_kernel,
        out_shape=[jax.ShapeDtypeStruct(s, t) for s, t in OUTPUTS.values()],
        in_specs=[vmem] * len(INPUTS),
        out_specs=[vmem] * len(OUTPUTS),
        scratch_shapes=list(scratch_table().values()),
        compiler_params=pltpu.CompilerParams(
            collective_id=0, has_side_effects=True, vmem_limit_bytes=VMEM_BYTES
        ),
    )(x_in, cotangent, mask, shards, norm_gain, norm_shift, bias, qbias, ubias)
    full = jnp.transpose(vectors[:, 0:12], (1, 0, 2)).reshape(2, 6, D)
    own = vectors[:, 16:28].reshape(MEMBERS, 2, 6, COLS)
    q_bias = jnp.transpose(own[:, :, 0], (1, 0, 2)).reshape(2, D)
    v_bias = jnp.transpose(own[:, :, 1], (1, 0, 2)).reshape(2, D)
    return (
        out_rows[:ROWS],
        gradient[:ROWS],
        sum_qo[:, :, 0:384].reshape(2, 64, 3, COLS),
        jnp.swapaxes(sum_qo[:, :, 384:], 1, 2),
        sum_up,
        jnp.swapaxes(sum_down, 1, 2),
        jnp.stack([full[:, 0], full[:, 3]], axis=1),
        jnp.stack([full[:, 1], full[:, 4]], axis=1),
        jnp.stack([q_bias, v_bias, full[:, 5], full[:, 2]], axis=1),
        jnp.transpose(own[:, :, 2:], (1, 0, 2, 3)).reshape(2, 4096),
    )


def solution(mesh):
    rows = P(("dp", "tensor"), None)
    weights = (P(None, "dp", None, "tensor"), P(None, "tensor", "dp"), P(None, "dp", "tensor"), P(None, "tensor", "dp"))
    return jax.shard_map(
        per_device,
        mesh=mesh,
        in_specs=(rows, P("dp"), *weights, P(), P(), P(), P(), rows),
        out_specs=(rows, rows, *weights, P(), P(), P(), P()),
        check_vma=False,
    )
```

```python
import types

import jax
import jax.numpy as jnp
from jax import lax
from jax.experimental import pallas as pl
from jax.experimental.pallas import tpu as pltpu
from jax.sharding import PartitionSpec as P

MESH = pl.DeviceIdType.MESH
F32, BF16 = jnp.float32, jnp.bfloat16

D = 1024
ROWS = 146
PAD = 160
COLS = 128
HEAD = 64
HID = 512
MEMBERS = 8
WCOLS = 1536
EPSILON = 1e-06
NEG_FILL = -1e30
VMEM_BYTES = 64 * 1024 * 1024 - 65536

NN = (((1,), (0,)), ((), ()))
NT = (((1,), (1,)), ((), ()))
TN = (((0,), (0,)), ((), ()))


def dot(a, b, dims=NN):
    return lax.dot_general(a, b, dims, preferred_element_type=F32)


class Place:
    def __init__(self):
        self.dp = lax.axis_index("dp")
        self.tensor = lax.axis_index("tensor")
        self.core = self.dp % 2
        self.pair = self.dp // 2
        self.zlo = self.tensor // 4
        self.x = self.tensor % 4
        self.slot = self.core * 4 + self.x
        self.group = self.pair * 2 + self.zlo

    def peer(self, core, x):
        return {"dp": self.pair * 2 + core, "tensor": self.zlo * 4 + x}

    def sibling(self):
        return self.peer(1 - self.core, self.x)


def greet(me, work):
    barrier = pltpu.get_barrier_semaphore()

    def member(i, carry):
        pl.semaphore_signal(
            barrier,
            inc=1,
            device_id=me.peer((me.core + i // 4) % 2, (me.x + i) % 4),
            device_id_type=MESH,
        )
        return carry

    lax.fori_loop(1, MEMBERS, member, 0)

    def other(i, carry):
        pair = (me.pair + i // 4) % 8
        zlo = (me.zlo + (i // 2) % 2) % 2
        pl.semaphore_signal(
            barrier,
            inc=1,
            device_id={"dp": pair * 2 + i % 2, "tensor": zlo * 4 + me.x},
            device_id_type=MESH,
        )
        return carry

    lax.fori_loop(2, 32, other, 0)
    work()
    pl.semaphore_wait(barrier, MEMBERS - 1 + 30)


def remote(src, dst, send, recv, device):
    return pltpu.make_async_remote_copy(
        src_ref=src,
        dst_ref=dst,
        send_sem=send,
        recv_sem=recv,
        device_id=device,
        device_id_type=MESH,
    )


def chip_at(me, i):
    return (me.x + (i == 1).astype(jnp.int32) * 3 + (i == 2).astype(jnp.int32) + (i == 3).astype(jnp.int32) * 2) % 4


HALF = PAD // 2
TOP, BOTTOM = pl.ds(0, HALF), pl.ds(HALF, HALF)


class Gather:
    def __init__(self, me, g, send, recv):
        self.me, self.g, self.send, self.recv = me, g, send, recv
        self.right = me.peer(me.core, (me.x + 1) % 4)
        self.left = me.peer(me.core, (me.x + 3) % 4)
        self.from_left = me.core * 4 + (me.x + 3) % 4
        self.from_right = me.core * 4 + (me.x + 1) % 4
        self.from_far = me.core * 4 + (me.x + 2) % 4

    def copy(self, k, slot, rows, device):
        block = self.g.at[slot] if rows is None else self.g.at[slot, rows]
        return remote(block, block, self.send.at[k], self.recv.at[k], device)

    def table(self):
        me = self.me
        sibling = me.sibling()
        return [
            (0, me.slot, TOP, self.right),
            (1, me.slot, BOTTOM, self.right),
            (2, me.slot, TOP, self.left),
            (3, me.slot, BOTTOM, self.left),
            (4, self.from_left, TOP, self.right),
            (5, self.from_right, BOTTOM, self.left),
            (6, me.slot, None, sibling),
            (7, self.from_left, None, sibling),
            (8, self.from_right, None, sibling),
            (9, self.from_far, None, sibling),
        ]

    def start_copies(self, *which):
        for k in which:
            self.copy(*self.table()[k]).start()

    def start(self):
        self.start_copies(6, 0, 3, 1, 2)

    def arrived(self, *which):
        for k in which:
            _, slot, rows, device = self.table()[k]
            self.copy(k, slot, rows, device).wait_recv()

    def relay(self):
        self.arrived(0)
        self.start_copies(4)
        self.arrived(3)
        self.start_copies(5)

    def run(self, image, consume, relayed=False):
        me = self.me

        def step(i, carry):
            if image == 0 and not relayed:

                @pl.when(i == 1 + me.core)
                def _():
                    self.relay()

            @pl.when((i == 1) & (me.core == image))
            def _():
                self.arrived(1)
                self.start_copies(7)

            @pl.when((i == 2) & (me.core == image))
            def _():
                self.arrived(2)
                self.start_copies(8)

            @pl.when((i == 3) & (me.core == image))
            def _():
                self.arrived(4, 5)
                self.start_copies(9)

            @pl.when(me.core != image)
            def _():
                slot = image * 4 + chip_at(me, i)
                self.copy(6 + i, slot, None, me.sibling()).wait_recv()

            consume(image * 4 + chip_at(me, i))
            return carry

        lax.fori_loop(0, 4, step, 0)

    def end(self):
        for row in self.table():
            self.copy(*row).wait_send()


GATHER_SEMS = [pltpu.SemaphoreType.DMA((10,)), pltpu.SemaphoreType.DMA((10,))]

SUM_SEND = [
    pltpu.VMEM((4, PAD, D), BF16),
    pltpu.VMEM((3, PAD, D), BF16),
    pltpu.VMEM((PAD, D), F32),
    pltpu.VMEM((2, HALF, D), F32),
]
SUM_LAND = [
    pltpu.VMEM((4, PAD, D), BF16),
    pltpu.VMEM((PAD, D), BF16),
    pltpu.VMEM((2, PAD, D), BF16),
    pltpu.SemaphoreType.DMA((4,)),
    pltpu.SemaphoreType.DMA((4,)),
    pltpu.SemaphoreType.DMA((6,)),
    pltpu.SemaphoreType.DMA((6,)),
]


class RowSum:
    def __init__(self, me, produce, send_bufs, land_bufs):
        self.me, self.produce, self.send_bufs, self.land_bufs = me, produce, send_bufs, land_bufs
        self.right, self.left = me.peer(me.core, (me.x + 1) % 4), me.peer(me.core, (me.x + 3) % 4)

    def chip(self, i):
        two, three = (i == 2).astype(jnp.int32), (i == 3).astype(jnp.int32)
        return (self.me.x + 2 + (i == 1).astype(jnp.int32) * 3 + two + three * 2) % 4

    def to_sibling(self, i):
        s1, r1, ss1, rs1 = self.send_bufs[0], self.land_bufs[0], self.land_bufs[3], self.land_bufs[4]
        return remote(s1.at[i], r1.at[i], ss1.at[i], rs1.at[i], self.me.sibling())

    def along(self, k):
        s2, (_, ra, rb, _, _, ss2, rs2) = self.send_bufs[1], self.land_bufs
        src, dst, device = (
            (s2.at[0, TOP], ra.at[TOP], self.right),
            (s2.at[0, BOTTOM], ra.at[BOTTOM], self.left),
            (s2.at[1, BOTTOM], rb.at[0, BOTTOM], self.right),
            (s2.at[2, TOP], rb.at[1, TOP], self.left),
            (s2.at[1, TOP], rb.at[0, TOP], self.right),
            (s2.at[2, BOTTOM], rb.at[1, BOTTOM], self.left),
        )[k]
        return remote(src, dst, ss2.at[k], rs2.at[k], device)

    def begin(self, image):
        me = self.me
        s1, s2, acc, hold = self.send_bufs
        r1 = self.land_bufs[0]

        def for_sibling(i, carry):
            s1[i] = self.produce(image * 4 + self.chip(i)).astype(BF16)
            self.to_sibling(i).start()
            return carry

        def own(i, carry):
            part = self.produce(image * 4 + self.chip(i))
            self.to_sibling(i).wait_recv()
            acc[...] = part + r1[i].astype(F32)

            @pl.when(i == 0)
            def _():
                s2[0] = acc[...].astype(BF16)
                self.along(0).start()
                self.along(1).start()

            @pl.when(i == 1)
            def _():
                s2[1, BOTTOM] = acc[BOTTOM].astype(BF16)
                self.along(2).start()
                hold[0] = acc[TOP]

            @pl.when(i == 2)
            def _():
                s2[2, TOP] = acc[TOP].astype(BF16)
                self.along(3).start()
                hold[1] = acc[BOTTOM]

            return carry

        @pl.when(me.core == image)
        def _():
            lax.fori_loop(0, 4, own, 0)

        @pl.when(me.core != image)
        def _():
            lax.fori_loop(0, 4, for_sibling, 0)

    def finish(self):
        _, s2, acc, hold = self.send_bufs
        _, ra, rb, _, _, _, _ = self.land_bufs
        self.along(0).wait_recv()
        s2[1, TOP] = (hold[0] + ra[TOP].astype(F32)).astype(BF16)
        self.along(4).start()
        self.along(1).wait_recv()
        s2[2, BOTTOM] = (hold[1] + ra[BOTTOM].astype(F32)).astype(BF16)
        self.along(5).start()
        for k in range(2, 6):
            self.along(k).wait_recv()
        return acc[...] + rb[0].astype(F32) + rb[1].astype(F32)

    def end(self):
        for i in range(4):
            self.to_sibling(i).wait_send()
        for k in range(6):
            self.along(k).wait_send()


PLANE_SEMS = [pltpu.SemaphoreType.DMA((16,)), pltpu.SemaphoreType.DMA((16,))]


def weights_copy(me, i, shard, full, send, recv):
    pair, zlo = (me.pair + i // 2) % 8, (me.zlo + i) % 2
    device = {"dp": pair * 2 + me.zlo, "tensor": zlo * 4 + me.x}
    return remote(shard, full.at[me.dp], send.at[i], recv.at[me.dp], device)


def weights_start(me, shard, full, send, recv):
    def step(i, carry):
        weights_copy(me, i, shard, full, send, recv).start()
        return carry

    own = me.core == me.zlo

    @pl.when(own)
    def _():
        pltpu.make_async_copy(shard, full.at[me.dp], recv.at[me.dp]).start()

    @pl.when(jnp.logical_not(own))
    def _():
        weights_copy(me, 0, shard, full, send, recv).start()

    lax.fori_loop(1, 16, step, 0)


def weights_arrived(me, shard, full, send, recv):
    def step(i, carry):
        remote(shard, full.at[i], send.at[i], recv.at[i], me.sibling()).wait_recv()
        return carry

    lax.fori_loop(0, 16, step, 0)


def weights_sent(me, shard, full, send, recv):
    @pl.when(me.core != me.zlo)
    def _():
        weights_copy(me, 0, shard, full, send, recv).wait_send()

    def step(i, carry):
        weights_copy(me, i, shard, full, send, recv).wait_send()
        return carry

    lax.fori_loop(1, 16, step, 0)


def grads_copy(me, i, part, land, send, recv):
    to = (me.dp + i) % 16
    device = {"dp": to, "tensor": me.slot}
    return remote(part.at[to], land.at[me.group], send.at[i], recv.at[me.group], device)


def grads_start(me, part, land, send, recv):
    own = me.zlo == me.core

    @pl.when(own)
    def _():
        pltpu.make_async_copy(part.at[me.dp], land.at[me.group], recv.at[me.group]).start()

    @pl.when(jnp.logical_not(own))
    def _():
        grads_copy(me, 0, part, land, send, recv).start()

    def step(i, carry):
        grads_copy(me, i, part, land, send, recv).start()
        return carry

    lax.fori_loop(1, 16, step, 0)


def grads_end(me, part, land, send, recv, out):
    def arrived(i, carry):
        remote(part.at[0], land.at[i], send.at[i], recv.at[i], me.sibling()).wait_recv()
        return carry

    lax.fori_loop(0, 16, arrived, 0)

    @pl.when(me.zlo != me.core)
    def _():
        grads_copy(me, 0, part, land, send, recv).wait_send()

    def sent(i, carry):
        grads_copy(me, i, part, land, send, recv).wait_send()
        return carry

    lax.fori_loop(1, 16, sent, 0)
    total = land[0].astype(F32)
    for i in range(1, 16):
        total = total + land[i].astype(F32)
    out[...] = total


def normalized(rows):
    centred = rows - jnp.mean(rows, axis=-1, keepdims=True)
    scale = lax.rsqrt(jnp.mean(centred * centred, axis=-1, keepdims=True) + EPSILON)
    return centred * scale, scale


def layer_norm(rows, gain, shift):
    return normalized(rows)[0] * gain + shift


def layer_norm_back(rows, gain, grad):
    unit, scale = normalized(rows)
    inner = grad * gain
    mean_one = jnp.mean(inner, axis=-1, keepdims=True)
    mean_two = jnp.mean(inner * unit, axis=-1, keepdims=True)
    back = scale * (inner - mean_one - unit * mean_two)
    return back, jnp.sum(grad * unit, axis=0, keepdims=True), jnp.sum(grad, axis=0, keepdims=True)


def erf(v):
    v = jnp.clip(v, -4.0, 4.0)
    s = v * v
    top = F32(-2.72614225801306e-10)
    for a in (
        2.77068142495902e-08,
        -2.10102402082508e-06,
        -5.69250639462346e-05,
        -7.34990630326855e-04,
        -2.95459980854025e-03,
        -1.60960333262415e-02,
    ):
        top = top * s + F32(a)
    low = F32(-1.45660718464996e-05)
    for b in (
        -2.13374055278905e-04,
        -1.68282697438203e-03,
        -7.37332916720468e-03,
        -1.42647390514189e-02,
    ):
        low = low * s + F32(b)
    return v * top / low


def normal_below(v):
    return 0.5 * (1.0 + erf(v * F32(0.7071067811865476)))


def gelu_and_slope(v):
    below = normal_below(v)
    return v * below, below + v * jnp.exp(-0.5 * v * v) * F32(0.3989422804014327)


def weight_grad(left, right, out, at, width):
    def tile(i, carry):
        a = left[:, :, pl.ds(pl.multiple_of(i * 256, 256), 256)].reshape(MEMBERS * PAD, 256)
        b = right[...].reshape(MEMBERS * PAD, width)
        block = dot(a, b, TN).astype(BF16).reshape(4, 64, width)
        out[pl.ds(i * 4, 4), :, at : at + width] = block
        return carry

    lax.fori_loop(0, D // 256, tile, 0)


def columns(w, at, width):
    return w[:, :, at : at + width].reshape(D, width)


def column_sum(ref):
    def step(i, total):
        return total + jnp.sum(ref[i].astype(F32), axis=0, keepdims=True)

    return lax.fori_loop(0, MEMBERS, step, jnp.zeros((1, ref.shape[2]), F32))


def head_parts(qkv, i, at):
    return qkv[pl.ds(i * 4, 4), :, at * COLS : (at + 1) * COLS].reshape(4 * PAD, COLS)


def attend(image, qkv, mask, out):
    lane = lax.broadcasted_iota(jnp.int32, (1, COLS), 1)

    def one(i, carry):
        q, k, v = (head_parts(qkv, i, j) for j in range(3))
        valid = mask[i, 0:1] > 0.5
        total = None
        for h in range(2):
            mine = (lane >= h * HEAD) & (lane < (h + 1) * HEAD)
            scores = dot(jnp.where(mine, q, jnp.zeros_like(q)), k, NT) * F32(HEAD**-0.5)
            scores = jnp.where(valid, scores, NEG_FILL)
            e = jnp.exp(scores - jnp.max(scores, axis=-1, keepdims=True))
            prob = (e * (1.0 / jnp.sum(e, axis=-1, keepdims=True))).astype(BF16)
            mixed = dot(prob, v)
            total = mixed if total is None else jnp.where(mine, mixed, total)
        out[pl.ds(i * 4, 4)] = total.astype(BF16).reshape(4, PAD, COLS)
        return carry

    lax.fori_loop(image, image + 1, one, 0)


def attend_back(image, qkv, mask, grad):
    lane = lax.broadcasted_iota(jnp.int32, (1, COLS), 1)

    def one(i, carry):
        q, k, v = (head_parts(qkv, i, j) for j in range(3))
        g = grad[pl.ds(i * 4, 4)].reshape(4 * PAD, COLS)
        valid = mask[i].T[:, 0:1] > 0.5
        parts = [None, None, None]
        for h in range(2):
            mine = (lane >= h * HEAD) & (lane < (h + 1) * HEAD)
            scores = dot(k, jnp.where(mine, q, jnp.zeros_like(q)), NT) * F32(HEAD**-0.5)
            scores = jnp.where(valid, scores, NEG_FILL)
            e = jnp.exp(scores - jnp.max(scores, axis=0, keepdims=True))
            prob = e * (1.0 / jnp.sum(e, axis=0, keepdims=True))
            grad_value = dot(prob.astype(BF16), g)
            grad_prob = dot(v, jnp.where(mine, g, jnp.zeros_like(g)), NT)
            inner = jnp.sum(grad_prob * prob, axis=0, keepdims=True)
            grad_scores = (prob * (grad_prob - inner)).astype(BF16)
            grad_key = dot(grad_scores, q) * F32(HEAD**-0.5)
            grad_query = dot(grad_scores, k, TN) * F32(HEAD**-0.5)
            new = [grad_query, grad_key, grad_value]
            parts = new if h == 0 else [jnp.where(mine, n, p) for n, p in zip(new, parts)]
        for j in range(3):
            qkv[pl.ds(i * 4, 4), :, j * COLS : (j + 1) * COLS] = parts[j].astype(BF16).reshape(4, PAD, COLS)
        return carry

    lax.fori_loop(image, image + 1, one, 0)


def vectors_start(me, wide, va, vl, send, recv):
    for s in range(MEMBERS):
        va[s] = wide[:, s * 128 : (s + 1) * 128]

    def step(i, carry):
        core, x = (me.core + i // 4) % 2, (me.x + i) % 4
        remote(va.at[core * 4 + x], vl.at[i], send.at[i], recv.at[i], me.peer(core, x)).start()
        return carry

    lax.fori_loop(1, MEMBERS, step, 0)


def vectors_end(me, narrow, va, vl, send, recv, vb, piece, send2, recv2, out, send3, recv3):
    total = va[me.slot]
    for i in range(1, MEMBERS):
        remote(va.at[0], vl.at[i], send.at[i], recv.at[i], me.sibling()).wait()
        total = total + vl[i]
    piece[0:16] = total
    piece[16:32] = narrow[...]

    def to_group(i):
        pair, zlo = (me.pair + i // 2) % 8, (me.zlo + i) % 2
        device = {"dp": pair * 2 + me.core, "tensor": zlo * 4 + me.x}
        return remote(piece, vb.at[me.group], send2.at[i], recv2.at[me.group], device)

    def start(i, carry):
        to_group(i).start()
        return carry

    lax.fori_loop(1, 16, start, 0)
    vb[me.group] = piece[...]

    def end(i, carry):
        to_group(i).wait_send()
        group = (me.group + i) % 16
        remote(piece, vb.at[group], send2.at[i], recv2.at[group], me.sibling()).wait_recv()
        return carry

    lax.fori_loop(1, 16, end, 0)
    total = vb[0]
    for i in range(1, 16):
        total = total + vb[i]
    out[me.slot] = total
    own = out.at[me.slot]

    def to_member(i):
        core, x = (me.core + i // 4) % 2, (me.x + i) % 4
        return remote(own, own, send3.at[i], recv3.at[me.slot], me.peer(core, x))

    def start_three(i, carry):
        to_member(i).start()
        return carry

    lax.fori_loop(1, MEMBERS, start_three, 0)

    def end_three(i, carry):
        to_member(i).wait_send()
        slot = ((me.core + i // 4) % 2) * 4 + (me.x + i) % 4
        remote(own, out.at[slot], send3.at[i], recv3.at[slot], me.sibling()).wait_recv()
        return carry

    lax.fori_loop(1, MEMBERS, end_three, 0)


class Weights:
    def __init__(self, me, shard, full, send, recv):
        self.args, self.full = (me, shard, full, send, recv), full

    def start(self):
        weights_start(*self.args)

    def arrived(self):
        weights_arrived(*self.args)

    def sent(self):
        weights_sent(*self.args)


class Grads:
    def __init__(self, me, part, land, send, recv, out):
        self.args, self.part = (me, part, land, send, recv, out), part

    def start(self):
        grads_start(*self.args[:5])

    def end(self):
        grads_end(*self.args)


class Swap:
    def __init__(self, me, src, dst, sems, k):
        self.away = me.core != me.zlo
        self.src, self.dst = src, dst
        partner = {"dp": me.pair * 2 + me.zlo, "tensor": me.core * 4 + me.x}
        self.copy = remote(src, dst, sems[0].at[k], sems[1].at[k], partner)

    def start(self):
        @pl.when(self.away)
        def _():
            self.copy.start()

    def end(self):
        @pl.when(self.away)
        def _():
            self.copy.wait()

        @pl.when(jnp.logical_not(self.away))
        def _():
            self.dst[...] = self.src[...]


ROWS_ALL, ROWS_OWN, PART = (MEMBERS, PAD, D), (PAD, D), (16, 64, 512)
HID_ALL, ATT_ALL, QKV_ALL, SUMMED = (MEMBERS, PAD, HID), (MEMBERS, PAD, COLS), (MEMBERS, PAD, 384), (64, 512)
DMA = pltpu.SemaphoreType.DMA

INPUTS = ("x_in", "cot_in", "mask_in", "shards", "gain", "shift", "bias", "qbias", "ubias")
OUTPUTS = {
    "out_rows": (ROWS_OWN, BF16),
    "gradient": (ROWS_OWN, F32),
    "sum_qo": ((2, *SUMMED), F32),
    "sum_up": ((2, *SUMMED), F32),
    "sum_down": ((2, *SUMMED), F32),
    "vectors": ((MEMBERS, 32, 128), F32),
}


def scratch_table():
    table = {"padded": pltpu.VMEM(ROWS_OWN, F32)}

    def add(name, shape, dtype, count=None):
        if count is None:
            table[name] = pltpu.VMEM(shape, dtype)
        for i in range(count or 0):
            table[f"{name}{i}"] = pltpu.VMEM(shape, dtype)

    for name in ("x_own", "x_rows", "cot_own", "cot_rows", "rows_away", "rows_home"):
        add(name, ROWS_OWN, BF16)
    add("mask", (2, 8, 4 * PAD), F32)
    for name in ("qo", "up", "down", "land_qo", "land_up", "land_down"):
        add(name, PART, BF16, 2)
    for name in ("dw_qo", "dw_up", "dw_down"):
        add(name, PART, BF16)
    add("normed_one", ROWS_ALL, BF16, 2)
    add("normed_two", ROWS_ALL, BF16, 2)
    add("qkv", QKV_ALL, BF16, 2)
    add("attended", ATT_ALL, BF16, 2)
    add("slope", HID_ALL, BF16, 2)
    add("act", HID_ALL, BF16, 2)
    add("middle", ROWS_OWN, F32, 2)
    add("state", ROWS_OWN, F32)
    add("g_rows", ROWS_ALL, BF16)
    add("g_attn", ROWS_ALL, BF16)
    add("grad_att", ATT_ALL, BF16)
    add("grad_mid", ROWS_OWN, F32)
    add("grad", ROWS_OWN, F32)
    add("wide", (16, D), F32)
    add("narrow", (16, 128), F32)
    add("va", (MEMBERS, 16, 128), F32)
    add("vl", (MEMBERS, 16, 128), F32)
    add("vb", (16, 32, 128), F32)
    add("piece", (32, 128), F32)
    for i, spec in enumerate(SUM_SEND):
        table[f"sum_send{i}"] = spec
    for j in range(2):
        for i, spec in enumerate(SUM_LAND):
            table[f"sum_land{j}_{i}"] = spec
    for name, count in (("rows", 10), ("cot", 10), ("swap", 5), ("v1", 8), ("v2", 16), ("v3", 8)):
        table[name + "_send"], table[name + "_recv"] = DMA((count,)), DMA((count,))
    for name in ("w", "g"):
        table[name + "_send"], table[name + "_recv"] = DMA((6, 16)), DMA((6, 16))
    return table


def whole_kernel(*refs):
    table = scratch_table()
    names = [*INPUTS, *OUTPUTS, *table]
    b = types.SimpleNamespace(**dict(zip(names, refs, strict=True)))
    me = Place()

    def padded(rows, out):
        b.padded[0:ROWS] = rows[...].astype(F32)
        b.padded[ROWS:PAD] = jnp.zeros((PAD - ROWS, D), F32)
        out[...] = b.padded[...].astype(BF16)

    def work():
        padded(b.x_in, b.x_own)
        padded(b.cot_in, b.cot_own)
        b.wide[...] = jnp.zeros_like(b.wide)
        b.narrow[...] = jnp.zeros_like(b.narrow)

    greet(me, work)

    def both(name):
        return getattr(b, name + "_send"), getattr(b, name + "_recv")

    def pair(name):
        return [getattr(b, name + "0"), getattr(b, name + "1")]

    cuts = {"qo": pl.ds(0, 512), "up": pl.ds(512, 512), "down": pl.ds(1024, 512)}
    weights, grads = {}, {}
    for n, name in enumerate(cuts):
        for l in range(2):
            k = n * 2 + l
            shard = b.shards.at[l, :, cuts[name]]
            weights[name, l] = Weights(me, shard, pair(name)[l], b.w_send.at[k], b.w_recv.at[k])
            part = getattr(b, "dw_" + name)
            out = getattr(b, "sum_" + name).at[l]
            grads[name, l] = Grads(me, part, pair("land_" + name)[l], b.g_send.at[k], b.g_recv.at[k], out)
    send_bufs = [getattr(b, f"sum_send{i}") for i in range(len(SUM_SEND))]
    land = [[getattr(b, f"sum_land{j}_{i}") for i in range(len(SUM_LAND))] for j in range(2)]
    normed_one, normed_two, qkv, attended = (pair(n) for n in ("normed_one", "normed_two", "qkv", "attended"))
    slope, act, middle = (pair(n) for n in ("slope", "act", "middle"))

    def norm_rows(rows, l, i, out):
        out[me.slot] = layer_norm(rows, b.gain[l, i : i + 1], b.shift[l, i : i + 1]).astype(BF16)

    def gather_of(ref, name="rows"):
        return Gather(me, ref, *both(name))

    def sum_of(produce, which):
        return RowSum(me, produce, send_bufs, land[which])

    swap_x = Swap(me, b.x_own, b.x_rows, both("swap"), 0)
    swap_x.start()
    swap_mask = Swap(me, b.mask_in, b.mask, both("swap"), 1)
    swap_mask.start()
    swap_cot = Swap(me, b.cot_own, b.cot_rows, both("swap"), 2)
    swap_x.end()
    weights["qo", 0].start()
    norm_rows(b.x_rows[...].astype(F32), 0, 0, normed_one[0])
    gather = gather_of(normed_one[0])
    gather.start()
    swap_mask.end()
    gather.relay()
    weights["qo", 0].arrived()
    swap_cot.start()
    weights["up", 0].start()
    gather_cot = gather_of(b.g_rows, "cot")

    def project(l):
        w = weights["qo", l].full

        def consume(slot):
            qkv[l][slot] = (dot(normed_one[l][slot], columns(w, 0, 384)) + b.qbias[l : l + 1]).astype(BF16)

        return consume

    def forward(l, gather, relayed, state, between, finish):
        w = weights["qo", l].full

        def out_product(slot):
            return dot(attended[l][slot], columns(w, 384, 128), NT)

        sums = sum_of(out_product, 0)
        for image in range(2):
            gather.run(image, project(l), relayed=relayed)
            if image == 0:
                between()
            attend(image, qkv[l], b.mask, attended[l])
            sums.begin(image)
        gather.end()
        weights["down", l].start()
        middle[l][...] = state() + (sums.finish() + b.bias[l, 2:3])
        norm_rows(middle[l][...], l, 1, normed_two[l])
        gather = gather_of(normed_two[l])
        gather.start()
        sums.end()
        weights["up", l].arrived()

        def consume(slot):
            h = dot(normed_two[l][slot], columns(weights["up", l].full, 0, 512)) + b.ubias[l : l + 1]
            value, slant = gelu_and_slope(h)
            act[l][slot] = value.astype(BF16)
            slope[l][slot] = slant.astype(BF16)

        def down_product(slot):
            return dot(act[l][slot], columns(weights["down", l].full, 0, 512), NT)

        sums = sum_of(down_product, 1)
        gather.run(0, consume)
        weights["down", l].arrived()
        if l == 0:
            weights["qo", 1].start()
        sums.begin(0)
        gather.run(1, consume)
        sums.begin(1)
        gather.end()
        finish(middle[l][...] + (sums.finish() + b.bias[l, 3:4]))
        sums.end()

    gather_one = gather_of(normed_one[1])

    def to_layer_one(rows):
        b.state[...] = rows
        norm_rows(rows, 1, 0, normed_one[1])
        gather_one.start()

    def cot_start():
        swap_cot.end()
        b.g_rows[me.slot] = b.cot_rows[...]
        gather_cot.start()

    forward(0, gather, True, lambda: b.x_rows[...].astype(F32), cot_start, to_layer_one)
    weights["qo", 1].arrived()
    weights["up", 1].start()
    swap_out = Swap(me, b.rows_away, b.out_rows, both("swap"), 3)

    def to_output(rows):
        b.rows_away[...] = rows.astype(BF16)
        swap_out.start()

    forward(1, gather_one, False, lambda: b.state[...], gather_cot.relay, to_output)

    def narrow_sum(ref, row, at, count):
        total = column_sum(ref)
        for i in range(count):
            b.narrow[row + i : row + i + 1] = total[:, (at + i) * 128 : (at + i + 1) * 128]

    def backward(l, g_own, gather, rows, after_down, before_up, before_qo, finish):
        down, up, w = weights["down", l].full, weights["up", l].full, weights["qo", l].full
        grad_hid, grad_qkv = slope[l], qkv[l]

        def consume(slot):
            grad_act = dot(b.g_rows[slot], columns(down, 0, 512))
            grad_hid[slot] = (grad_act * grad_hid[slot].astype(F32)).astype(BF16)

        def up_back(slot):
            return dot(grad_hid[slot], columns(up, 0, 512), NT)

        sums = sum_of(up_back, 0)
        for image in range(2):
            gather.run(image, consume, relayed=l == 1)
            sums.begin(image)
        gather.end()
        weight_grad(b.g_rows, act[l], b.dw_down, 0, 512)
        grads["down", l].start()
        back, gain_sum, shift_sum = layer_norm_back(middle[l][...], b.gain[l, 1:2], sums.finish())
        mid = g_own() + back
        b.grad_mid[...] = mid
        b.g_attn[me.slot] = mid.astype(BF16)
        gather = gather_of(b.g_attn)
        gather.start()
        sums.end()
        row = l * 6 + 2
        b.wide[row : row + 1] = jnp.sum(g_own(), axis=0, keepdims=True)
        b.wide[row + 1 : row + 2] = gain_sum
        b.wide[row + 2 : row + 3] = shift_sum
        b.wide[row + 3 : row + 4] = jnp.sum(mid, axis=0, keepdims=True)
        before_up()
        weight_grad(normed_two[l], grad_hid, b.dw_up, 0, 512)
        grads["up", l].start()

        def att_back(slot):
            b.grad_att[slot] = dot(b.g_attn[slot], columns(w, 384, 128)).astype(BF16)

        def back_product(slot):
            return dot(grad_qkv[slot], columns(w, 0, 384), NT)

        sums = sum_of(back_product, 1)
        for image in range(2):
            gather.run(image, att_back)
            attend_back(image, grad_qkv, b.mask, b.grad_att)
            sums.begin(image)
        gather.end()
        before_qo()
        weight_grad(normed_one[l], grad_qkv, b.dw_qo, 0, 384)
        weight_grad(b.g_attn, attended[l], b.dw_qo, 384, 128)
        grads["qo", l].start()
        back, gain_sum, shift_sum = layer_norm_back(rows(), b.gain[l, 0:1], sums.finish())
        finish(b.grad_mid[...] + back)
        b.wide[l * 6 : l * 6 + 1] = gain_sum
        b.wide[l * 6 + 1 : l * 6 + 2] = shift_sum
        total = column_sum(grad_qkv)
        b.narrow[l * 6 : l * 6 + 1] = total[:, 0:128]
        b.narrow[l * 6 + 1 : l * 6 + 2] = total[:, 256:384]
        narrow_sum(grad_hid, l * 6 + 2, 0, 4)
        sums.end()
        after_down()

    gather_g = gather_of(b.g_rows, "cot")

    def to_layer_zero(rows):
        b.grad[...] = rows
        b.g_rows[me.slot] = rows.astype(BF16)
        gather_g.start()

    backward(
        1, lambda: b.cot_rows[...].astype(F32), gather_cot, lambda: b.state[...], grads["down", 1].end, nothing, nothing,
        to_layer_zero,
    )
    swap_out.end()
    swap_grad = Swap(me, b.rows_away, b.rows_home, both("swap"), 4)

    def to_input(rows):
        b.gradient[...] = rows
        b.rows_away[...] = rows.astype(BF16)
        swap_grad.start()

    backward(
        0, lambda: b.grad[...], gather_g, lambda: b.x_rows[...].astype(F32), grads["down", 0].end, grads["up", 1].end,
        grads["qo", 1].end, to_input,
    )
    vectors_start(me, b.wide, b.va, b.vl, *both("v1"))
    for name in cuts:
        for l in range(2):
            weights[name, l].sent()
    vectors_end(me, b.narrow, b.va, b.vl, *both("v1"), b.vb, b.piece, *both("v2"), b.vectors, *both("v3"))
    swap_grad.end()

    @pl.when(me.core != me.zlo)
    def _():
        b.gradient[...] = b.rows_home[...].astype(F32)

    grads["up", 0].end()
    grads["qo", 0].end()


def nothing():
    pass


def per_device(
    x_in, valid_len, w_qkv, w_out, w_up, w_down, norm_gain, norm_shift, bias, up_bias, cotangent
):
    dp, tensor = lax.axis_index("dp"), lax.axis_index("tensor")
    slot = (dp % 2) * 4 + tensor % 4
    at = jnp.arange(4 * PAD)
    token = (at // PAD) * ROWS + at % PAD
    mask = (at % PAD < ROWS) & (token < valid_len[:, None])
    mask = jnp.broadcast_to(mask[:, None].astype(F32), (2, 8, 4 * PAD))
    shards = jnp.concatenate(
        [w_qkv.reshape(2, 64, 384), jnp.swapaxes(w_out, 1, 2), w_up, jnp.swapaxes(w_down, 1, 2)], axis=2
    )
    own_bias = lax.dynamic_slice_in_dim(bias, slot * COLS, COLS, axis=2)
    qbias = jnp.concatenate([own_bias[:, 0], jnp.zeros((2, COLS), F32), own_bias[:, 1]], axis=1)
    ubias = lax.dynamic_slice_in_dim(up_bias, slot * HID, HID, axis=1)
    vmem = pl.BlockSpec(memory_space=pltpu.VMEM)
    out_rows, gradient, sum_qo, sum_up, sum_down, vectors = pl.pallas_call(
        whole_kernel,
        out_shape=[jax.ShapeDtypeStruct(s, t) for s, t in OUTPUTS.values()],
        in_specs=[vmem] * len(INPUTS),
        out_specs=[vmem] * len(OUTPUTS),
        scratch_shapes=list(scratch_table().values()),
        compiler_params=pltpu.CompilerParams(
            collective_id=0, has_side_effects=True, vmem_limit_bytes=VMEM_BYTES
        ),
    )(x_in, cotangent, mask, shards, norm_gain, norm_shift, bias, qbias, ubias)
    full = jnp.transpose(vectors[:, 0:12], (1, 0, 2)).reshape(2, 6, D)
    own = vectors[:, 16:28].reshape(MEMBERS, 2, 6, COLS)
    q_bias = jnp.transpose(own[:, :, 0], (1, 0, 2)).reshape(2, D)
    v_bias = jnp.transpose(own[:, :, 1], (1, 0, 2)).reshape(2, D)
    return (
        out_rows[:ROWS],
        gradient[:ROWS],
        sum_qo[:, :, 0:384].reshape(2, 64, 3, COLS),
        jnp.swapaxes(sum_qo[:, :, 384:], 1, 2),
        sum_up,
        jnp.swapaxes(sum_down, 1, 2),
        jnp.stack([full[:, 0], full[:, 3]], axis=1),
        jnp.stack([full[:, 1], full[:, 4]], axis=1),
        jnp.stack([q_bias, v_bias, full[:, 5], full[:, 2]], axis=1),
        jnp.transpose(own[:, :, 2:], (1, 0, 2, 3)).reshape(2, 4096),
    )


def solution(mesh):
    rows = P(("dp", "tensor"), None)
    weights = (P(None, "dp", None, "tensor"), P(None, "tensor", "dp"), P(None, "dp", "tensor"), P(None, "tensor", "dp"))
    return jax.shard_map(
        per_device,
        mesh=mesh,
        in_specs=(rows, P("dp"), *weights, P(), P(), P(), P(), rows),
        out_specs=(rows, rows, *weights, P(), P(), P(), P()),
        check_vma=False,
    )
```

```python
import types

import jax
import jax.numpy as jnp
from jax import lax
from jax.experimental import pallas as pl
from jax.experimental.pallas import tpu as pltpu
from jax.sharding import PartitionSpec as P

MESH = pl.DeviceIdType.MESH
F32, BF16 = jnp.float32, jnp.bfloat16

D = 1024
ROWS = 146
PAD = 160
COLS = 128
HEAD = 64
HID = 512
MEMBERS = 8
WCOLS = 1536
EPSILON = 1e-06
NEG_FILL = -1e30
VMEM_BYTES = 64 * 1024 * 1024 - 65536

NN = (((1,), (0,)), ((), ()))
NT = (((1,), (1,)), ((), ()))
TN = (((0,), (0,)), ((), ()))


def dot(a, b, dims=NN):
    return lax.dot_general(a, b, dims, preferred_element_type=F32)


class Place:
    def __init__(self):
        self.dp = lax.axis_index("dp")
        self.tensor = lax.axis_index("tensor")
        self.core = self.dp % 2
        self.pair = self.dp // 2
        self.zlo = self.tensor // 4
        self.x = self.tensor % 4
        self.slot = self.core * 4 + self.x
        self.group = self.pair * 2 + self.zlo

    def peer(self, core, x):
        return {"dp": self.pair * 2 + core, "tensor": self.zlo * 4 + x}

    def sibling(self):
        return self.peer(1 - self.core, self.x)


def greet(me, work):
    barrier = pltpu.get_barrier_semaphore()

    def member(i, carry):
        pl.semaphore_signal(
            barrier,
            inc=1,
            device_id=me.peer((me.core + i // 4) % 2, (me.x + i) % 4),
            device_id_type=MESH,
        )
        return carry

    lax.fori_loop(1, MEMBERS, member, 0)

    def other(i, carry):
        pair = (me.pair + i // 4) % 8
        zlo = (me.zlo + (i // 2) % 2) % 2
        pl.semaphore_signal(
            barrier,
            inc=1,
            device_id={"dp": pair * 2 + i % 2, "tensor": zlo * 4 + me.x},
            device_id_type=MESH,
        )
        return carry

    lax.fori_loop(2, 32, other, 0)
    work()
    pl.semaphore_wait(barrier, MEMBERS - 1 + 30)


def remote(src, dst, send, recv, device):
    return pltpu.make_async_remote_copy(
        src_ref=src,
        dst_ref=dst,
        send_sem=send,
        recv_sem=recv,
        device_id=device,
        device_id_type=MESH,
    )


def slot_at(me, i):
    sibling = (i == 1) | (i == 4) | (i == 5) | (i == 7)
    far = (i >= 6).astype(jnp.int32) * 2
    left = ((i == 2) | (i == 4)).astype(jnp.int32) * 3
    right = ((i == 3) | (i == 5)).astype(jnp.int32)
    core = (me.core + sibling.astype(jnp.int32)) % 2
    return core * 4 + (me.x + far + left + right) % 4


HALF = PAD // 2
TOP, BOTTOM = pl.ds(0, HALF), pl.ds(HALF, HALF)


class Gather:
    def __init__(self, me, g, send, recv):
        self.me, self.g, self.send, self.recv = me, g, send, recv
        self.right = me.peer(me.core, (me.x + 1) % 4)
        self.left = me.peer(me.core, (me.x + 3) % 4)
        self.from_left = me.core * 4 + (me.x + 3) % 4
        self.from_right = me.core * 4 + (me.x + 1) % 4
        self.from_far = me.core * 4 + (me.x + 2) % 4

    def copy(self, k, slot, rows, device):
        block = self.g.at[slot] if rows is None else self.g.at[slot, rows]
        return remote(block, block, self.send.at[k], self.recv.at[k], device)

    def table(self):
        me = self.me
        sibling = me.sibling()
        return [
            (0, me.slot, TOP, self.right),
            (1, me.slot, BOTTOM, self.right),
            (2, me.slot, TOP, self.left),
            (3, me.slot, BOTTOM, self.left),
            (4, self.from_left, TOP, self.right),
            (5, self.from_right, BOTTOM, self.left),
            (6, me.slot, None, sibling),
            (7, self.from_left, None, sibling),
            (8, self.from_right, None, sibling),
            (9, self.from_far, None, sibling),
        ]

    def start_copies(self, *which):
        for k in which:
            self.copy(*self.table()[k]).start()

    def start(self):
        self.start_copies(6, 0, 3)

    def second(self):
        for k in (0, 3):
            self.copy(*self.table()[k]).wait_send()
        self.start_copies(1, 2)

    def arrived(self, *which):
        for k in which:
            _, slot, rows, device = self.table()[k]
            self.copy(k, slot, rows, device).wait_recv()

    def relay(self):
        self.arrived(0)
        self.start_copies(4)
        self.arrived(3)
        self.start_copies(5)

    def run(self, consume, fill=None, relayed=False):
        def step(i, carry):
            @pl.when(i == 1)
            def _():
                if not relayed:
                    self.second()
                self.arrived(6)

            @pl.when(i == 2)
            def _():
                if not relayed:
                    self.relay()
                if fill is not None:
                    fill()
                self.arrived(1)
                self.start_copies(7)

            @pl.when(i == 3)
            def _():
                self.arrived(2)
                self.start_copies(8)

            @pl.when(i == 4)
            def _():
                self.arrived(7)

            @pl.when(i == 5)
            def _():
                self.arrived(8)

            @pl.when(i == 6)
            def _():
                self.arrived(4, 5)
                self.start_copies(9)

            @pl.when(i == 7)
            def _():
                self.arrived(9)

            consume(slot_at(self.me, i))
            return carry

        lax.fori_loop(0, MEMBERS, step, 0)

    def end(self):
        for row in self.table():
            if row[0] not in (0, 3):
                self.copy(*row).wait_send()


GATHER_SEMS = [pltpu.SemaphoreType.DMA((10,)), pltpu.SemaphoreType.DMA((10,))]

SUM_SEND = [
    pltpu.VMEM((4, PAD, D), BF16),
    pltpu.VMEM((3, PAD, D), BF16),
    pltpu.VMEM((PAD, D), F32),
    pltpu.VMEM((2, HALF, D), F32),
]
SUM_LAND = [
    pltpu.VMEM((4, PAD, D), BF16),
    pltpu.VMEM((PAD, D), BF16),
    pltpu.VMEM((2, PAD, D), BF16),
    pltpu.SemaphoreType.DMA((4,)),
    pltpu.SemaphoreType.DMA((4,)),
    pltpu.SemaphoreType.DMA((6,)),
    pltpu.SemaphoreType.DMA((6,)),
]


def sum_rows(me, produce, send_bufs, land_bufs, fill=None):
    s1, s2, acc, hold = send_bufs
    r1, ra, rb, ss1, rs1, ss2, rs2 = land_bufs
    sibling = me.sibling()
    right, left = me.peer(me.core, (me.x + 1) % 4), me.peer(me.core, (me.x + 3) % 4)

    def chip(i):
        return (me.x + 2 + (i == 1).astype(jnp.int32) * 3 + (i == 2).astype(jnp.int32) + (i == 3).astype(jnp.int32) * 2) % 4

    def to_sibling(i):
        return remote(s1.at[i], r1.at[i], ss1.at[i], rs1.at[i], sibling)

    def along(k):
        src, dst, device = (
            (s2.at[0, TOP], ra.at[TOP], right),
            (s2.at[0, BOTTOM], ra.at[BOTTOM], left),
            (s2.at[1, BOTTOM], rb.at[0, BOTTOM], right),
            (s2.at[2, TOP], rb.at[1, TOP], left),
            (s2.at[1, TOP], rb.at[0, TOP], right),
            (s2.at[2, BOTTOM], rb.at[1, BOTTOM], left),
        )[k]
        return remote(src, dst, ss2.at[k], rs2.at[k], device)

    def for_sibling(i, carry):
        s1[i] = produce((1 - me.core) * 4 + chip(i)).astype(BF16)
        to_sibling(i).start()
        return carry

    def own(i, carry):
        part = produce(me.core * 4 + chip(i))
        to_sibling(i).wait_recv()
        acc[...] = part + r1[i].astype(F32)

        @pl.when(i == 0)
        def _():
            s2[0] = acc[...].astype(BF16)
            along(0).start()
            along(1).start()

        @pl.when(i == 1)
        def _():
            s2[1, BOTTOM] = acc[BOTTOM].astype(BF16)
            along(2).start()
            hold[0] = acc[TOP]

        @pl.when(i == 2)
        def _():
            s2[2, TOP] = acc[TOP].astype(BF16)
            along(3).start()
            hold[1] = acc[BOTTOM]

        @pl.when(i < 2)
        def _():
            for_sibling(i + 2, 0)

        return carry

    lax.fori_loop(0, 2, for_sibling, 0)
    lax.fori_loop(0, 4, own, 0)
    if fill is not None:
        fill()
    along(0).wait_recv()
    s2[1, TOP] = (hold[0] + ra[TOP].astype(F32)).astype(BF16)
    along(4).start()
    along(1).wait_recv()
    s2[2, BOTTOM] = (hold[1] + ra[BOTTOM].astype(F32)).astype(BF16)
    along(5).start()
    for k in range(2, 6):
        along(k).wait_recv()
    total = acc[...] + rb[0].astype(F32) + rb[1].astype(F32)
    for i in range(4):
        to_sibling(i).wait_send()
    for k in range(6):
        along(k).wait_send()
    return total


PLANE_SEMS = [pltpu.SemaphoreType.DMA((16,)), pltpu.SemaphoreType.DMA((16,))]


def weights_copy(me, i, shard, full, send, recv):
    pair, zlo = (me.pair + i // 2) % 8, (me.zlo + i) % 2
    device = {"dp": pair * 2 + me.zlo, "tensor": zlo * 4 + me.x}
    return remote(shard, full.at[me.dp], send.at[i], recv.at[me.dp], device)


def weights_start(me, shard, full, send, recv):
    def step(i, carry):
        weights_copy(me, i, shard, full, send, recv).start()
        return carry

    own = me.core == me.zlo

    @pl.when(own)
    def _():
        pltpu.make_async_copy(shard, full.at[me.dp], recv.at[me.dp]).start()

    @pl.when(jnp.logical_not(own))
    def _():
        weights_copy(me, 0, shard, full, send, recv).start()

    lax.fori_loop(1, 16, step, 0)


def weights_arrived(me, shard, full, send, recv):
    def step(i, carry):
        remote(shard, full.at[i], send.at[i], recv.at[i], me.sibling()).wait_recv()
        return carry

    lax.fori_loop(0, 16, step, 0)


def weights_sent(me, shard, full, send, recv):
    @pl.when(me.core != me.zlo)
    def _():
        weights_copy(me, 0, shard, full, send, recv).wait_send()

    def step(i, carry):
        weights_copy(me, i, shard, full, send, recv).wait_send()
        return carry

    lax.fori_loop(1, 16, step, 0)


def grads_copy(me, i, part, land, send, recv):
    to = (me.dp + i) % 16
    device = {"dp": to, "tensor": me.slot}
    return remote(part.at[to], land.at[me.group], send.at[i], recv.at[me.group], device)


def grads_start(me, part, land, send, recv):
    own = me.zlo == me.core

    @pl.when(own)
    def _():
        pltpu.make_async_copy(part.at[me.dp], land.at[me.group], recv.at[me.group]).start()

    @pl.when(jnp.logical_not(own))
    def _():
        grads_copy(me, 0, part, land, send, recv).start()

    def step(i, carry):
        grads_copy(me, i, part, land, send, recv).start()
        return carry

    lax.fori_loop(1, 16, step, 0)


def grads_end(me, part, land, send, recv, store):
    def arrived(i, carry):
        remote(part.at[0], land.at[i], send.at[i], recv.at[i], me.sibling()).wait_recv()
        return carry

    lax.fori_loop(0, 16, arrived, 0)

    @pl.when(me.zlo != me.core)
    def _():
        grads_copy(me, 0, part, land, send, recv).wait_send()

    def sent(i, carry):
        grads_copy(me, i, part, land, send, recv).wait_send()
        return carry

    lax.fori_loop(1, 16, sent, 0)
    total = land[0].astype(F32)
    for i in range(1, 16):
        total = total + land[i].astype(F32)
    store(total)


def normalized(rows):
    centred = rows - jnp.mean(rows, axis=-1, keepdims=True)
    scale = lax.rsqrt(jnp.mean(centred * centred, axis=-1, keepdims=True) + EPSILON)
    return centred * scale, scale


def layer_norm(rows, gain, shift):
    return normalized(rows)[0] * gain + shift


def layer_norm_back(rows, gain, grad):
    unit, scale = normalized(rows)
    inner = grad * gain
    mean_one = jnp.mean(inner, axis=-1, keepdims=True)
    mean_two = jnp.mean(inner * unit, axis=-1, keepdims=True)
    back = scale * (inner - mean_one - unit * mean_two)
    return back, jnp.sum(grad * unit, axis=0, keepdims=True), jnp.sum(grad, axis=0, keepdims=True)


def erf(v):
    v = jnp.clip(v, -4.0, 4.0)
    s = v * v
    top = F32(-2.72614225801306e-10)
    for a in (
        2.77068142495902e-08,
        -2.10102402082508e-06,
        -5.69250639462346e-05,
        -7.34990630326855e-04,
        -2.95459980854025e-03,
        -1.60960333262415e-02,
    ):
        top = top * s + F32(a)
    low = F32(-1.45660718464996e-05)
    for b in (
        -2.13374055278905e-04,
        -1.68282697438203e-03,
        -7.37332916720468e-03,
        -1.42647390514189e-02,
    ):
        low = low * s + F32(b)
    return v * top / low


def normal_below(v):
    return 0.5 * (1.0 + erf(v * F32(0.7071067811865476)))


def gelu_and_slope(v):
    below = normal_below(v)
    return v * below, below + v * jnp.exp(-0.5 * v * v) * F32(0.3989422804014327)


def weight_grad(left, right, out, at, width):
    def tile(i, carry):
        a = left[:, :, pl.ds(pl.multiple_of(i * 256, 256), 256)].reshape(MEMBERS * PAD, 256)
        b = right[...].reshape(MEMBERS * PAD, width)
        block = dot(a, b, TN).astype(BF16).reshape(4, 64, width)
        out[pl.ds(i * 4, 4), :, at : at + width] = block
        return carry

    lax.fori_loop(0, D // 256, tile, 0)


def columns(w, at, width):
    return w[:, :, at : at + width].reshape(D, width)


def column_sum(ref):
    def step(i, total):
        return total + jnp.sum(ref[i].astype(F32), axis=0, keepdims=True)

    return lax.fori_loop(0, MEMBERS, step, jnp.zeros((1, ref.shape[2]), F32))


def head_parts(qkv, i, at):
    return qkv[pl.ds(i * 4, 4), :, at * COLS : (at + 1) * COLS].reshape(4 * PAD, COLS)


def attend(qkv, mask, out):
    lane = lax.broadcasted_iota(jnp.int32, (1, COLS), 1)

    def image(i, carry):
        q, k, v = (head_parts(qkv, i, j) for j in range(3))
        q = q * BF16(HEAD**-0.5)
        valid = mask[i, 0:1] > 0.5
        total = None
        for h in range(2):
            mine = (lane >= h * HEAD) & (lane < (h + 1) * HEAD)
            scores = dot(jnp.where(mine, q, jnp.zeros_like(q)), k, NT)
            scores = jnp.where(valid, scores, NEG_FILL)
            e = jnp.exp(scores - jnp.max(scores, axis=-1, keepdims=True))
            prob = (e * (1.0 / jnp.sum(e, axis=-1, keepdims=True))).astype(BF16)
            mixed = dot(prob, v)
            total = mixed if total is None else jnp.where(mine, mixed, total)
        out[pl.ds(i * 4, 4)] = total.astype(BF16).reshape(4, PAD, COLS)
        return carry

    lax.fori_loop(0, 2, image, 0)


def attend_back(qkv, mask, grad):
    lane = lax.broadcasted_iota(jnp.int32, (1, COLS), 1)

    def image(i, carry):
        q, k, v = (head_parts(qkv, i, j) for j in range(3))
        q = q * BF16(HEAD**-0.5)
        g = grad[pl.ds(i * 4, 4)].reshape(4 * PAD, COLS)
        valid = mask[i].T[:, 0:1] > 0.5
        parts = [None, None, None]
        for h in range(2):
            mine = (lane >= h * HEAD) & (lane < (h + 1) * HEAD)
            scores = dot(k, jnp.where(mine, q, jnp.zeros_like(q)), NT)
            scores = jnp.where(valid, scores, NEG_FILL)
            e = jnp.exp(scores - jnp.max(scores, axis=0, keepdims=True))
            prob = e * (1.0 / jnp.sum(e, axis=0, keepdims=True))
            grad_value = dot(prob.astype(BF16), g)
            grad_prob = dot(v, jnp.where(mine, g, jnp.zeros_like(g)), NT)
            inner = jnp.sum(grad_prob * prob, axis=0, keepdims=True)
            grad_scores = (prob * (grad_prob - inner)).astype(BF16)
            grad_key = dot(grad_scores, q)
            grad_query = dot(grad_scores, k, TN) * F32(HEAD**-0.5)
            new = [grad_query, grad_key, grad_value]
            parts = new if h == 0 else [jnp.where(mine, n, p) for n, p in zip(new, parts)]
        for j in range(3):
            qkv[pl.ds(i * 4, 4), :, j * COLS : (j + 1) * COLS] = parts[j].astype(BF16).reshape(4, PAD, COLS)
        return carry

    lax.fori_loop(0, 2, image, 0)


def vectors_start(me, wide, va, vl, send, recv):
    for s in range(MEMBERS):
        va[s] = wide[:, s * 128 : (s + 1) * 128]

    def step(i, carry):
        core, x = (me.core + i // 4) % 2, (me.x + i) % 4
        remote(va.at[core * 4 + x], vl.at[i], send.at[i], recv.at[i], me.peer(core, x)).start()
        return carry

    lax.fori_loop(1, MEMBERS, step, 0)


def vectors_end(me, narrow, va, vl, send, recv, vb, piece, send2, recv2, out, send3, recv3):
    total = va[me.slot]
    for i in range(1, MEMBERS):
        remote(va.at[0], vl.at[i], send.at[i], recv.at[i], me.sibling()).wait()
        total = total + vl[i]
    piece[0:16] = total
    piece[16:32] = narrow[...]

    def to_group(i):
        pair, zlo = (me.pair + i // 2) % 8, (me.zlo + i) % 2
        device = {"dp": pair * 2 + me.core, "tensor": zlo * 4 + me.x}
        return remote(piece, vb.at[me.group], send2.at[i], recv2.at[me.group], device)

    def start(i, carry):
        to_group(i).start()
        return carry

    lax.fori_loop(1, 16, start, 0)
    vb[me.group] = piece[...]

    def end(i, carry):
        to_group(i).wait_send()
        group = (me.group + i) % 16
        remote(piece, vb.at[group], send2.at[i], recv2.at[group], me.sibling()).wait_recv()
        return carry

    lax.fori_loop(1, 16, end, 0)
    total = vb[0]
    for i in range(1, 16):
        total = total + vb[i]
    out[me.slot] = total
    own = out.at[me.slot]

    def to_member(i):
        core, x = (me.core + i // 4) % 2, (me.x + i) % 4
        return remote(own, own, send3.at[i], recv3.at[me.slot], me.peer(core, x))

    def start_three(i, carry):
        to_member(i).start()
        return carry

    lax.fori_loop(1, MEMBERS, start_three, 0)

    def end_three(i, carry):
        to_member(i).wait_send()
        slot = ((me.core + i // 4) % 2) * 4 + (me.x + i) % 4
        remote(own, out.at[slot], send3.at[i], recv3.at[slot], me.sibling()).wait_recv()
        return carry

    lax.fori_loop(1, MEMBERS, end_three, 0)


class Weights:
    def __init__(self, me, shard, full, send, recv):
        self.args, self.full = (me, shard, full, send, recv), full

    def start(self):
        weights_start(*self.args)

    def arrived(self):
        weights_arrived(*self.args)

    def sent(self):
        weights_sent(*self.args)


class Grads:
    def __init__(self, me, part, land, send, recv, out):
        self.args, self.part = (me, part, land, send, recv, out), part

    def start(self):
        grads_start(*self.args[:5])

    def end(self):
        grads_end(*self.args)


class Swap:
    def __init__(self, me, src, dst, sems, k):
        self.away = me.core != me.zlo
        self.src, self.dst = src, dst
        partner = {"dp": me.pair * 2 + me.zlo, "tensor": me.core * 4 + me.x}
        self.copy = remote(src, dst, sems[0].at[k], sems[1].at[k], partner)

    def start(self):
        @pl.when(self.away)
        def _():
            self.copy.start()

    def end(self):
        @pl.when(self.away)
        def _():
            self.copy.wait()

        @pl.when(jnp.logical_not(self.away))
        def _():
            self.dst[...] = self.src[...]


ROWS_ALL, ROWS_OWN, PART = (MEMBERS, PAD, D), (PAD, D), (16, 64, 512)
HID_ALL, ATT_ALL, QKV_ALL, SUMMED = (MEMBERS, PAD, HID), (MEMBERS, PAD, COLS), (MEMBERS, PAD, 384), (64, 512)
DMA = pltpu.SemaphoreType.DMA

INPUTS = ("x_in", "cot_in", "mask_in", "shards", "gain", "shift", "bias", "up_bias")
OUTPUTS = {
    "out_rows": ((ROWS, D), BF16),
    "gradient": ((ROWS, D), F32),
    "grad_qkv": ((2, 64, 3, COLS), F32),
    "grad_out": ((2, COLS, 64), F32),
    "grad_up": ((2, 64, HID), F32),
    "grad_down": ((2, HID, 64), F32),
    "grad_gain": ((2, 2, D), F32),
    "grad_shift": ((2, 2, D), F32),
    "grad_bias": ((2, 4, D), F32),
    "grad_up_bias": ((2, 4096), F32),
}


def scratch_table():
    table = {"padded": pltpu.VMEM(ROWS_OWN, F32)}

    def add(name, shape, dtype, count=None):
        if count is None:
            table[name] = pltpu.VMEM(shape, dtype)
        for i in range(count or 0):
            table[f"{name}{i}"] = pltpu.VMEM(shape, dtype)

    for name in ("x_own", "x_rows", "cot_own", "cot_rows", "rows_away", "rows_home"):
        add(name, ROWS_OWN, BF16)
    add("mask", (2, 8, 4 * PAD), F32)
    for name in ("qo", "up", "down", "land_qo", "land_up", "land_down"):
        add(name, PART, BF16, 2)
    for name in ("dw_qo", "dw_up", "dw_down"):
        add(name, PART, BF16)
    add("normed_one", ROWS_ALL, BF16, 2)
    add("normed_two", ROWS_ALL, BF16, 2)
    add("qkv", QKV_ALL, BF16, 2)
    add("attended", ATT_ALL, BF16, 2)
    add("slope", HID_ALL, BF16, 2)
    add("act", HID_ALL, BF16, 2)
    add("middle", ROWS_OWN, F32, 2)
    add("state", ROWS_OWN, F32)
    add("g_rows", ROWS_ALL, BF16)
    add("g_attn", ROWS_ALL, BF16)
    add("grad_att", ATT_ALL, BF16)
    add("grad_mid", ROWS_OWN, F32)
    add("grad", ROWS_OWN, F32)
    add("wide", (16, D), F32)
    add("narrow", (16, 128), F32)
    add("va", (MEMBERS, 16, 128), F32)
    add("vl", (MEMBERS, 16, 128), F32)
    add("vectors", (MEMBERS, 32, 128), F32)
    add("qbias", (2, 384), F32)
    add("vb", (16, 32, 128), F32)
    add("piece", (32, 128), F32)
    for i, spec in enumerate(SUM_SEND):
        table[f"sum_send{i}"] = spec
    for j in range(2):
        for i, spec in enumerate(SUM_LAND):
            table[f"sum_land{j}_{i}"] = spec
    for name, count in (("rows", 10), ("cot", 10), ("swap", 5), ("v1", 8), ("v2", 16), ("v3", 8)):
        table[name + "_send"], table[name + "_recv"] = DMA((count,)), DMA((count,))
    for name in ("w", "g"):
        table[name + "_send"], table[name + "_recv"] = DMA((6, 16)), DMA((6, 16))
    return table


def whole_kernel(*refs):
    table = scratch_table()
    names = [*INPUTS, *OUTPUTS, *table]
    b = types.SimpleNamespace(**dict(zip(names, refs, strict=True)))
    me = Place()

    def padded(rows, out):
        b.padded[0:ROWS] = rows[...].astype(F32)
        b.padded[ROWS:PAD] = jnp.zeros((PAD - ROWS, D), F32)
        out[...] = b.padded[...].astype(BF16)

    own_cols = pl.ds(pl.multiple_of(me.slot * COLS, COLS), COLS)
    own_hid = pl.ds(pl.multiple_of(me.slot * HID, HID), HID)

    def work():
        padded(b.x_in, b.x_own)
        padded(b.cot_in, b.cot_own)
        b.wide[...] = jnp.zeros_like(b.wide)
        b.narrow[...] = jnp.zeros_like(b.narrow)
        b.qbias[...] = jnp.zeros_like(b.qbias)
        for l in range(2):
            b.qbias[l : l + 1, 0:COLS] = b.bias[l, 0:1, own_cols]
            b.qbias[l : l + 1, 2 * COLS :] = b.bias[l, 1:2, own_cols]

    greet(me, work)

    def both(name):
        return getattr(b, name + "_send"), getattr(b, name + "_recv")

    def pair(name):
        return [getattr(b, name + "0"), getattr(b, name + "1")]

    cuts = {"qo": pl.ds(0, 512), "up": pl.ds(512, 512), "down": pl.ds(1024, 512)}
    weights, grads = {}, {}

    def store_qo(l):
        def store(total):
            for j in range(3):
                b.grad_qkv[l, :, j, :] = total[:, j * COLS : (j + 1) * COLS]
            b.grad_out[l] = total[:, 3 * COLS :].T

        return store

    def store_up(l):
        def store(total):
            b.grad_up[l] = total

        return store

    def store_down(l):
        def store(total):
            b.grad_down[l] = total.T

        return store

    stores = {"qo": store_qo, "up": store_up, "down": store_down}
    for n, name in enumerate(cuts):
        for l in range(2):
            k = n * 2 + l
            shard = b.shards.at[l, :, cuts[name]]
            weights[name, l] = Weights(me, shard, pair(name)[l], b.w_send.at[k], b.w_recv.at[k])
            part = getattr(b, "dw_" + name)
            land_part = pair("land_" + name)[l]
            grads[name, l] = Grads(me, part, land_part, b.g_send.at[k], b.g_recv.at[k], stores[name](l))
    send_bufs = [getattr(b, f"sum_send{i}") for i in range(len(SUM_SEND))]
    land = [[getattr(b, f"sum_land{j}_{i}") for i in range(len(SUM_LAND))] for j in range(2)]
    normed_one, normed_two, qkv, attended = (pair(n) for n in ("normed_one", "normed_two", "qkv", "attended"))
    slope, act, middle = (pair(n) for n in ("slope", "act", "middle"))

    swap_x = Swap(me, b.x_own, b.x_rows, both("swap"), 0)
    swap_x.start()
    swap_mask = Swap(me, b.mask_in, b.mask, both("swap"), 1)
    swap_mask.start()
    swap_cot = Swap(me, b.cot_own, b.cot_rows, both("swap"), 2)
    swap_x.end()
    weights["qo", 0].start()

    def norm_rows(rows, l, i, out):
        out[me.slot] = layer_norm(rows, b.gain[l, i : i + 1], b.shift[l, i : i + 1]).astype(BF16)

    def project(l):
        w = weights["qo", l].full

        def consume(slot):
            qkv[l][slot] = (dot(normed_one[l][slot], columns(w, 0, 384)) + b.qbias[l : l + 1]).astype(BF16)

        return consume

    def forward(l, state, before_up, before_down, after_up):
        attend(qkv[l], b.mask, attended[l])
        before_up()
        w = weights["qo", l].full

        def out_product(slot):
            return dot(attended[l][slot], columns(w, 384, 128), NT)

        branch = sum_rows(me, out_product, send_bufs, land[0])
        middle[l][...] = state() + (branch + b.bias[l, 2:3])
        norm_rows(middle[l][...], l, 1, normed_two[l])
        gather = Gather(me, normed_two[l], *both("rows"))
        gather.start()
        before_down()
        weights["up", l].arrived()

        def consume(slot):
            h = dot(normed_two[l][slot], columns(weights["up", l].full, 0, 512)) + b.up_bias[l : l + 1, own_hid]
            value, slant = gelu_and_slope(h)
            act[l][slot] = value.astype(BF16)
            slope[l][slot] = slant.astype(BF16)

        gather.run(consume)
        weights["down", l].arrived()
        after_up()

        def down_product(slot):
            return dot(act[l][slot], columns(weights["down", l].full, 0, 512), NT)

        total = sum_rows(me, down_product, send_bufs, land[1])
        gather.end()
        return middle[l][...] + (total + b.bias[l, 3:4])

    norm_rows(b.x_rows[...].astype(F32), 0, 0, normed_one[0])
    gather = Gather(me, normed_one[0], *both("rows"))
    gather.start()
    swap_mask.end()
    gather.second()
    gather.relay()
    weights["qo", 0].arrived()
    swap_cot.start()
    weights["up", 0].start()
    gather.run(project(0), relayed=True)
    gather.end()
    swap_cot.end()
    b.g_rows[me.slot] = b.cot_rows[...]
    gather_cot = Gather(me, b.g_rows, *both("cot"))
    gather_cot.start()

    def cot_second():
        gather_cot.second()
        weights["down", 0].start()

    b.state[...] = forward(
        0,
        lambda: b.x_rows[...].astype(F32),
        cot_second,
        nothing,
        weights["qo", 1].start,
    )
    norm_rows(b.state[...], 1, 0, normed_one[1])
    gather = Gather(me, normed_one[1], *both("rows"))
    gather.start()
    weights["qo", 1].arrived()
    weights["up", 1].start()
    gather.run(project(1))
    gather.end()
    gather_cot.relay()
    b.rows_away[...] = forward(1, lambda: b.state[...], weights["down", 1].start, nothing, nothing).astype(BF16)
    swap_out = Swap(me, b.rows_away, b.rows_home, both("swap"), 3)
    swap_out.start()

    def narrow_sum(ref, row, at, count):
        total = column_sum(ref)
        for i in range(count):
            b.narrow[row + i : row + i + 1] = total[:, (at + i) * 128 : (at + i + 1) * 128]

    def backward(l, g_own, gather_g, after_down, after_up):
        down, up, w = weights["down", l].full, weights["up", l].full, weights["qo", l].full

        def consume(slot):
            grad_act = dot(b.g_rows[slot], columns(down, 0, 512))
            slope[l][slot] = (grad_act * slope[l][slot].astype(F32)).astype(BF16)

        gather_g.run(consume, relayed=l == 1)
        grad_hid = slope[l]

        def up_back(slot):
            return dot(grad_hid[slot], columns(up, 0, 512), NT)

        def fill():
            weight_grad(b.g_rows, act[l], b.dw_down, 0, 512)
            grads["down", l].start()
            narrow_sum(grad_hid, l * 6 + 2, 0, 4)
            after_down()

        grad = sum_rows(me, up_back, send_bufs, land[0], fill)
        gather_g.end()
        back, gain_sum, shift_sum = layer_norm_back(middle[l][...], b.gain[l, 1:2], grad)
        mid = g_own() + back
        b.grad_mid[...] = mid
        b.g_attn[me.slot] = mid.astype(BF16)
        gather = Gather(me, b.g_attn, *both("rows"))
        gather.start()
        row = l * 6 + 2
        b.wide[row : row + 1] = jnp.sum(g_own(), axis=0, keepdims=True)
        b.wide[row + 1 : row + 2] = gain_sum
        b.wide[row + 2 : row + 3] = shift_sum
        b.wide[row + 3 : row + 4] = jnp.sum(mid, axis=0, keepdims=True)

        def fill_two():
            after_up()
            weight_grad(normed_two[l], grad_hid, b.dw_up, 0, 512)
            grads["up", l].start()

        def att_back(slot):
            b.grad_att[slot] = dot(b.g_attn[slot], columns(w, 384, 128)).astype(BF16)

        gather.run(att_back, fill_two)
        gather.end()
        attend_back(qkv[l], b.mask, b.grad_att)

    def first_back(l, rows, more):
        w, grad_qkv = weights["qo", l].full, qkv[l]

        def back_product(slot):
            return dot(grad_qkv[slot], columns(w, 0, 384), NT)

        def fill():
            weight_grad(normed_one[l], grad_qkv, b.dw_qo, 0, 384)
            weight_grad(b.g_attn, attended[l], b.dw_qo, 384, 128)
            grads["qo", l].start()
            more()
            total = column_sum(grad_qkv)
            b.narrow[l * 6 : l * 6 + 1] = total[:, 0:128]
            b.narrow[l * 6 + 1 : l * 6 + 2] = total[:, 256:384]

        grad = sum_rows(me, back_product, send_bufs, land[1], fill)
        back, gain_sum, shift_sum = layer_norm_back(rows(), b.gain[l, 0:1], grad)
        b.wide[l * 6 : l * 6 + 1] = gain_sum
        b.wide[l * 6 + 1 : l * 6 + 2] = shift_sum
        return b.grad_mid[...] + back

    backward(1, lambda: b.cot_rows[...].astype(F32), gather_cot, nothing, nothing)
    b.grad[...] = first_back(1, lambda: b.state[...], grads["down", 1].end)
    b.g_rows[me.slot] = b.grad[...].astype(BF16)
    gather_g = Gather(me, b.g_rows, *both("cot"))
    gather_g.start()
    swap_out.end()
    b.out_rows[...] = b.rows_home[...].astype(F32)[:ROWS].astype(BF16)
    backward(0, lambda: b.grad[...], gather_g, grads["up", 1].end, grads["qo", 1].end)
    b.grad[...] = first_back(0, lambda: b.x_rows[...].astype(F32), grads["down", 0].end)
    b.rows_away[...] = b.grad[...].astype(BF16)
    vectors_start(me, b.wide, b.va, b.vl, *both("v1"))
    swap_grad = Swap(me, b.rows_away, b.x_own, both("swap"), 4)
    swap_grad.start()
    for name in cuts:
        for l in range(2):
            weights[name, l].sent()
    grads["up", 0].end()
    vectors_end(me, b.narrow, b.va, b.vl, *both("v1"), b.vb, b.piece, *both("v2"), b.vectors, *both("v3"))
    for s in range(MEMBERS):
        cols = slice(s * COLS, (s + 1) * COLS)
        for l in range(2):
            for ref, at, row in (
                (b.grad_gain, 0, 0),
                (b.grad_shift, 0, 1),
                (b.grad_bias, 3, 2),
                (b.grad_gain, 1, 3),
                (b.grad_shift, 1, 4),
                (b.grad_bias, 2, 5),
                (b.grad_bias, 0, 16),
                (b.grad_bias, 1, 17),
            ):
                ref[l, at : at + 1, cols] = b.vectors[s, row + 6 * l : row + 6 * l + 1]
            for j in range(4):
                to = s * HID + j * COLS
                b.grad_up_bias[l : l + 1, to : to + COLS] = b.vectors[s, 18 + 6 * l + j : 19 + 6 * l + j]
    swap_grad.end()

    @pl.when(me.core == me.zlo)
    def _():
        b.gradient[...] = b.grad[...][:ROWS]

    @pl.when(me.core != me.zlo)
    def _():
        b.gradient[...] = b.x_own[...].astype(F32)[:ROWS]

    grads["qo", 0].end()


def nothing():
    pass


def per_device(
    x_in, valid_len, w_qkv, w_out, w_up, w_down, norm_gain, norm_shift, bias, up_bias, cotangent
):
    at = jnp.arange(4 * PAD)
    token = (at // PAD) * ROWS + at % PAD
    mask = (at % PAD < ROWS) & (token < valid_len[:, None])
    mask = jnp.broadcast_to(mask[:, None].astype(F32), (2, 8, 4 * PAD))
    shards = jnp.concatenate(
        [w_qkv.reshape(2, 64, 384), jnp.swapaxes(w_out, 1, 2), w_up, jnp.swapaxes(w_down, 1, 2)], axis=2
    )
    vmem = pl.BlockSpec(memory_space=pltpu.VMEM)
    return pl.pallas_call(
        whole_kernel,
        out_shape=[jax.ShapeDtypeStruct(s, t) for s, t in OUTPUTS.values()],
        in_specs=[vmem] * len(INPUTS),
        out_specs=[vmem] * len(OUTPUTS),
        scratch_shapes=list(scratch_table().values()),
        compiler_params=pltpu.CompilerParams(
            collective_id=0, has_side_effects=True, vmem_limit_bytes=VMEM_BYTES
        ),
    )(x_in, cotangent, mask, shards, norm_gain, norm_shift, bias, up_bias)


def solution(mesh):
    rows = P(("dp", "tensor"), None)
    weights = (P(None, "dp", None, "tensor"), P(None, "tensor", "dp"), P(None, "dp", "tensor"), P(None, "tensor", "dp"))
    return jax.shard_map(
        per_device,
        mesh=mesh,
        in_specs=(rows, P("dp"), *weights, P(), P(), P(), P(), rows),
        out_specs=(rows, rows, *weights, P(), P(), P(), P()),
        check_vma=False,
    )
```

```python
import types

import jax
import jax.numpy as jnp
from jax import lax
from jax.experimental import pallas as pl
from jax.experimental.pallas import tpu as pltpu
from jax.sharding import PartitionSpec as P

MESH = pl.DeviceIdType.MESH
F32, BF16 = jnp.float32, jnp.bfloat16

D = 1024
ROWS = 146
PAD = 160
COLS = 128
HEAD = 64
HID = 512
MEMBERS = 8
WCOLS = 1536
EPSILON = 1e-06
NEG_FILL = -1e30
VMEM_BYTES = 64 * 1024 * 1024 - 65536

NN = (((1,), (0,)), ((), ()))
NT = (((1,), (1,)), ((), ()))
TN = (((0,), (0,)), ((), ()))


def dot(a, b, dims=NN):
    return lax.dot_general(a, b, dims, preferred_element_type=F32)


class Place:
    def __init__(self):
        self.dp = lax.axis_index("dp")
        self.tensor = lax.axis_index("tensor")
        self.core = self.dp % 2
        self.pair = self.dp // 2
        self.zlo = self.tensor // 4
        self.x = self.tensor % 4
        self.slot = self.core * 4 + self.x
        self.group = self.pair * 2 + self.zlo

    def peer(self, core, x):
        return {"dp": self.pair * 2 + core, "tensor": self.zlo * 4 + x}

    def sibling(self):
        return self.peer(1 - self.core, self.x)


def greet(me, work):
    barrier = pltpu.get_barrier_semaphore()

    def member(i, carry):
        pl.semaphore_signal(
            barrier,
            inc=1,
            device_id=me.peer((me.core + i // 4) % 2, (me.x + i) % 4),
            device_id_type=MESH,
        )
        return carry

    lax.fori_loop(1, MEMBERS, member, 0)

    def other(i, carry):
        pair = (me.pair + i // 4) % 8
        zlo = (me.zlo + (i // 2) % 2) % 2
        pl.semaphore_signal(
            barrier,
            inc=1,
            device_id={"dp": pair * 2 + i % 2, "tensor": zlo * 4 + me.x},
            device_id_type=MESH,
        )
        return carry

    lax.fori_loop(2, 32, other, 0)
    work()
    pl.semaphore_wait(barrier, MEMBERS - 1 + 30)


def remote(src, dst, send, recv, device):
    return pltpu.make_async_remote_copy(
        src_ref=src,
        dst_ref=dst,
        send_sem=send,
        recv_sem=recv,
        device_id=device,
        device_id_type=MESH,
    )


def slot_at(me, i):
    sibling = (i == 1) | (i == 4) | (i == 5) | (i == 7)
    far = (i >= 6).astype(jnp.int32) * 2
    left = ((i == 2) | (i == 4)).astype(jnp.int32) * 3
    right = ((i == 3) | (i == 5)).astype(jnp.int32)
    core = (me.core + sibling.astype(jnp.int32)) % 2
    return core * 4 + (me.x + far + left + right) % 4


HALF = PAD // 2
TOP, BOTTOM = pl.ds(0, HALF), pl.ds(HALF, HALF)


class Gather:
    def __init__(self, me, g, send, recv):
        self.me, self.g, self.send, self.recv = me, g, send, recv
        self.right = me.peer(me.core, (me.x + 1) % 4)
        self.left = me.peer(me.core, (me.x + 3) % 4)
        self.from_left = me.core * 4 + (me.x + 3) % 4
        self.from_right = me.core * 4 + (me.x + 1) % 4
        self.from_far = me.core * 4 + (me.x + 2) % 4

    def copy(self, k, slot, rows, device):
        block = self.g.at[slot] if rows is None else self.g.at[slot, rows]
        return remote(block, block, self.send.at[k], self.recv.at[k], device)

    def table(self):
        me = self.me
        sibling = me.sibling()
        return [
            (0, me.slot, TOP, self.right),
            (1, me.slot, BOTTOM, self.right),
            (2, me.slot, TOP, self.left),
            (3, me.slot, BOTTOM, self.left),
            (4, self.from_left, TOP, self.right),
            (5, self.from_right, BOTTOM, self.left),
            (6, me.slot, None, sibling),
            (7, self.from_left, None, sibling),
            (8, self.from_right, None, sibling),
            (9, self.from_far, None, sibling),
        ]

    def start_copies(self, *which):
        for k in which:
            self.copy(*self.table()[k]).start()

    def start(self):
        self.start_copies(6, 0, 3, 1, 2)

    def arrived(self, *which):
        for k in which:
            _, slot, rows, device = self.table()[k]
            self.copy(k, slot, rows, device).wait_recv()

    def relay(self):
        self.arrived(0)
        self.start_copies(4)
        self.arrived(3)
        self.start_copies(5)

    def run(self, consume, fill=None, relayed=False):
        def step(i, carry):
            @pl.when(i == 1)
            def _():
                self.arrived(6)

            @pl.when(i == 2)
            def _():
                if not relayed:
                    self.relay()
                if fill is not None:
                    fill()
                self.arrived(1)
                self.start_copies(7)

            @pl.when(i == 3)
            def _():
                self.arrived(2)
                self.start_copies(8)

            @pl.when(i == 4)
            def _():
                self.arrived(7)

            @pl.when(i == 5)
            def _():
                self.arrived(8)

            @pl.when(i == 6)
            def _():
                self.arrived(4, 5)
                self.start_copies(9)

            @pl.when(i == 7)
            def _():
                self.arrived(9)

            consume(slot_at(self.me, i))
            return carry

        lax.fori_loop(0, MEMBERS, step, 0)

    def end(self):
        for row in self.table():
            self.copy(*row).wait_send()


GATHER_SEMS = [pltpu.SemaphoreType.DMA((10,)), pltpu.SemaphoreType.DMA((10,))]

SUM_SEND = [
    pltpu.VMEM((4, PAD, D), BF16),
    pltpu.VMEM((3, PAD, D), BF16),
    pltpu.VMEM((PAD, D), F32),
    pltpu.VMEM((2, HALF, D), F32),
]
SUM_LAND = [
    pltpu.VMEM((4, PAD, D), BF16),
    pltpu.VMEM((PAD, D), BF16),
    pltpu.VMEM((2, PAD, D), BF16),
    pltpu.SemaphoreType.DMA((4,)),
    pltpu.SemaphoreType.DMA((4,)),
    pltpu.SemaphoreType.DMA((6,)),
    pltpu.SemaphoreType.DMA((6,)),
]


def sum_rows(me, produce, send_bufs, land_bufs, fill=None):
    s1, s2, acc, hold = send_bufs
    r1, ra, rb, ss1, rs1, ss2, rs2 = land_bufs
    sibling = me.sibling()
    right, left = me.peer(me.core, (me.x + 1) % 4), me.peer(me.core, (me.x + 3) % 4)

    def chip(i):
        return (me.x + 2 + (i == 1).astype(jnp.int32) * 3 + (i == 2).astype(jnp.int32) + (i == 3).astype(jnp.int32) * 2) % 4

    def to_sibling(i):
        return remote(s1.at[i], r1.at[i], ss1.at[i], rs1.at[i], sibling)

    def along(k):
        src, dst, device = (
            (s2.at[0, TOP], ra.at[TOP], right),
            (s2.at[0, BOTTOM], ra.at[BOTTOM], left),
            (s2.at[1, BOTTOM], rb.at[0, BOTTOM], right),
            (s2.at[2, TOP], rb.at[1, TOP], left),
            (s2.at[1, TOP], rb.at[0, TOP], right),
            (s2.at[2, BOTTOM], rb.at[1, BOTTOM], left),
        )[k]
        return remote(src, dst, ss2.at[k], rs2.at[k], device)

    def for_sibling(i, carry):
        s1[i] = produce((1 - me.core) * 4 + chip(i)).astype(BF16)
        to_sibling(i).start()
        return carry

    def own(i, carry):
        part = produce(me.core * 4 + chip(i))
        to_sibling(i).wait_recv()
        acc[...] = part + r1[i].astype(F32)

        @pl.when(i == 0)
        def _():
            s2[0] = acc[...].astype(BF16)
            along(0).start()
            along(1).start()

        @pl.when(i == 1)
        def _():
            s2[1, BOTTOM] = acc[BOTTOM].astype(BF16)
            along(2).start()
            hold[0] = acc[TOP]

        @pl.when(i == 2)
        def _():
            s2[2, TOP] = acc[TOP].astype(BF16)
            along(3).start()
            hold[1] = acc[BOTTOM]

        @pl.when(i < 2)
        def _():
            for_sibling(i + 2, 0)

        return carry

    lax.fori_loop(0, 2, for_sibling, 0)
    lax.fori_loop(0, 4, own, 0)
    if fill is not None:
        fill()
    along(0).wait_recv()
    s2[1, TOP] = (hold[0] + ra[TOP].astype(F32)).astype(BF16)
    along(4).start()
    along(1).wait_recv()
    s2[2, BOTTOM] = (hold[1] + ra[BOTTOM].astype(F32)).astype(BF16)
    along(5).start()
    for k in range(2, 6):
        along(k).wait_recv()
    total = acc[...] + rb[0].astype(F32) + rb[1].astype(F32)
    for i in range(4):
        to_sibling(i).wait_send()
    for k in range(6):
        along(k).wait_send()
    return total


PLANE_SEMS = [pltpu.SemaphoreType.DMA((16,)), pltpu.SemaphoreType.DMA((16,))]


def weights_copy(me, i, shard, full, send, recv):
    pair, zlo = (me.pair + i // 2) % 8, (me.zlo + i) % 2
    device = {"dp": pair * 2 + me.zlo, "tensor": zlo * 4 + me.x}
    return remote(shard, full.at[me.dp], send.at[i], recv.at[me.dp], device)


def weights_start(me, shard, full, send, recv):
    def step(i, carry):
        weights_copy(me, i, shard, full, send, recv).start()
        return carry

    own = me.core == me.zlo

    @pl.when(own)
    def _():
        pltpu.make_async_copy(shard, full.at[me.dp], recv.at[me.dp]).start()

    @pl.when(jnp.logical_not(own))
    def _():
        weights_copy(me, 0, shard, full, send, recv).start()

    lax.fori_loop(1, 16, step, 0)


def weights_arrived(me, shard, full, send, recv):
    def step(i, carry):
        remote(shard, full.at[i], send.at[i], recv.at[i], me.sibling()).wait_recv()
        return carry

    lax.fori_loop(0, 16, step, 0)


def weights_sent(me, shard, full, send, recv):
    @pl.when(me.core != me.zlo)
    def _():
        weights_copy(me, 0, shard, full, send, recv).wait_send()

    def step(i, carry):
        weights_copy(me, i, shard, full, send, recv).wait_send()
        return carry

    lax.fori_loop(1, 16, step, 0)


def grads_copy(me, i, part, land, send, recv):
    to = (me.dp + i) % 16
    device = {"dp": to, "tensor": me.slot}
    return remote(part.at[to], land.at[me.group], send.at[i], recv.at[me.group], device)


def grads_start(me, part, land, send, recv):
    own = me.zlo == me.core

    @pl.when(own)
    def _():
        pltpu.make_async_copy(part.at[me.dp], land.at[me.group], recv.at[me.group]).start()

    @pl.when(jnp.logical_not(own))
    def _():
        grads_copy(me, 0, part, land, send, recv).start()

    def step(i, carry):
        grads_copy(me, i, part, land, send, recv).start()
        return carry

    lax.fori_loop(1, 16, step, 0)


def grads_end(me, part, land, send, recv, store):
    def arrived(i, carry):
        remote(part.at[0], land.at[i], send.at[i], recv.at[i], me.sibling()).wait_recv()
        return carry

    lax.fori_loop(0, 16, arrived, 0)

    @pl.when(me.zlo != me.core)
    def _():
        grads_copy(me, 0, part, land, send, recv).wait_send()

    def sent(i, carry):
        grads_copy(me, i, part, land, send, recv).wait_send()
        return carry

    lax.fori_loop(1, 16, sent, 0)
    total = land[0].astype(F32)
    for i in range(1, 16):
        total = total + land[i].astype(F32)
    store(total)


def normalized(rows):
    centred = rows - jnp.mean(rows, axis=-1, keepdims=True)
    scale = lax.rsqrt(jnp.mean(centred * centred, axis=-1, keepdims=True) + EPSILON)
    return centred * scale, scale


def layer_norm(rows, gain, shift):
    return normalized(rows)[0] * gain + shift


def layer_norm_back(rows, gain, grad):
    unit, scale = normalized(rows)
    inner = grad * gain
    mean_one = jnp.mean(inner, axis=-1, keepdims=True)
    mean_two = jnp.mean(inner * unit, axis=-1, keepdims=True)
    back = scale * (inner - mean_one - unit * mean_two)
    return back, jnp.sum(grad * unit, axis=0, keepdims=True), jnp.sum(grad, axis=0, keepdims=True)


def erf(v):
    v = jnp.clip(v, -4.0, 4.0)
    s = v * v
    top = F32(-2.72614225801306e-10)
    for a in (
        2.77068142495902e-08,
        -2.10102402082508e-06,
        -5.69250639462346e-05,
        -7.34990630326855e-04,
        -2.95459980854025e-03,
        -1.60960333262415e-02,
    ):
        top = top * s + F32(a)
    low = F32(-1.45660718464996e-05)
    for b in (
        -2.13374055278905e-04,
        -1.68282697438203e-03,
        -7.37332916720468e-03,
        -1.42647390514189e-02,
    ):
        low = low * s + F32(b)
    return v * top / low


def normal_below(v):
    return 0.5 * (1.0 + erf(v * F32(0.7071067811865476)))


def gelu_and_slope(v):
    below = normal_below(v)
    return v * below, below + v * jnp.exp(-0.5 * v * v) * F32(0.3989422804014327)


def weight_grad(left, right, out, at, width):
    def tile(i, carry):
        a = left[:, :, pl.ds(pl.multiple_of(i * 256, 256), 256)].reshape(MEMBERS * PAD, 256)
        b = right[...].reshape(MEMBERS * PAD, width)
        block = dot(a, b, TN).astype(BF16).reshape(4, 64, width)
        out[pl.ds(i * 4, 4), :, at : at + width] = block
        return carry

    lax.fori_loop(0, D // 256, tile, 0)


def columns(w, at, width):
    return w[:, :, at : at + width].reshape(D, width)


def column_sum(ref):
    def step(i, total):
        return total + jnp.sum(ref[i].astype(F32), axis=0, keepdims=True)

    return lax.fori_loop(0, MEMBERS, step, jnp.zeros((1, ref.shape[2]), F32))


def head_parts(qkv, i, at):
    return qkv[pl.ds(i * 4, 4), :, at * COLS : (at + 1) * COLS].reshape(4 * PAD, COLS)


def attend(qkv, mask, out):
    lane = lax.broadcasted_iota(jnp.int32, (1, COLS), 1)

    def image(i, carry):
        q, k, v = (head_parts(qkv, i, j) for j in range(3))
        q = q * BF16(HEAD**-0.5)
        valid = mask[i, 0:1] > 0.5
        total = None
        for h in range(2):
            mine = (lane >= h * HEAD) & (lane < (h + 1) * HEAD)
            scores = dot(jnp.where(mine, q, jnp.zeros_like(q)), k, NT)
            scores = jnp.where(valid, scores, NEG_FILL)
            e = jnp.exp(scores - jnp.max(scores, axis=-1, keepdims=True))
            prob = (e * (1.0 / jnp.sum(e, axis=-1, keepdims=True))).astype(BF16)
            mixed = dot(prob, v)
            total = mixed if total is None else jnp.where(mine, mixed, total)
        out[pl.ds(i * 4, 4)] = total.astype(BF16).reshape(4, PAD, COLS)
        return carry

    lax.fori_loop(0, 2, image, 0)


def attend_back(qkv, mask, grad):
    lane = lax.broadcasted_iota(jnp.int32, (1, COLS), 1)

    def image(i, carry):
        q, k, v = (head_parts(qkv, i, j) for j in range(3))
        q = q * BF16(HEAD**-0.5)
        g = grad[pl.ds(i * 4, 4)].reshape(4 * PAD, COLS)
        valid = mask[i].T[:, 0:1] > 0.5
        parts = [None, None, None]
        for h in range(2):
            mine = (lane >= h * HEAD) & (lane < (h + 1) * HEAD)
            scores = dot(k, jnp.where(mine, q, jnp.zeros_like(q)), NT)
            scores = jnp.where(valid, scores, NEG_FILL)
            e = jnp.exp(scores - jnp.max(scores, axis=0, keepdims=True))
            prob = e * (1.0 / jnp.sum(e, axis=0, keepdims=True))
            grad_value = dot(prob.astype(BF16), g)
            grad_prob = dot(v, jnp.where(mine, g, jnp.zeros_like(g)), NT)
            inner = jnp.sum(grad_prob * prob, axis=0, keepdims=True)
            grad_scores = (prob * (grad_prob - inner)).astype(BF16)
            grad_key = dot(grad_scores, q)
            grad_query = dot(grad_scores, k, TN) * F32(HEAD**-0.5)
            new = [grad_query, grad_key, grad_value]
            parts = new if h == 0 else [jnp.where(mine, n, p) for n, p in zip(new, parts)]
        for j in range(3):
            qkv[pl.ds(i * 4, 4), :, j * COLS : (j + 1) * COLS] = parts[j].astype(BF16).reshape(4, PAD, COLS)
        return carry

    lax.fori_loop(0, 2, image, 0)


def vectors_start(me, wide, va, vl, send, recv):
    for s in range(MEMBERS):
        va[s] = wide[:, s * 128 : (s + 1) * 128]

    def step(i, carry):
        core, x = (me.core + i // 4) % 2, (me.x + i) % 4
        remote(va.at[core * 4 + x], vl.at[i], send.at[i], recv.at[i], me.peer(core, x)).start()
        return carry

    lax.fori_loop(1, MEMBERS, step, 0)


def vectors_end(me, narrow, va, vl, send, recv, vb, piece, send2, recv2, out, send3, recv3):
    total = va[me.slot]
    for i in range(1, MEMBERS):
        remote(va.at[0], vl.at[i], send.at[i], recv.at[i], me.sibling()).wait()
        total = total + vl[i]
    piece[0:16] = total
    piece[16:32] = narrow[...]

    def to_group(i):
        pair, zlo = (me.pair + i // 2) % 8, (me.zlo + i) % 2
        device = {"dp": pair * 2 + me.core, "tensor": zlo * 4 + me.x}
        return remote(piece, vb.at[me.group], send2.at[i], recv2.at[me.group], device)

    def start(i, carry):
        to_group(i).start()
        return carry

    lax.fori_loop(1, 16, start, 0)
    vb[me.group] = piece[...]

    def end(i, carry):
        to_group(i).wait_send()
        group = (me.group + i) % 16
        remote(piece, vb.at[group], send2.at[i], recv2.at[group], me.sibling()).wait_recv()
        return carry

    lax.fori_loop(1, 16, end, 0)
    total = vb[0]
    for i in range(1, 16):
        total = total + vb[i]
    out[me.slot] = total
    own = out.at[me.slot]

    def to_member(i):
        core, x = (me.core + i // 4) % 2, (me.x + i) % 4
        return remote(own, own, send3.at[i], recv3.at[me.slot], me.peer(core, x))

    def start_three(i, carry):
        to_member(i).start()
        return carry

    lax.fori_loop(1, MEMBERS, start_three, 0)

    def end_three(i, carry):
        to_member(i).wait_send()
        slot = ((me.core + i // 4) % 2) * 4 + (me.x + i) % 4
        remote(own, out.at[slot], send3.at[i], recv3.at[slot], me.sibling()).wait_recv()
        return carry

    lax.fori_loop(1, MEMBERS, end_three, 0)


class Weights:
    def __init__(self, me, shard, full, send, recv):
        self.args, self.full = (me, shard, full, send, recv), full

    def start(self):
        weights_start(*self.args)

    def arrived(self):
        weights_arrived(*self.args)

    def sent(self):
        weights_sent(*self.args)


class Grads:
    def __init__(self, me, part, land, send, recv, out):
        self.args, self.part = (me, part, land, send, recv, out), part

    def start(self):
        grads_start(*self.args[:5])

    def end(self):
        grads_end(*self.args)


class Swap:
    def __init__(self, me, src, dst, sems, k):
        self.away = me.core != me.zlo
        self.src, self.dst = src, dst
        partner = {"dp": me.pair * 2 + me.zlo, "tensor": me.core * 4 + me.x}
        self.copy = remote(src, dst, sems[0].at[k], sems[1].at[k], partner)

    def start(self):
        @pl.when(self.away)
        def _():
            self.copy.start()

    def end(self):
        @pl.when(self.away)
        def _():
            self.copy.wait()

        @pl.when(jnp.logical_not(self.away))
        def _():
            self.dst[...] = self.src[...]


ROWS_ALL, ROWS_OWN, PART = (MEMBERS, PAD, D), (PAD, D), (16, 64, 512)
HID_ALL, ATT_ALL, QKV_ALL, SUMMED = (MEMBERS, PAD, HID), (MEMBERS, PAD, COLS), (MEMBERS, PAD, 384), (64, 512)
DMA = pltpu.SemaphoreType.DMA

INPUTS = ("x_in", "cot_in", "mask_in", "shards", "gain", "shift", "bias", "up_bias")
OUTPUTS = {
    "out_rows": (ROWS_OWN, BF16),
    "gradient": (ROWS_OWN, F32),
    "sum_qo": ((2, *SUMMED), F32),
    "sum_up": ((2, *SUMMED), F32),
    "sum_down": ((2, *SUMMED), F32),
    "vectors": ((MEMBERS, 32, 128), F32),
}
RESULTS = {
    "out_rows": ((ROWS, D), BF16),
    "gradient": ((ROWS, D), F32),
    "grad_qkv": ((2, 3, 64, COLS), F32),
    "grad_out": ((2, 64, COLS), F32),
    "grad_up": ((2, 64, HID), F32),
    "grad_down": ((2, 64, HID), F32),
    "grad_gain": ((2, 2, D), F32),
    "grad_shift": ((2, 2, D), F32),
    "grad_bias": ((2, 4, D), F32),
    "grad_up_bias": ((2, 4096), F32),
}


def result_kernel(*refs):
    b = types.SimpleNamespace(**dict(zip([*["in_" + n for n in OUTPUTS], *RESULTS], refs, strict=True)))
    b.out_rows[...] = b.in_out_rows[...].astype(F32)[:ROWS].astype(BF16)
    b.gradient[...] = b.in_gradient[...][:ROWS]
    for j in range(3):
        b.grad_qkv[:, j] = b.in_sum_qo[:, :, j * COLS : (j + 1) * COLS]
    b.grad_out[...] = b.in_sum_qo[:, :, 3 * COLS :]
    b.grad_up[...] = b.in_sum_up[...]
    b.grad_down[...] = b.in_sum_down[...]
    for s in range(MEMBERS):
        cols = slice(s * COLS, (s + 1) * COLS)
        for l in range(2):
            for ref, at, row in (
                (b.grad_gain, 0, 0),
                (b.grad_shift, 0, 1),
                (b.grad_bias, 3, 2),
                (b.grad_gain, 1, 3),
                (b.grad_shift, 1, 4),
                (b.grad_bias, 2, 5),
                (b.grad_bias, 0, 16),
                (b.grad_bias, 1, 17),
            ):
                ref[l, at : at + 1, cols] = b.in_vectors[s, row + 6 * l : row + 6 * l + 1]
            for j in range(4):
                to = s * HID + j * COLS
                b.grad_up_bias[l : l + 1, to : to + COLS] = b.in_vectors[s, 18 + 6 * l + j : 19 + 6 * l + j]


def scratch_table():
    table = {"padded": pltpu.VMEM(ROWS_OWN, F32)}

    def add(name, shape, dtype, count=None):
        if count is None:
            table[name] = pltpu.VMEM(shape, dtype)
        for i in range(count or 0):
            table[f"{name}{i}"] = pltpu.VMEM(shape, dtype)

    for name in ("x_own", "x_rows", "cot_own", "cot_rows", "rows_away", "rows_home"):
        add(name, ROWS_OWN, BF16)
    add("mask", (2, 8, 4 * PAD), F32)
    for name in ("qo", "up", "down", "land_qo", "land_up", "land_down"):
        add(name, PART, BF16, 2)
    for name in ("dw_qo", "dw_up", "dw_down"):
        add(name, PART, BF16)
    add("normed_one", ROWS_ALL, BF16, 2)
    add("normed_two", ROWS_ALL, BF16, 2)
    add("qkv", QKV_ALL, BF16, 2)
    add("attended", ATT_ALL, BF16, 2)
    add("slope", HID_ALL, BF16, 2)
    add("act", HID_ALL, BF16, 2)
    add("middle", ROWS_OWN, F32, 2)
    add("state", ROWS_OWN, F32)
    add("g_rows", ROWS_ALL, BF16)
    add("g_attn", ROWS_ALL, BF16)
    add("grad_att", ATT_ALL, BF16)
    add("grad_mid", ROWS_OWN, F32)
    add("grad", ROWS_OWN, F32)
    add("wide", (16, D), F32)
    add("narrow", (16, 128), F32)
    add("va", (MEMBERS, 16, 128), F32)
    add("vl", (MEMBERS, 16, 128), F32)
    add("qbias", (2, 384), F32)
    add("vb", (16, 32, 128), F32)
    add("piece", (32, 128), F32)
    for i, spec in enumerate(SUM_SEND):
        table[f"sum_send{i}"] = spec
    for j in range(2):
        for i, spec in enumerate(SUM_LAND):
            table[f"sum_land{j}_{i}"] = spec
    for name, count in (("rows", 10), ("cot", 10), ("swap", 5), ("v1", 8), ("v2", 16), ("v3", 8)):
        table[name + "_send"], table[name + "_recv"] = DMA((count,)), DMA((count,))
    for name in ("w", "g"):
        table[name + "_send"], table[name + "_recv"] = DMA((6, 16)), DMA((6, 16))
    return table


def whole_kernel(*refs):
    table = scratch_table()
    names = [*INPUTS, *OUTPUTS, *table]
    b = types.SimpleNamespace(**dict(zip(names, refs, strict=True)))
    me = Place()

    def padded(rows, out):
        b.padded[0:ROWS] = rows[...].astype(F32)
        b.padded[ROWS:PAD] = jnp.zeros((PAD - ROWS, D), F32)
        out[...] = b.padded[...].astype(BF16)

    own_cols = pl.ds(pl.multiple_of(me.slot * COLS, COLS), COLS)
    own_hid = pl.ds(pl.multiple_of(me.slot * HID, HID), HID)

    def work():
        padded(b.x_in, b.x_own)
        padded(b.cot_in, b.cot_own)
        b.wide[...] = jnp.zeros_like(b.wide)
        b.narrow[...] = jnp.zeros_like(b.narrow)
        b.qbias[...] = jnp.zeros_like(b.qbias)
        for l in range(2):
            b.qbias[l : l + 1, 0:COLS] = b.bias[l, 0:1, own_cols]
            b.qbias[l : l + 1, 2 * COLS :] = b.bias[l, 1:2, own_cols]

    greet(me, work)

    def both(name):
        return getattr(b, name + "_send"), getattr(b, name + "_recv")

    def pair(name):
        return [getattr(b, name + "0"), getattr(b, name + "1")]

    cuts = {"qo": pl.ds(0, 512), "up": pl.ds(512, 512), "down": pl.ds(1024, 512)}
    weights, grads = {}, {}

    def store_qo(l):
        def store(total):
            b.sum_qo[l] = total

        return store

    def store_up(l):
        def store(total):
            b.sum_up[l] = total

        return store

    def store_down(l):
        def store(total):
            b.sum_down[l] = total

        return store

    stores = {"qo": store_qo, "up": store_up, "down": store_down}
    for n, name in enumerate(cuts):
        for l in range(2):
            k = n * 2 + l
            shard = b.shards.at[l, :, cuts[name]]
            weights[name, l] = Weights(me, shard, pair(name)[l], b.w_send.at[k], b.w_recv.at[k])
            part = getattr(b, "dw_" + name)
            land_part = pair("land_" + name)[l]
            grads[name, l] = Grads(me, part, land_part, b.g_send.at[k], b.g_recv.at[k], stores[name](l))
    send_bufs = [getattr(b, f"sum_send{i}") for i in range(len(SUM_SEND))]
    land = [[getattr(b, f"sum_land{j}_{i}") for i in range(len(SUM_LAND))] for j in range(2)]
    normed_one, normed_two, qkv, attended = (pair(n) for n in ("normed_one", "normed_two", "qkv", "attended"))
    slope, act, middle = (pair(n) for n in ("slope", "act", "middle"))

    weights["qo", 0].start()
    swap_x = Swap(me, b.x_own, b.x_rows, both("swap"), 0)
    swap_x.start()
    swap_mask = Swap(me, b.mask_in, b.mask, both("swap"), 1)
    swap_mask.start()
    swap_cot = Swap(me, b.cot_own, b.cot_rows, both("swap"), 2)
    swap_x.end()

    def norm_rows(rows, l, i, out):
        out[me.slot] = layer_norm(rows, b.gain[l, i : i + 1], b.shift[l, i : i + 1]).astype(BF16)

    def project(l):
        w = weights["qo", l].full

        def consume(slot):
            qkv[l][slot] = (dot(normed_one[l][slot], columns(w, 0, 384)) + b.qbias[l : l + 1]).astype(BF16)

        return consume

    def forward(l, state, before_up, before_down, after_up):
        attend(qkv[l], b.mask, attended[l])
        before_up()
        w = weights["qo", l].full

        def out_product(slot):
            return dot(attended[l][slot], columns(w, 384, 128), NT)

        branch = sum_rows(me, out_product, send_bufs, land[0])
        middle[l][...] = state() + (branch + b.bias[l, 2:3])
        norm_rows(middle[l][...], l, 1, normed_two[l])
        gather = Gather(me, normed_two[l], *both("rows"))
        gather.start()
        before_down()
        weights["up", l].arrived()

        def consume(slot):
            h = dot(normed_two[l][slot], columns(weights["up", l].full, 0, 512)) + b.up_bias[l : l + 1, own_hid]
            value, slant = gelu_and_slope(h)
            act[l][slot] = value.astype(BF16)
            slope[l][slot] = slant.astype(BF16)

        gather.run(consume)
        weights["down", l].arrived()
        after_up()

        def down_product(slot):
            return dot(act[l][slot], columns(weights["down", l].full, 0, 512), NT)

        total = sum_rows(me, down_product, send_bufs, land[1])
        gather.end()
        return middle[l][...] + (total + b.bias[l, 3:4])

    norm_rows(b.x_rows[...].astype(F32), 0, 0, normed_one[0])
    gather = Gather(me, normed_one[0], *both("rows"))
    gather.start()
    swap_mask.end()
    gather.relay()
    weights["qo", 0].arrived()
    swap_cot.start()
    weights["up", 0].start()
    gather.run(project(0), relayed=True)
    gather.end()
    swap_cot.end()
    b.g_rows[me.slot] = b.cot_rows[...]
    gather_cot = Gather(me, b.g_rows, *both("cot"))
    gather_cot.start()

    b.state[...] = forward(
        0,
        lambda: b.x_rows[...].astype(F32),
        weights["down", 0].start,
        nothing,
        weights["qo", 1].start,
    )
    norm_rows(b.state[...], 1, 0, normed_one[1])
    gather = Gather(me, normed_one[1], *both("rows"))
    gather.start()
    weights["qo", 1].arrived()
    weights["up", 1].start()
    gather.run(project(1))
    gather.end()
    gather_cot.relay()
    b.rows_away[...] = forward(1, lambda: b.state[...], weights["down", 1].start, nothing, nothing).astype(BF16)
    swap_out = Swap(me, b.rows_away, b.rows_home, both("swap"), 3)
    swap_out.start()

    def narrow_sum(ref, row, at, count):
        total = column_sum(ref)
        for i in range(count):
            b.narrow[row + i : row + i + 1] = total[:, (at + i) * 128 : (at + i + 1) * 128]

    def backward(l, g_own, gather_g, after_down, after_up):
        down, up, w = weights["down", l].full, weights["up", l].full, weights["qo", l].full

        def consume(slot):
            grad_act = dot(b.g_rows[slot], columns(down, 0, 512))
            slope[l][slot] = (grad_act * slope[l][slot].astype(F32)).astype(BF16)

        gather_g.run(consume, relayed=l == 1)
        grad_hid = slope[l]

        def up_back(slot):
            return dot(grad_hid[slot], columns(up, 0, 512), NT)

        def fill():
            weight_grad(b.g_rows, act[l], b.dw_down, 0, 512)
            grads["down", l].start()
            narrow_sum(grad_hid, l * 6 + 2, 0, 4)
            after_down()

        grad = sum_rows(me, up_back, send_bufs, land[0], fill)
        gather_g.end()
        back, gain_sum, shift_sum = layer_norm_back(middle[l][...], b.gain[l, 1:2], grad)
        mid = g_own() + back
        b.grad_mid[...] = mid
        b.g_attn[me.slot] = mid.astype(BF16)
        gather = Gather(me, b.g_attn, *both("rows"))
        gather.start()
        row = l * 6 + 2
        b.wide[row : row + 1] = jnp.sum(g_own(), axis=0, keepdims=True)
        b.wide[row + 1 : row + 2] = gain_sum
        b.wide[row + 2 : row + 3] = shift_sum
        b.wide[row + 3 : row + 4] = jnp.sum(mid, axis=0, keepdims=True)

        def fill_two():
            after_up()
            weight_grad(normed_two[l], grad_hid, b.dw_up, 0, 512)
            grads["up", l].start()

        def att_back(slot):
            b.grad_att[slot] = dot(b.g_attn[slot], columns(w, 384, 128)).astype(BF16)

        gather.run(att_back, fill_two)
        gather.end()
        attend_back(qkv[l], b.mask, b.grad_att)

    def first_back(l, rows, more):
        w, grad_qkv = weights["qo", l].full, qkv[l]

        def back_product(slot):
            return dot(grad_qkv[slot], columns(w, 0, 384), NT)

        def fill():
            weight_grad(normed_one[l], grad_qkv, b.dw_qo, 0, 384)
            weight_grad(b.g_attn, attended[l], b.dw_qo, 384, 128)
            grads["qo", l].start()
            more()
            total = column_sum(grad_qkv)
            b.narrow[l * 6 : l * 6 + 1] = total[:, 0:128]
            b.narrow[l * 6 + 1 : l * 6 + 2] = total[:, 256:384]

        grad = sum_rows(me, back_product, send_bufs, land[1], fill)
        back, gain_sum, shift_sum = layer_norm_back(rows(), b.gain[l, 0:1], grad)
        b.wide[l * 6 : l * 6 + 1] = gain_sum
        b.wide[l * 6 + 1 : l * 6 + 2] = shift_sum
        return b.grad_mid[...] + back

    backward(1, lambda: b.cot_rows[...].astype(F32), gather_cot, nothing, nothing)
    b.grad[...] = first_back(1, lambda: b.state[...], grads["down", 1].end)
    b.g_rows[me.slot] = b.grad[...].astype(BF16)
    gather_g = Gather(me, b.g_rows, *both("cot"))
    gather_g.start()
    swap_out.end()
    b.out_rows[...] = b.rows_home[...]
    backward(0, lambda: b.grad[...], gather_g, grads["up", 1].end, grads["qo", 1].end)
    b.grad[...] = first_back(0, lambda: b.x_rows[...].astype(F32), grads["down", 0].end)
    b.rows_away[...] = b.grad[...].astype(BF16)
    vectors_start(me, b.wide, b.va, b.vl, *both("v1"))
    swap_grad = Swap(me, b.rows_away, b.x_own, both("swap"), 4)
    swap_grad.start()
    for name in cuts:
        for l in range(2):
            weights[name, l].sent()
    grads["up", 0].end()
    vectors_end(me, b.narrow, b.va, b.vl, *both("v1"), b.vb, b.piece, *both("v2"), b.vectors, *both("v3"))
    swap_grad.end()

    @pl.when(me.core == me.zlo)
    def _():
        b.gradient[...] = b.grad[...]

    @pl.when(me.core != me.zlo)
    def _():
        b.gradient[...] = b.x_own[...].astype(F32)

    grads["qo", 0].end()


def nothing():
    pass


def per_device(
    x_in, valid_len, w_qkv, w_out, w_up, w_down, norm_gain, norm_shift, bias, up_bias, cotangent
):
    at = jnp.arange(4 * PAD)
    token = (at // PAD) * ROWS + at % PAD
    mask = (at % PAD < ROWS) & (token < valid_len[:, None])
    mask = jnp.broadcast_to(mask[:, None].astype(F32), (2, 8, 4 * PAD))
    shards = jnp.concatenate(
        [w_qkv.reshape(2, 64, 384), jnp.swapaxes(w_out, 1, 2), w_up, jnp.swapaxes(w_down, 1, 2)], axis=2
    )
    vmem = pl.BlockSpec(memory_space=pltpu.VMEM)
    arrays = pl.pallas_call(
        whole_kernel,
        out_shape=[jax.ShapeDtypeStruct(s, t) for s, t in OUTPUTS.values()],
        in_specs=[vmem] * len(INPUTS),
        out_specs=[vmem] * len(OUTPUTS),
        scratch_shapes=list(scratch_table().values()),
        compiler_params=pltpu.CompilerParams(
            collective_id=0, has_side_effects=True, vmem_limit_bytes=VMEM_BYTES
        ),
    )(x_in, cotangent, mask, shards, norm_gain, norm_shift, bias, up_bias)
    results = list(pl.pallas_call(
        result_kernel,
        out_shape=[jax.ShapeDtypeStruct(s, t) for s, t in RESULTS.values()],
        in_specs=[vmem] * len(OUTPUTS),
        out_specs=[vmem] * len(RESULTS),
    )(*arrays))
    results[2] = jnp.swapaxes(results[2], 1, 2)
    results[3] = jnp.swapaxes(results[3], 1, 2)
    results[5] = jnp.swapaxes(results[5], 1, 2)
    return tuple(results)


def solution(mesh):
    rows = P(("dp", "tensor"), None)
    weights = (P(None, "dp", None, "tensor"), P(None, "tensor", "dp"), P(None, "dp", "tensor"), P(None, "tensor", "dp"))
    return jax.shard_map(
        per_device,
        mesh=mesh,
        in_specs=(rows, P("dp"), *weights, P(), P(), P(), P(), rows),
        out_specs=(rows, rows, *weights, P(), P(), P(), P()),
        check_vma=False,
    )
```

```python
import types

import jax
import jax.numpy as jnp
from jax import lax
from jax.experimental import pallas as pl
from jax.experimental.pallas import tpu as pltpu
from jax.sharding import PartitionSpec as P

MESH = pl.DeviceIdType.MESH
F32, BF16 = jnp.float32, jnp.bfloat16

D = 1024
ROWS = 146
PAD = 160
COLS = 128
HEAD = 64
HID = 512
MEMBERS = 8
WCOLS = 1536
EPSILON = 1e-06
NEG_FILL = -1e30
VMEM_BYTES = 64 * 1024 * 1024 - 65536

NN = (((1,), (0,)), ((), ()))
NT = (((1,), (1,)), ((), ()))
TN = (((0,), (0,)), ((), ()))


def dot(a, b, dims=NN):
    return lax.dot_general(a, b, dims, preferred_element_type=F32)


class Place:
    def __init__(self):
        self.dp = lax.axis_index("dp")
        self.tensor = lax.axis_index("tensor")
        self.core = self.dp % 2
        self.pair = self.dp // 2
        self.zlo = self.tensor // 4
        self.x = self.tensor % 4
        self.slot = self.core * 4 + self.x
        self.group = self.pair * 2 + self.zlo

    def peer(self, core, x):
        return {"dp": self.pair * 2 + core, "tensor": self.zlo * 4 + x}

    def sibling(self):
        return self.peer(1 - self.core, self.x)


def greet(me, work):
    barrier = pltpu.get_barrier_semaphore()

    def member(i, carry):
        pl.semaphore_signal(
            barrier,
            inc=1,
            device_id=me.peer((me.core + i // 4) % 2, (me.x + i) % 4),
            device_id_type=MESH,
        )
        return carry

    lax.fori_loop(1, MEMBERS, member, 0)

    def other(i, carry):
        pair = (me.pair + i // 4) % 8
        zlo = (me.zlo + (i // 2) % 2) % 2
        pl.semaphore_signal(
            barrier,
            inc=1,
            device_id={"dp": pair * 2 + i % 2, "tensor": zlo * 4 + me.x},
            device_id_type=MESH,
        )
        return carry

    lax.fori_loop(2, 32, other, 0)
    work()
    pl.semaphore_wait(barrier, MEMBERS - 1 + 30)


def remote(src, dst, send, recv, device):
    return pltpu.make_async_remote_copy(
        src_ref=src,
        dst_ref=dst,
        send_sem=send,
        recv_sem=recv,
        device_id=device,
        device_id_type=MESH,
    )


def slot_at(me, i):
    sibling = (i == 1) | (i == 4) | (i == 5) | (i == 7)
    far = (i >= 6).astype(jnp.int32) * 2
    left = ((i == 2) | (i == 4)).astype(jnp.int32) * 3
    right = ((i == 3) | (i == 5)).astype(jnp.int32)
    core = (me.core + sibling.astype(jnp.int32)) % 2
    return core * 4 + (me.x + far + left + right) % 4


HALF = PAD // 2
TOP, BOTTOM = pl.ds(0, HALF), pl.ds(HALF, HALF)


class Gather:
    def __init__(self, me, g, send, recv):
        self.me, self.g, self.send, self.recv = me, g, send, recv
        self.right = me.peer(me.core, (me.x + 1) % 4)
        self.left = me.peer(me.core, (me.x + 3) % 4)
        self.from_left = me.core * 4 + (me.x + 3) % 4
        self.from_right = me.core * 4 + (me.x + 1) % 4
        self.from_far = me.core * 4 + (me.x + 2) % 4

    def copy(self, k, slot, rows, device):
        block = self.g.at[slot] if rows is None else self.g.at[slot, rows]
        return remote(block, block, self.send.at[k], self.recv.at[k], device)

    def table(self):
        me = self.me
        sibling = me.sibling()
        return [
            (0, me.slot, TOP, self.right),
            (1, me.slot, BOTTOM, self.right),
            (2, me.slot, TOP, self.left),
            (3, me.slot, BOTTOM, self.left),
            (4, self.from_left, TOP, self.right),
            (5, self.from_right, BOTTOM, self.left),
            (6, me.slot, None, sibling),
            (7, self.from_left, None, sibling),
            (8, self.from_right, None, sibling),
            (9, self.from_far, None, sibling),
        ]

    def start_copies(self, *which):
        for k in which:
            self.copy(*self.table()[k]).start()

    def start(self):
        self.start_copies(6, 0, 3, 1, 2)

    def arrived(self, *which):
        for k in which:
            _, slot, rows, device = self.table()[k]
            self.copy(k, slot, rows, device).wait_recv()

    def relay(self):
        self.arrived(0)
        self.start_copies(4)
        self.arrived(3)
        self.start_copies(5)

    def run(self, consume, fill=None, relayed=False):
        def step(i, carry):
            @pl.when(i == 1)
            def _():
                self.arrived(6)

            @pl.when(i == 2)
            def _():
                if not relayed:
                    self.relay()
                if fill is not None:
                    fill()
                self.arrived(1)
                self.start_copies(7)

            @pl.when(i == 3)
            def _():
                self.arrived(2)
                self.start_copies(8)

            @pl.when(i == 4)
            def _():
                self.arrived(7)

            @pl.when(i == 5)
            def _():
                self.arrived(8)

            @pl.when(i == 6)
            def _():
                self.arrived(4, 5)
                self.start_copies(9)

            @pl.when(i == 7)
            def _():
                self.arrived(9)

            consume(slot_at(self.me, i))
            return carry

        lax.fori_loop(0, MEMBERS, step, 0)

    def end(self):
        for row in self.table():
            self.copy(*row).wait_send()


GATHER_SEMS = [pltpu.SemaphoreType.DMA((10,)), pltpu.SemaphoreType.DMA((10,))]

SUM_SEND = [
    pltpu.VMEM((4, PAD, D), BF16),
    pltpu.VMEM((3, PAD, D), BF16),
    pltpu.VMEM((PAD, D), F32),
    pltpu.VMEM((2, HALF, D), F32),
]
SUM_LAND = [
    pltpu.VMEM((4, PAD, D), BF16),
    pltpu.VMEM((PAD, D), BF16),
    pltpu.VMEM((2, PAD, D), BF16),
    pltpu.SemaphoreType.DMA((4,)),
    pltpu.SemaphoreType.DMA((4,)),
    pltpu.SemaphoreType.DMA((6,)),
    pltpu.SemaphoreType.DMA((6,)),
]


def sum_rows(me, produce, send_bufs, land_bufs, pending, fill=None):
    for wait in pending:
        wait()
    pending.clear()
    s1, s2, acc, hold = send_bufs
    r1, ra, rb, ss1, rs1, ss2, rs2 = land_bufs
    sibling = me.sibling()
    right, left = me.peer(me.core, (me.x + 1) % 4), me.peer(me.core, (me.x + 3) % 4)

    def chip(i):
        return (me.x + 2 + (i == 1).astype(jnp.int32) * 3 + (i == 2).astype(jnp.int32) + (i == 3).astype(jnp.int32) * 2) % 4

    def to_sibling(i):
        return remote(s1.at[i], r1.at[i], ss1.at[i], rs1.at[i], sibling)

    def along(k):
        src, dst, device = (
            (s2.at[0, TOP], ra.at[TOP], right),
            (s2.at[0, BOTTOM], ra.at[BOTTOM], left),
            (s2.at[1, BOTTOM], rb.at[0, BOTTOM], right),
            (s2.at[2, TOP], rb.at[1, TOP], left),
            (s2.at[1, TOP], rb.at[0, TOP], right),
            (s2.at[2, BOTTOM], rb.at[1, BOTTOM], left),
        )[k]
        return remote(src, dst, ss2.at[k], rs2.at[k], device)

    def for_sibling(i, carry):
        s1[i] = produce((1 - me.core) * 4 + chip(i)).astype(BF16)
        to_sibling(i).start()
        return carry

    def own(i, carry):
        part = produce(me.core * 4 + chip(i))
        to_sibling(i).wait_recv()
        acc[...] = part + r1[i].astype(F32)

        @pl.when(i == 0)
        def _():
            s2[0] = acc[...].astype(BF16)
            along(0).start()
            along(1).start()

        @pl.when(i == 1)
        def _():
            s2[1, BOTTOM] = acc[BOTTOM].astype(BF16)
            along(2).start()
            hold[0] = acc[TOP]

        @pl.when(i == 2)
        def _():
            s2[2, TOP] = acc[TOP].astype(BF16)
            along(3).start()
            hold[1] = acc[BOTTOM]

        @pl.when(i < 2)
        def _():
            for_sibling(i + 2, 0)

        return carry

    lax.fori_loop(0, 2, for_sibling, 0)
    lax.fori_loop(0, 4, own, 0)
    if fill is not None:
        fill()
    along(0).wait_recv()
    s2[1, TOP] = (hold[0] + ra[TOP].astype(F32)).astype(BF16)
    along(4).start()
    along(1).wait_recv()
    s2[2, BOTTOM] = (hold[1] + ra[BOTTOM].astype(F32)).astype(BF16)
    along(5).start()
    for k in range(2, 6):
        along(k).wait_recv()
    total = acc[...] + rb[0].astype(F32) + rb[1].astype(F32)

    def sent():
        for i in range(4):
            to_sibling(i).wait_send()
        for k in range(6):
            along(k).wait_send()

    pending.append(sent)
    return total


PLANE_SEMS = [pltpu.SemaphoreType.DMA((16,)), pltpu.SemaphoreType.DMA((16,))]


def weights_copy(me, i, shard, full, send, recv):
    pair, zlo = (me.pair + i // 2) % 8, (me.zlo + i) % 2
    device = {"dp": pair * 2 + me.zlo, "tensor": zlo * 4 + me.x}
    return remote(shard, full.at[me.dp], send.at[i], recv.at[me.dp], device)


def weights_start(me, shard, full, send, recv):
    def step(i, carry):
        weights_copy(me, i, shard, full, send, recv).start()
        return carry

    own = me.core == me.zlo

    @pl.when(own)
    def _():
        pltpu.make_async_copy(shard, full.at[me.dp], recv.at[me.dp]).start()

    @pl.when(jnp.logical_not(own))
    def _():
        weights_copy(me, 0, shard, full, send, recv).start()

    lax.fori_loop(1, 16, step, 0)


def weights_arrived(me, shard, full, send, recv):
    def step(i, carry):
        remote(shard, full.at[i], send.at[i], recv.at[i], me.sibling()).wait_recv()
        return carry

    lax.fori_loop(0, 16, step, 0)


def weights_sent(me, shard, full, send, recv):
    @pl.when(me.core != me.zlo)
    def _():
        weights_copy(me, 0, shard, full, send, recv).wait_send()

    def step(i, carry):
        weights_copy(me, i, shard, full, send, recv).wait_send()
        return carry

    lax.fori_loop(1, 16, step, 0)


def grads_copy(me, i, part, land, send, recv):
    to = (me.dp + i) % 16
    device = {"dp": to, "tensor": me.slot}
    return remote(part.at[to], land.at[me.group], send.at[i], recv.at[me.group], device)


def grads_start(me, part, land, send, recv):
    own = me.zlo == me.core

    @pl.when(own)
    def _():
        pltpu.make_async_copy(part.at[me.dp], land.at[me.group], recv.at[me.group]).start()

    @pl.when(jnp.logical_not(own))
    def _():
        grads_copy(me, 0, part, land, send, recv).start()

    def step(i, carry):
        grads_copy(me, i, part, land, send, recv).start()
        return carry

    lax.fori_loop(1, 16, step, 0)


def grads_end(me, part, land, send, recv, store):
    def arrived(i, carry):
        remote(part.at[0], land.at[i], send.at[i], recv.at[i], me.sibling()).wait_recv()
        return carry

    lax.fori_loop(0, 16, arrived, 0)

    @pl.when(me.zlo != me.core)
    def _():
        grads_copy(me, 0, part, land, send, recv).wait_send()

    def sent(i, carry):
        grads_copy(me, i, part, land, send, recv).wait_send()
        return carry

    lax.fori_loop(1, 16, sent, 0)
    total = land[0].astype(F32)
    for i in range(1, 16):
        total = total + land[i].astype(F32)
    store(total)


def normalized(rows):
    centred = rows - jnp.mean(rows, axis=-1, keepdims=True)
    scale = lax.rsqrt(jnp.mean(centred * centred, axis=-1, keepdims=True) + EPSILON)
    return centred * scale, scale


def layer_norm(rows, gain, shift):
    return normalized(rows)[0] * gain + shift


def layer_norm_back(rows, gain, grad):
    unit, scale = normalized(rows)
    inner = grad * gain
    mean_one = jnp.mean(inner, axis=-1, keepdims=True)
    mean_two = jnp.mean(inner * unit, axis=-1, keepdims=True)
    back = scale * (inner - mean_one - unit * mean_two)
    return back, jnp.sum(grad * unit, axis=0, keepdims=True), jnp.sum(grad, axis=0, keepdims=True)


def erf(v):
    v = jnp.clip(v, -4.0, 4.0)
    s = v * v
    top = F32(-2.72614225801306e-10)
    for a in (
        2.77068142495902e-08,
        -2.10102402082508e-06,
        -5.69250639462346e-05,
        -7.34990630326855e-04,
        -2.95459980854025e-03,
        -1.60960333262415e-02,
    ):
        top = top * s + F32(a)
    low = F32(-1.45660718464996e-05)
    for b in (
        -2.13374055278905e-04,
        -1.68282697438203e-03,
        -7.37332916720468e-03,
        -1.42647390514189e-02,
    ):
        low = low * s + F32(b)
    return v * top / low


def normal_below(v):
    return 0.5 * (1.0 + erf(v * F32(0.7071067811865476)))


def gelu_and_slope(v):
    below = normal_below(v)
    return v * below, below + v * jnp.exp(-0.5 * v * v) * F32(0.3989422804014327)


def weight_grad(left, right, out, at, width):
    def tile(i, carry):
        a = left[:, :, pl.ds(pl.multiple_of(i * 256, 256), 256)].reshape(MEMBERS * PAD, 256)
        b = right[...].reshape(MEMBERS * PAD, width)
        block = dot(a, b, TN).astype(BF16).reshape(4, 64, width)
        out[pl.ds(i * 4, 4), :, at : at + width] = block
        return carry

    lax.fori_loop(0, D // 256, tile, 0)


def columns(w, at, width):
    return w[:, :, at : at + width].reshape(D, width)


def column_sum(ref):
    def step(i, total):
        return total + jnp.sum(ref[i].astype(F32), axis=0, keepdims=True)

    return lax.fori_loop(0, MEMBERS, step, jnp.zeros((1, ref.shape[2]), F32))


def head_parts(qkv, i, at):
    return qkv[pl.ds(i * 4, 4), :, at * COLS : (at + 1) * COLS].reshape(4 * PAD, COLS)


def attend(qkv, mask, out):
    lane = lax.broadcasted_iota(jnp.int32, (1, COLS), 1)

    def image(i, carry):
        q, k, v = (head_parts(qkv, i, j) for j in range(3))
        q = q * BF16(HEAD**-0.5)
        valid = mask[i, 0:1] > 0.5
        total = None
        for h in range(2):
            mine = (lane >= h * HEAD) & (lane < (h + 1) * HEAD)
            scores = dot(jnp.where(mine, q, jnp.zeros_like(q)), k, NT)
            scores = jnp.where(valid, scores, NEG_FILL)
            e = jnp.exp(scores - jnp.max(scores, axis=-1, keepdims=True))
            prob = (e * (1.0 / jnp.sum(e, axis=-1, keepdims=True))).astype(BF16)
            mixed = dot(prob, v)
            total = mixed if total is None else jnp.where(mine, mixed, total)
        out[pl.ds(i * 4, 4)] = total.astype(BF16).reshape(4, PAD, COLS)
        return carry

    lax.fori_loop(0, 2, image, 0)


def attend_back(qkv, mask, grad):
    lane = lax.broadcasted_iota(jnp.int32, (1, COLS), 1)

    def image(i, carry):
        q, k, v = (head_parts(qkv, i, j) for j in range(3))
        q = q * BF16(HEAD**-0.5)
        g = grad[pl.ds(i * 4, 4)].reshape(4 * PAD, COLS)
        valid = mask[i].T[:, 0:1] > 0.5
        parts = [None, None, None]
        for h in range(2):
            mine = (lane >= h * HEAD) & (lane < (h + 1) * HEAD)
            scores = dot(k, jnp.where(mine, q, jnp.zeros_like(q)), NT)
            scores = jnp.where(valid, scores, NEG_FILL)
            e = jnp.exp(scores - jnp.max(scores, axis=0, keepdims=True))
            prob = e * (1.0 / jnp.sum(e, axis=0, keepdims=True))
            grad_value = dot(prob.astype(BF16), g)
            grad_prob = dot(v, jnp.where(mine, g, jnp.zeros_like(g)), NT)
            inner = jnp.sum(grad_prob * prob, axis=0, keepdims=True)
            grad_scores = (prob * (grad_prob - inner)).astype(BF16)
            grad_key = dot(grad_scores, q)
            grad_query = dot(grad_scores, k, TN) * F32(HEAD**-0.5)
            new = [grad_query, grad_key, grad_value]
            parts = new if h == 0 else [jnp.where(mine, n, p) for n, p in zip(new, parts)]
        for j in range(3):
            qkv[pl.ds(i * 4, 4), :, j * COLS : (j + 1) * COLS] = parts[j].astype(BF16).reshape(4, PAD, COLS)
        return carry

    lax.fori_loop(0, 2, image, 0)


def vectors_start(me, wide, va, vl, send, recv):
    for s in range(MEMBERS):
        va[s] = wide[:, s * 128 : (s + 1) * 128]

    def step(i, carry):
        core, x = (me.core + i // 4) % 2, (me.x + i) % 4
        remote(va.at[core * 4 + x], vl.at[i], send.at[i], recv.at[i], me.peer(core, x)).start()
        return carry

    lax.fori_loop(1, MEMBERS, step, 0)


def vectors_end(me, narrow, va, vl, send, recv, vb, piece, send2, recv2, out, send3, recv3):
    total = va[me.slot]
    for i in range(1, MEMBERS):
        remote(va.at[0], vl.at[i], send.at[i], recv.at[i], me.sibling()).wait()
        total = total + vl[i]
    piece[0:16] = total
    piece[16:32] = narrow[...]

    def to_group(i):
        pair, zlo = (me.pair + i // 2) % 8, (me.zlo + i) % 2
        device = {"dp": pair * 2 + me.core, "tensor": zlo * 4 + me.x}
        return remote(piece, vb.at[me.group], send2.at[i], recv2.at[me.group], device)

    def start(i, carry):
        to_group(i).start()
        return carry

    lax.fori_loop(1, 16, start, 0)
    vb[me.group] = piece[...]

    def end(i, carry):
        to_group(i).wait_send()
        group = (me.group + i) % 16
        remote(piece, vb.at[group], send2.at[i], recv2.at[group], me.sibling()).wait_recv()
        return carry

    lax.fori_loop(1, 16, end, 0)
    total = vb[0]
    for i in range(1, 16):
        total = total + vb[i]
    out[me.slot] = total
    own = out.at[me.slot]

    def to_member(i):
        core, x = (me.core + i // 4) % 2, (me.x + i) % 4
        return remote(own, own, send3.at[i], recv3.at[me.slot], me.peer(core, x))

    def start_three(i, carry):
        to_member(i).start()
        return carry

    lax.fori_loop(1, MEMBERS, start_three, 0)

    def end_three(i, carry):
        to_member(i).wait_send()
        slot = ((me.core + i // 4) % 2) * 4 + (me.x + i) % 4
        remote(own, out.at[slot], send3.at[i], recv3.at[slot], me.sibling()).wait_recv()
        return carry

    lax.fori_loop(1, MEMBERS, end_three, 0)


class Weights:
    def __init__(self, me, shard, full, send, recv):
        self.args, self.full = (me, shard, full, send, recv), full

    def start(self):
        weights_start(*self.args)

    def arrived(self):
        weights_arrived(*self.args)

    def sent(self):
        weights_sent(*self.args)


class Grads:
    def __init__(self, me, part, land, send, recv, out):
        self.args, self.part = (me, part, land, send, recv, out), part

    def start(self):
        grads_start(*self.args[:5])

    def end(self):
        grads_end(*self.args)


class Swap:
    def __init__(self, me, src, dst, sems, k):
        self.away = me.core != me.zlo
        self.src, self.dst = src, dst
        partner = {"dp": me.pair * 2 + me.zlo, "tensor": me.core * 4 + me.x}
        self.copy = remote(src, dst, sems[0].at[k], sems[1].at[k], partner)

    def start(self):
        @pl.when(self.away)
        def _():
            self.copy.start()

    def end(self):
        @pl.when(self.away)
        def _():
            self.copy.wait()

        @pl.when(jnp.logical_not(self.away))
        def _():
            self.dst[...] = self.src[...]


ROWS_ALL, ROWS_OWN, PART = (MEMBERS, PAD, D), (PAD, D), (16, 64, 512)
HID_ALL, ATT_ALL, QKV_ALL, SUMMED = (MEMBERS, PAD, HID), (MEMBERS, PAD, COLS), (MEMBERS, PAD, 384), (64, 512)
DMA = pltpu.SemaphoreType.DMA

INPUTS = ("x_in", "cot_in", "mask_in", "shards", "gain", "shift", "bias", "up_bias")
OUTPUTS = {
    "out_rows": (ROWS_OWN, BF16),
    "gradient": (ROWS_OWN, F32),
    "sum_qo": ((2, *SUMMED), F32),
    "sum_up": ((2, *SUMMED), F32),
    "sum_down": ((2, *SUMMED), F32),
    "vectors": ((MEMBERS, 32, 128), F32),
}
RESULTS = {
    "out_rows": ((ROWS, D), BF16),
    "gradient": ((ROWS, D), F32),
    "grad_qkv": ((2, 3, 64, COLS), F32),
    "grad_out": ((2, 64, COLS), F32),
    "grad_up": ((2, 64, HID), F32),
    "grad_down": ((2, 64, HID), F32),
    "grad_gain": ((2, 2, D), F32),
    "grad_shift": ((2, 2, D), F32),
    "grad_bias": ((2, 4, D), F32),
    "grad_up_bias": ((2, 4096), F32),
}


def result_kernel(*refs):
    b = types.SimpleNamespace(**dict(zip([*["in_" + n for n in OUTPUTS], *RESULTS], refs, strict=True)))
    b.out_rows[...] = b.in_out_rows[...].astype(F32)[:ROWS].astype(BF16)
    b.gradient[...] = b.in_gradient[...][:ROWS]
    for j in range(3):
        b.grad_qkv[:, j] = b.in_sum_qo[:, :, j * COLS : (j + 1) * COLS]
    b.grad_out[...] = b.in_sum_qo[:, :, 3 * COLS :]
    b.grad_up[...] = b.in_sum_up[...]
    b.grad_down[...] = b.in_sum_down[...]
    for s in range(MEMBERS):
        cols = slice(s * COLS, (s + 1) * COLS)
        for l in range(2):
            for ref, at, row in (
                (b.grad_gain, 0, 0),
                (b.grad_shift, 0, 1),
                (b.grad_bias, 3, 2),
                (b.grad_gain, 1, 3),
                (b.grad_shift, 1, 4),
                (b.grad_bias, 2, 5),
                (b.grad_bias, 0, 16),
                (b.grad_bias, 1, 17),
            ):
                ref[l, at : at + 1, cols] = b.in_vectors[s, row + 6 * l : row + 6 * l + 1]
            for j in range(4):
                to = s * HID + j * COLS
                b.grad_up_bias[l : l + 1, to : to + COLS] = b.in_vectors[s, 18 + 6 * l + j : 19 + 6 * l + j]


def scratch_table():
    table = {"padded": pltpu.VMEM(ROWS_OWN, F32)}

    def add(name, shape, dtype, count=None):
        if count is None:
            table[name] = pltpu.VMEM(shape, dtype)
        for i in range(count or 0):
            table[f"{name}{i}"] = pltpu.VMEM(shape, dtype)

    for name in ("x_own", "x_rows", "cot_own", "cot_rows", "rows_away", "rows_home"):
        add(name, ROWS_OWN, BF16)
    add("mask", (2, 8, 4 * PAD), F32)
    for name in ("qo", "up", "down", "land_qo", "land_up", "land_down"):
        add(name, PART, BF16, 2)
    for name in ("dw_qo", "dw_up", "dw_down"):
        add(name, PART, BF16)
    add("normed_one", ROWS_ALL, BF16, 2)
    add("normed_two", ROWS_ALL, BF16, 2)
    add("qkv", QKV_ALL, BF16, 2)
    add("attended", ATT_ALL, BF16, 2)
    add("slope", HID_ALL, BF16, 2)
    add("act", HID_ALL, BF16, 2)
    add("middle", ROWS_OWN, F32, 2)
    add("state", ROWS_OWN, F32)
    add("g_rows", ROWS_ALL, BF16)
    add("g_attn", ROWS_ALL, BF16)
    add("grad_att", ATT_ALL, BF16)
    add("grad_mid", ROWS_OWN, F32)
    add("grad", ROWS_OWN, F32)
    add("wide", (16, D), F32)
    add("narrow", (16, 128), F32)
    add("va", (MEMBERS, 16, 128), F32)
    add("vl", (MEMBERS, 16, 128), F32)
    add("qbias", (2, 384), F32)
    add("vb", (16, 32, 128), F32)
    add("piece", (32, 128), F32)
    for i, spec in enumerate(SUM_SEND):
        table[f"sum_send{i}"] = spec
    for j in range(2):
        for i, spec in enumerate(SUM_LAND):
            table[f"sum_land{j}_{i}"] = spec
    for name, count in (("rows", 10), ("cot", 10), ("swap", 5), ("v1", 8), ("v2", 16), ("v3", 8)):
        table[name + "_send"], table[name + "_recv"] = DMA((count,)), DMA((count,))
    for name in ("w", "g"):
        table[name + "_send"], table[name + "_recv"] = DMA((6, 16)), DMA((6, 16))
    return table


def whole_kernel(*refs):
    table = scratch_table()
    names = [*INPUTS, *OUTPUTS, *table]
    b = types.SimpleNamespace(**dict(zip(names, refs, strict=True)))
    me = Place()

    def padded(rows, out):
        b.padded[0:ROWS] = rows[...].astype(F32)
        b.padded[ROWS:PAD] = jnp.zeros((PAD - ROWS, D), F32)
        out[...] = b.padded[...].astype(BF16)

    own_cols = pl.ds(pl.multiple_of(me.slot * COLS, COLS), COLS)
    own_hid = pl.ds(pl.multiple_of(me.slot * HID, HID), HID)

    def work():
        padded(b.x_in, b.x_own)
        padded(b.cot_in, b.cot_own)
        b.wide[...] = jnp.zeros_like(b.wide)
        b.narrow[...] = jnp.zeros_like(b.narrow)
        b.qbias[...] = jnp.zeros_like(b.qbias)
        for l in range(2):
            b.qbias[l : l + 1, 0:COLS] = b.bias[l, 0:1, own_cols]
            b.qbias[l : l + 1, 2 * COLS :] = b.bias[l, 1:2, own_cols]

    greet(me, work)

    def both(name):
        return getattr(b, name + "_send"), getattr(b, name + "_recv")

    def pair(name):
        return [getattr(b, name + "0"), getattr(b, name + "1")]

    cuts = {"qo": pl.ds(0, 512), "up": pl.ds(512, 512), "down": pl.ds(1024, 512)}
    weights, grads, pending = {}, {}, []

    def store_qo(l):
        def store(total):
            b.sum_qo[l] = total

        return store

    def store_up(l):
        def store(total):
            b.sum_up[l] = total

        return store

    def store_down(l):
        def store(total):
            b.sum_down[l] = total

        return store

    stores = {"qo": store_qo, "up": store_up, "down": store_down}
    for n, name in enumerate(cuts):
        for l in range(2):
            k = n * 2 + l
            shard = b.shards.at[l, :, cuts[name]]
            weights[name, l] = Weights(me, shard, pair(name)[l], b.w_send.at[k], b.w_recv.at[k])
            part = getattr(b, "dw_" + name)
            land_part = pair("land_" + name)[l]
            grads[name, l] = Grads(me, part, land_part, b.g_send.at[k], b.g_recv.at[k], stores[name](l))
    send_bufs = [getattr(b, f"sum_send{i}") for i in range(len(SUM_SEND))]
    land = [[getattr(b, f"sum_land{j}_{i}") for i in range(len(SUM_LAND))] for j in range(2)]
    normed_one, normed_two, qkv, attended = (pair(n) for n in ("normed_one", "normed_two", "qkv", "attended"))
    slope, act, middle = (pair(n) for n in ("slope", "act", "middle"))

    weights["qo", 0].start()
    swap_x = Swap(me, b.x_own, b.x_rows, both("swap"), 0)
    swap_x.start()
    swap_mask = Swap(me, b.mask_in, b.mask, both("swap"), 1)
    swap_mask.start()
    swap_cot = Swap(me, b.cot_own, b.cot_rows, both("swap"), 2)
    swap_x.end()

    def norm_rows(rows, l, i, out):
        out[me.slot] = layer_norm(rows, b.gain[l, i : i + 1], b.shift[l, i : i + 1]).astype(BF16)

    def project(l):
        w = weights["qo", l].full

        def consume(slot):
            qkv[l][slot] = (dot(normed_one[l][slot], columns(w, 0, 384)) + b.qbias[l : l + 1]).astype(BF16)

        return consume

    def forward(l, state, before_up, before_down, after_up):
        attend(qkv[l], b.mask, attended[l])
        before_up()
        w = weights["qo", l].full

        def out_product(slot):
            return dot(attended[l][slot], columns(w, 384, 128), NT)

        branch = sum_rows(me, out_product, send_bufs, land[0], pending)
        middle[l][...] = state() + (branch + b.bias[l, 2:3])
        norm_rows(middle[l][...], l, 1, normed_two[l])
        gather = Gather(me, normed_two[l], *both("rows"))
        gather.start()
        before_down()
        weights["up", l].arrived()

        def consume(slot):
            h = dot(normed_two[l][slot], columns(weights["up", l].full, 0, 512)) + b.up_bias[l : l + 1, own_hid]
            value, slant = gelu_and_slope(h)
            act[l][slot] = value.astype(BF16)
            slope[l][slot] = slant.astype(BF16)

        gather.run(consume)
        weights["down", l].arrived()
        after_up()

        def down_product(slot):
            return dot(act[l][slot], columns(weights["down", l].full, 0, 512), NT)

        total = sum_rows(me, down_product, send_bufs, land[1], pending)
        gather.end()
        return middle[l][...] + (total + b.bias[l, 3:4])

    norm_rows(b.x_rows[...].astype(F32), 0, 0, normed_one[0])
    gather = Gather(me, normed_one[0], *both("rows"))
    gather.start()
    swap_mask.end()
    gather.relay()
    weights["qo", 0].arrived()
    swap_cot.start()
    weights["up", 0].start()
    gather.run(project(0), relayed=True)
    pending.append(gather.end)
    swap_cot.end()
    b.g_rows[me.slot] = b.cot_rows[...]
    gather_cot = Gather(me, b.g_rows, *both("cot"))
    gather_cot.start()

    b.state[...] = forward(
        0,
        lambda: b.x_rows[...].astype(F32),
        weights["down", 0].start,
        nothing,
        weights["qo", 1].start,
    )
    norm_rows(b.state[...], 1, 0, normed_one[1])
    gather = Gather(me, normed_one[1], *both("rows"))
    gather.start()
    weights["qo", 1].arrived()
    weights["up", 1].start()
    gather.run(project(1))
    pending.append(gather.end)
    gather_cot.relay()
    b.rows_away[...] = forward(1, lambda: b.state[...], weights["down", 1].start, nothing, nothing).astype(BF16)
    swap_out = Swap(me, b.rows_away, b.rows_home, both("swap"), 3)
    swap_out.start()

    def narrow_sum(ref, row, at, count):
        total = column_sum(ref)
        for i in range(count):
            b.narrow[row + i : row + i + 1] = total[:, (at + i) * 128 : (at + i + 1) * 128]

    def backward(l, g_own, gather_g, after_down, after_up):
        down, up, w = weights["down", l].full, weights["up", l].full, weights["qo", l].full

        def consume(slot):
            grad_act = dot(b.g_rows[slot], columns(down, 0, 512))
            slope[l][slot] = (grad_act * slope[l][slot].astype(F32)).astype(BF16)

        gather_g.run(consume, relayed=l == 1)
        grad_hid = slope[l]

        def up_back(slot):
            return dot(grad_hid[slot], columns(up, 0, 512), NT)

        def fill():
            weight_grad(b.g_rows, act[l], b.dw_down, 0, 512)
            grads["down", l].start()
            narrow_sum(grad_hid, l * 6 + 2, 0, 4)
            after_down()

        grad = sum_rows(me, up_back, send_bufs, land[0], pending, fill)
        pending.append(gather_g.end)
        back, gain_sum, shift_sum = layer_norm_back(middle[l][...], b.gain[l, 1:2], grad)
        mid = g_own() + back
        b.grad_mid[...] = mid
        b.g_attn[me.slot] = mid.astype(BF16)
        gather = Gather(me, b.g_attn, *both("rows"))
        gather.start()
        row = l * 6 + 2
        b.wide[row : row + 1] = jnp.sum(g_own(), axis=0, keepdims=True)
        b.wide[row + 1 : row + 2] = gain_sum
        b.wide[row + 2 : row + 3] = shift_sum
        b.wide[row + 3 : row + 4] = jnp.sum(mid, axis=0, keepdims=True)

        def fill_two():
            after_up()
            weight_grad(normed_two[l], grad_hid, b.dw_up, 0, 512)
            grads["up", l].start()

        def att_back(slot):
            b.grad_att[slot] = dot(b.g_attn[slot], columns(w, 384, 128)).astype(BF16)

        gather.run(att_back, fill_two)
        pending.append(gather.end)
        attend_back(qkv[l], b.mask, b.grad_att)

    def first_back(l, rows, more):
        w, grad_qkv = weights["qo", l].full, qkv[l]

        def back_product(slot):
            return dot(grad_qkv[slot], columns(w, 0, 384), NT)

        def fill():
            weight_grad(normed_one[l], grad_qkv, b.dw_qo, 0, 384)
            weight_grad(b.g_attn, attended[l], b.dw_qo, 384, 128)
            grads["qo", l].start()
            more()
            total = column_sum(grad_qkv)
            b.narrow[l * 6 : l * 6 + 1] = total[:, 0:128]
            b.narrow[l * 6 + 1 : l * 6 + 2] = total[:, 256:384]

        grad = sum_rows(me, back_product, send_bufs, land[1], pending, fill)
        back, gain_sum, shift_sum = layer_norm_back(rows(), b.gain[l, 0:1], grad)
        b.wide[l * 6 : l * 6 + 1] = gain_sum
        b.wide[l * 6 + 1 : l * 6 + 2] = shift_sum
        return b.grad_mid[...] + back

    backward(1, lambda: b.cot_rows[...].astype(F32), gather_cot, nothing, nothing)
    b.grad[...] = first_back(1, lambda: b.state[...], grads["down", 1].end)
    b.g_rows[me.slot] = b.grad[...].astype(BF16)
    gather_g = Gather(me, b.g_rows, *both("cot"))
    gather_g.start()
    swap_out.end()
    b.out_rows[...] = b.rows_home[...]
    backward(0, lambda: b.grad[...], gather_g, grads["up", 1].end, grads["qo", 1].end)
    b.grad[...] = first_back(0, lambda: b.x_rows[...].astype(F32), grads["down", 0].end)
    b.rows_away[...] = b.grad[...].astype(BF16)
    vectors_start(me, b.wide, b.va, b.vl, *both("v1"))
    swap_grad = Swap(me, b.rows_away, b.x_own, both("swap"), 4)
    swap_grad.start()
    for name in cuts:
        for l in range(2):
            weights[name, l].sent()
    grads["up", 0].end()
    vectors_end(me, b.narrow, b.va, b.vl, *both("v1"), b.vb, b.piece, *both("v2"), b.vectors, *both("v3"))
    swap_grad.end()

    @pl.when(me.core == me.zlo)
    def _():
        b.gradient[...] = b.grad[...]

    @pl.when(me.core != me.zlo)
    def _():
        b.gradient[...] = b.x_own[...].astype(F32)

    grads["qo", 0].end()
    for wait in pending:
        wait()


def nothing():
    pass


def per_device(
    x_in, valid_len, w_qkv, w_out, w_up, w_down, norm_gain, norm_shift, bias, up_bias, cotangent
):
    at = jnp.arange(4 * PAD)
    token = (at // PAD) * ROWS + at % PAD
    mask = (at % PAD < ROWS) & (token < valid_len[:, None])
    mask = jnp.broadcast_to(mask[:, None].astype(F32), (2, 8, 4 * PAD))
    shards = jnp.concatenate(
        [w_qkv.reshape(2, 64, 384), jnp.swapaxes(w_out, 1, 2), w_up, jnp.swapaxes(w_down, 1, 2)], axis=2
    )
    vmem = pl.BlockSpec(memory_space=pltpu.VMEM)
    arrays = pl.pallas_call(
        whole_kernel,
        out_shape=[jax.ShapeDtypeStruct(s, t) for s, t in OUTPUTS.values()],
        in_specs=[vmem] * len(INPUTS),
        out_specs=[vmem] * len(OUTPUTS),
        scratch_shapes=list(scratch_table().values()),
        compiler_params=pltpu.CompilerParams(
            collective_id=0, has_side_effects=True, vmem_limit_bytes=VMEM_BYTES
        ),
    )(x_in, cotangent, mask, shards, norm_gain, norm_shift, bias, up_bias)
    results = list(pl.pallas_call(
        result_kernel,
        out_shape=[jax.ShapeDtypeStruct(s, t) for s, t in RESULTS.values()],
        in_specs=[vmem] * len(OUTPUTS),
        out_specs=[vmem] * len(RESULTS),
    )(*arrays))
    results[2] = jnp.swapaxes(results[2], 1, 2)
    results[3] = jnp.swapaxes(results[3], 1, 2)
    results[5] = jnp.swapaxes(results[5], 1, 2)
    return tuple(results)


def solution(mesh):
    rows = P(("dp", "tensor"), None)
    weights = (P(None, "dp", None, "tensor"), P(None, "tensor", "dp"), P(None, "dp", "tensor"), P(None, "tensor", "dp"))
    return jax.shard_map(
        per_device,
        mesh=mesh,
        in_specs=(rows, P("dp"), *weights, P(), P(), P(), P(), rows),
        out_specs=(rows, rows, *weights, P(), P(), P(), P()),
        check_vma=False,
    )
```
